32 devices in a mesh: ctx: 8 (over y, x, core), fsdp: 4 (over z).
Axes of the slice: x: 2, y: 2, z: 4, core: 2. Of those that a mesh axis runs over, the one named last changes fastest.
Arguments:
- pixels: bfloat16 [4, 8192, 261], P('fsdp', 'ctx'), may hold values from -8 to 8
- latents: bfloat16 [4, 1024, 1024], P('fsdp', 'ctx'), may hold values from -6 to 6
- cotangent: bfloat16 [4, 1024, 1024], P('fsdp', 'ctx'), may hold values from -6 to 6
- doc_lengths: int32 [4, 4], P('fsdp'), may hold values from 1 to 6144, 8192 in all within a row
- latent_offsets: int32 [4, 1024], P('fsdp'), may hold values from 0 to 7
- block_deal: int32 [16], replicated, may hold values from 0 to 15, each once
- query_cross: float32 [1024, 1024], P('fsdp'), may hold values from -0.1875 to 0.1875
- key_cross: float32 [261, 1024], P(None, 'fsdp'), may hold values from -0.375 to 0.375
- value_cross: float32 [261, 1024], P(None, 'fsdp'), may hold values from -0.375 to 0.375
- out_cross: float32 [1024, 1024], P('fsdp'), may hold values from -3 to 3
- up_cross: float32 [1024, 1024], P('fsdp'), may hold values from -0.1875 to 0.1875
- down_cross: float32 [1024, 1024], P('fsdp'), may hold values from -0.1875 to 0.1875
- query_self: float32 [1024, 1024], P('fsdp'), may hold values from -0.1875 to 0.1875
- key_self: float32 [1024, 1024], P('fsdp'), may hold values from -0.1875 to 0.1875
- value_self: float32 [1024, 1024], P('fsdp'), may hold values from -0.1875 to 0.1875
- out_self: float32 [1024, 1024], P('fsdp'), may hold values from -3 to 3
- up_self: float32 [1024, 1024], P('fsdp'), may hold values from -0.1875 to 0.1875
- down_self: float32 [1024, 1024], P('fsdp'), may hold values from -0.1875 to 0.1875
- gain_input: float32 [261], replicated, may hold values from 0.1 to 1.9
- gain_latent: float32 [1024], replicated, may hold values from 0.1 to 1.9
- gain_cross_mlp: float32 [1024], replicated, may hold values from 0.1 to 1.9
- gain_self: float32 [1024], replicated, may hold values from 0.1 to 1.9
- gain_self_mlp: float32 [1024], replicated, may hold values from 0.1 to 1.9
Outputs:
- layer_out: bfloat16 [4, 1024, 1024], P('fsdp', 'ctx')
- grad_pixels: float32 [4, 8192, 261], P('fsdp', 'ctx')
- grad_latents: float32 [4, 1024, 1024], P('fsdp', 'ctx')
- grad_query_cross: float32 [1024, 1024], P('fsdp')
- grad_key_cross: float32 [261, 1024], P(None, 'fsdp')
- grad_value_cross: float32 [261, 1024], P(None, 'fsdp')
- grad_out_cross: float32 [1024, 1024], P('fsdp')
- grad_up_cross: float32 [1024, 1024], P('fsdp')
- grad_down_cross: float32 [1024, 1024], P('fsdp')
- grad_query_self: float32 [1024, 1024], P('fsdp')
- grad_key_self: float32 [1024, 1024], P('fsdp')
- grad_value_self: float32 [1024, 1024], P('fsdp')
- grad_out_self: float32 [1024, 1024], P('fsdp')
- grad_up_self: float32 [1024, 1024], P('fsdp')
- grad_down_self: float32 [1024, 1024], P('fsdp')
- grad_gain_input: float32 [261], replicated
- grad_gain_latent: float32 [1024], replicated
- grad_gain_cross_mlp: float32 [1024], replicated
- grad_gain_self: float32 [1024], replicated
- grad_gain_self_mlp: float32 [1024], replicated
The draws below stay inside these ranges and needn't reach their ends.
Inputs may be any that keep to these rules, and one draw needn't show every extreme that they name: `doc_lengths`: each row holds the lengths of 4 documents that together fill the 8192 pixel rows of its sequence; one is exactly 6144 long. `block_deal`: a permutation of the 16 latent blocks.
All inputs are finite; a program needn't handle non-finite values.
Results may differ from the reference program's by a relative error of at most 0.028.
Values may be sent and summed in bfloat16 or wider, within the bound.
A program may use at most 320 MiB of HBM per device.

```python
import math
import jax
import jax.numpy as jnp
import numpy as np
from jax import lax

D = 1024
C = 261
HEADS = 8
FFN = 1024
STRIDE = 8
NDOC = 4
LBLK = 64
NPIX = 8192
NLAT = 1024
NLBLK = 16
BATCH = 4
DOC_MOST = 6144


def draw_pixels(key, part):
    key = jax.random.fold_in(key, 11)
    rough_key, common_key = jax.random.split(key)
    rough = jax.random.normal(rough_key, (BATCH, NPIX, C), jnp.float32)
    common = jax.random.normal(common_key, (BATCH, 1, C), jnp.float32)
    return jnp.clip(rough + common, -8.0, 8.0).astype(jnp.bfloat16)


def plant(entries, rng, least, top_value):
    extent = entries.shape
    spot = [jax.random.randint(jax.random.fold_in(rng, axis), (), 0, extent[axis]) for axis in range(len(extent))]
    entries = entries.at[tuple(spot)].set(least)
    longest = extent.index(max(extent))
    spot[longest] = (spot[longest] + 1) % extent[longest]
    return entries.at[tuple(spot)].set(top_value)


def steps_of(own_key, shape, cuts, smallest, top_value):
    def one(axis_at, shards_of):
        draws = jax.random.uniform(jax.random.fold_in(jax.random.fold_in(own_key, 6), axis_at), (shards_of,), jnp.float32, smallest / len(cuts), top_value / len(cuts))
        return jnp.repeat(jnp.exp(draws), shape[axis_at] // shards_of).reshape((-1,) + (1,) * (len(shape) - axis_at - 1))

    loudness = one(*cuts[0])
    for cut in cuts[1:]:
        loudness = loudness * one(*cut)
    return loudness


def profile(amount, total, limit, skew):
    loads = [(1 << 20) // math.isqrt(rank ** skew) + 1 for rank in range(2, amount + 1)]
    surplus, given = total - limit - (amount - 1), [1] * (amount - 1)
    while surplus > 0:
        free = [i for i in range(amount - 1) if given[i] < limit]
        whole, budget = sum([loads[i] for i in free]), surplus
        for i in free:
            more = min(limit - given[i], max(1, budget * loads[i] // whole), surplus)
            given[i] = given[i] + more
            surplus = surplus - more
    return np.array([limit] + given)


def ragged_sizes(rng, number_of, total, limit, slope):
    if number_of == 2:
        one = jax.random.randint(rng, (), max(1, total - limit), min(limit, total - 1) + 1)
        return jnp.stack([one, total - one])
    sizes = jnp.asarray(profile(number_of, total, limit, slope), jnp.int32)
    pairs = (number_of - 1) // 2
    giver, receiver = sizes[1:1 + 2 * pairs:2], sizes[2:2 + 2 * pairs:2]
    margin = jnp.minimum(giver - 1, limit - receiver)
    moved = jax.random.randint(jax.random.fold_in(rng, 1), (pairs,), 0, 1 << 20) % (margin + 1)
    sizes = sizes.at[1:1 + 2 * pairs:2].set(giver - moved).at[2:2 + 2 * pairs:2].set(receiver + moved)
    return sizes[jax.random.permutation(jax.random.fold_in(rng, 2), number_of)]


def noise(key, extent, width, limit, cuts=(), kind=jnp.bfloat16):
    values = width * jax.random.normal(key, extent, jnp.float32)
    if cuts:
        values = values * steps_of(key, extent, cuts, -0.22, 0.18)
    return jnp.clip(values, -limit, limit).astype(kind)


def setup_inputs(seed: int = 0) -> dict:
    arg_keys = jax.random.split(jax.random.key(seed), 24)
    return {
        "pixels": draw_pixels(jax.random.fold_in(arg_keys[23], 71), 0),
        "latents": noise(arg_keys[1], (BATCH, NLAT, D), 1.0, 6.0, ((0, 4), (1, 8))),
        "cotangent": noise(arg_keys[2], (BATCH, NLAT, D), 1.0, 6.0, ((0, 4), (1, 8))),
        "doc_lengths": jax.vmap(lambda own: ragged_sizes(own, NDOC, NPIX, DOC_MOST, 2))(jax.random.split(arg_keys[3], BATCH)).reshape((BATCH, NDOC)).astype(jnp.int32),
        "latent_offsets": plant(jax.random.randint(arg_keys[4], (BATCH, NLAT), 0, STRIDE), jax.random.fold_in(arg_keys[4], 1), 0, STRIDE - 1).astype(jnp.int32),
        "block_deal": jax.random.permutation(arg_keys[5], NLBLK).astype(jnp.int32),
        "query_cross": noise(arg_keys[6], (D, D), D ** -0.5, 0.1875, ((0, 4),), jnp.float32),
        "key_cross": noise(arg_keys[7], (C, D), C ** -0.5, 0.375, ((1, 4),), jnp.float32),
        "value_cross": noise(arg_keys[8], (C, D), C ** -0.5, 0.375, ((1, 4),), jnp.float32),
        "out_cross": noise(arg_keys[9], (D, D), (max(D // 256, 1)) ** -0.5, 3.0, ((0, 4),), jnp.float32),
        "up_cross": noise(arg_keys[10], (D, FFN), D ** -0.5, 0.1875, ((0, 4),), jnp.float32),
        "down_cross": noise(arg_keys[11], (FFN, D), FFN ** -0.5, 0.1875, ((0, 4),), jnp.float32),
        "query_self": noise(arg_keys[12], (D, D), D ** -0.5, 0.1875, ((0, 4),), jnp.float32),
        "key_self": noise(arg_keys[13], (D, D), D ** -0.5, 0.1875, ((0, 4),), jnp.float32),
        "value_self": noise(arg_keys[14], (D, D), D ** -0.5, 0.1875, ((0, 4),), jnp.float32),
        "out_self": noise(arg_keys[15], (D, D), (max(D // 256, 1)) ** -0.5, 3.0, ((0, 4),), jnp.float32),
        "up_self": noise(arg_keys[16], (D, FFN), D ** -0.5, 0.1875, ((0, 4),), jnp.float32),
        "down_self": noise(arg_keys[17], (FFN, D), FFN ** -0.5, 0.1875, ((0, 4),), jnp.float32),
        "gain_input": jnp.clip(1.0 + 0.18 * jax.random.normal(arg_keys[18], (C,), jnp.float32), 0.1, 1.9),
        "gain_latent": jnp.clip(1.0 + 0.18 * jax.random.normal(arg_keys[19], (D,), jnp.float32), 0.1, 1.9),
        "gain_cross_mlp": jnp.clip(1.0 + 0.18 * jax.random.normal(arg_keys[20], (D,), jnp.float32), 0.1, 1.9),
        "gain_self": jnp.clip(1.0 + 0.18 * jax.random.normal(arg_keys[21], (D,), jnp.float32), 0.1, 1.9),
        "gain_self_mlp": jnp.clip(1.0 + 0.18 * jax.random.normal(arg_keys[22], (D,), jnp.float32), 0.1, 1.9),
    }


@jax.custom_vjp
def low(v):
    return lax.optimization_barrier(v.astype(jnp.bfloat16)).astype(jnp.float32)

@jax.custom_vjp
def low_back(v):
    return v

def low_keep(v):
    return (low(v), None)

def low_pass(kept, grad):
    return (grad,)

def back_keep(v):
    return (v, None)

def back_low(kept, grad):
    return (low(grad),)
low.defvjp(low_keep, low_pass)
low_back.defvjp(back_keep, back_low)
masked_fill = -1e+30

def product(inputs, weight):
    return jnp.dot(inputs, weight, precision=lax.Precision.HIGHEST, preferred_element_type=jnp.float32)

def layer_norm(values, gain):
    center = values - lax.optimization_barrier(jnp.mean(values, axis=-1, keepdims=True))
    spread = lax.optimization_barrier(jnp.mean(center * center, axis=-1, keepdims=True))
    return center * lax.rsqrt(spread + 1e-05) * gain

def doc_index(positions, starts):
    return lax.optimization_barrier(jnp.sum((positions[:, None] >= starts[None, :]).astype(jnp.int32), axis=1)) - 1

def latent_positions(block_deal, offsets):
    base = (block_deal[:, None] * LBLK + jnp.arange(LBLK, dtype=jnp.int32)[None, :]).reshape(-1)
    return base * STRIDE + offsets

def feed_forward(residual, gain, up_matrix, down_matrix):
    normed = low(layer_norm(residual, gain))
    active = low(jax.nn.gelu(low_back(product(normed, up_matrix))))
    return residual + low_back(product(active, down_matrix))

def layer(pix_rows, lat_rows, lengths, offsets, block_deal, lowered, gain_list):
    query_cross, key_cross, value_cross, out_cross, up_cross, down_cross, query_self, key_self, value_self, out_self, up_self, down_self = lowered
    gain_input, gain_latent, gain_cross_mlp, gain_self, gain_self_mlp = gain_list
    head_dim = D // HEADS
    cross_scale = 1.0 / math.sqrt(D)
    self_scale = 1.0 / math.sqrt(head_dim)
    starts = jnp.cumsum(lengths) - lengths
    lat_pos = latent_positions(block_deal, offsets)
    lat_doc = doc_index(lat_pos, starts)
    pix_pos = jnp.arange(NPIX, dtype=jnp.int32)
    pix_doc = doc_index(pix_pos, starts)
    block_rows = min(512, NLAT)
    count_blocks = NLAT // block_rows
    normed_pix = low(layer_norm(pix_rows, gain_input))
    keys_cross = low(low_back(product(normed_pix, key_cross)))
    values_cross = low(low_back(product(normed_pix, value_cross)))
    normed_lat = low(layer_norm(lat_rows, gain_latent))
    queries = low(low_back(product(normed_lat, query_cross)))

    def cross_block(packed):
        query_rows, pos_rows, doc_rows = packed
        raw_scores = low_back(jnp.einsum('qd,kd->qk', query_rows, keys_cross, precision=lax.Precision.HIGHEST))
        allowed = (doc_rows[:, None] == pix_doc[None, :]) & (pix_pos[None, :] <= pos_rows[:, None])
        scores = jnp.where(allowed, raw_scores * cross_scale, masked_fill)
        attention = low(jax.nn.softmax(scores, axis=-1))
        return low(low_back(product(attention, values_cross)))
    attended = lax.map(jax.checkpoint(cross_block), (queries.reshape(count_blocks, block_rows, D), lat_pos.reshape(count_blocks, block_rows), lat_doc.reshape(count_blocks, block_rows))).reshape(NLAT, D)
    residual_one = lat_rows + low_back(product(attended, out_cross))
    residual_two = feed_forward(residual_one, gain_cross_mlp, up_cross, down_cross)
    normed_two = low(layer_norm(residual_two, gain_self))
    self_queries = low(low_back(product(normed_two, query_self))).reshape(NLAT, HEADS, head_dim)
    self_keys = low(low_back(product(normed_two, key_self))).reshape(NLAT, HEADS, head_dim)
    self_values = low(low_back(product(normed_two, value_self))).reshape(NLAT, HEADS, head_dim)

    def self_block(packed):
        query_rows, pos_rows, doc_rows = packed
        raw_scores = low_back(jnp.einsum('qhd,khd->hqk', query_rows, self_keys, precision=lax.Precision.HIGHEST))
        allowed = (doc_rows[:, None] == lat_doc[None, :]) & (lat_pos[None, :] <= pos_rows[:, None])
        scores = jnp.where(allowed[None], raw_scores * self_scale, masked_fill)
        attention = low(jax.nn.softmax(scores, axis=-1))
        joined = jnp.einsum('hqk,khd->qhd', attention, self_values, precision=lax.Precision.HIGHEST)
        return low(low_back(joined.reshape(joined.shape[0], D)))
    self_attended = lax.map(jax.checkpoint(self_block), (self_queries.reshape(count_blocks, block_rows, HEADS, head_dim), lat_pos.reshape(count_blocks, block_rows), lat_doc.reshape(count_blocks, block_rows))).reshape(NLAT, D)
    residual_three = residual_two + low_back(product(self_attended, out_self))
    return feed_forward(residual_three, gain_self_mlp, up_self, down_self)

def reference(pixels, latents, cotangent, doc_lengths, latent_offsets, block_deal, query_cross, key_cross, value_cross, out_cross, up_cross, down_cross, query_self, key_self, value_self, out_self, up_self, down_self, gain_input, gain_latent, gain_cross_mlp, gain_self, gain_self_mlp):
    weights = (query_cross.astype(jnp.float32), key_cross.astype(jnp.float32), value_cross.astype(jnp.float32), out_cross.astype(jnp.float32), up_cross.astype(jnp.float32), down_cross.astype(jnp.float32), query_self.astype(jnp.float32), key_self.astype(jnp.float32), value_self.astype(jnp.float32), out_self.astype(jnp.float32), up_self.astype(jnp.float32), down_self.astype(jnp.float32))
    gains = (gain_input, gain_latent, gain_cross_mlp, gain_self, gain_self_mlp)
    pix_float = pixels.astype(jnp.float32)
    lat_float = latents.astype(jnp.float32)

    def forward(pix_all, lat_all, weight_list, gain_list):
        lowered = tuple((low(matrix) for matrix in weight_list))

        def one_sequence(packed):
            pix_rows, lat_rows, lengths, offsets = packed
            return layer(pix_rows, lat_rows, lengths, offsets, block_deal, lowered, gain_list)
        return lax.map(jax.checkpoint(one_sequence), (pix_all, lat_all, doc_lengths, latent_offsets))
    result, pullback = jax.vjp(forward, pix_float, lat_float, weights, gains)
    grad_pix, grad_lat, grad_weights, grad_gains = pullback(cotangent.astype(jnp.float32))
    return (result.astype(jnp.bfloat16), grad_pix, grad_lat, grad_weights[0], grad_weights[1], grad_weights[2], grad_weights[3], grad_weights[4], grad_weights[5], grad_weights[6], grad_weights[7], grad_weights[8], grad_weights[9], grad_weights[10], grad_weights[11], grad_gains[0], grad_gains[1], grad_gains[2], grad_gains[3], grad_gains[4])
```

```python
import math

import jax
import jax.numpy as jnp
from jax import lax
from jax.sharding import PartitionSpec as P

D = 1024
HEADS = 8
HEAD = D // HEADS
STRIDE = 8
LBLK = 64
BF = jnp.bfloat16
F32 = jnp.float32
CROSS_SCALE = 1.0 / math.sqrt(D)
SELF_SCALE = 1.0 / math.sqrt(HEAD)
MASKED = -1e30
GELU_K = math.sqrt(2.0 / math.pi)
GELU_A = 0.044715


def mm(a, b):
    return jnp.dot(a, b, preferred_element_type=F32)


def mm_nt(a, b):
    return lax.dot_general(a, b, (((1,), (1,)), ((), ())), preferred_element_type=F32)


def mm_tn(a, b):
    return lax.dot_general(a, b, (((0,), (0,)), ((), ())), preferred_element_type=F32)


def norm_parts(x):
    center = x - jnp.mean(x, axis=-1, keepdims=True)
    r = lax.rsqrt(jnp.mean(center * center, axis=-1, keepdims=True) + 1e-05)
    return center * r, r


def norm_back(dy, x, gain):
    hat, r = norm_parts(x)
    dhat = dy * gain
    dx = r * (
        dhat
        - jnp.mean(dhat, axis=-1, keepdims=True)
        - hat * jnp.mean(dhat * hat, axis=-1, keepdims=True)
    )
    return dx, jnp.sum(dy * hat, axis=0)


def gelu(u):
    return 0.5 * u * (1.0 + jnp.tanh(GELU_K * (u + GELU_A * u * u * u)))


def gelu_slope(u):
    t = jnp.tanh(GELU_K * (u + GELU_A * u * u * u))
    return 0.5 * (1.0 + t) + 0.5 * u * (1.0 - t * t) * GELU_K * (1.0 + 3.0 * GELU_A * u * u)


def intervals(lengths, offsets, deal):
    count = lengths.shape[0]
    before = jnp.arange(count)[:, None] > jnp.arange(count)[None, :]
    starts = jnp.sum(jnp.where(before, lengths[None, :], 0), axis=1)
    base = (deal[:, None] * LBLK + jnp.arange(LBLK, dtype=jnp.int32)[None, :]).reshape(-1)
    pos = base * STRIDE + offsets
    lo = jnp.max(jnp.where(starts[None, :] <= pos[:, None], starts[None, :], -1), axis=1)
    return lo, pos


def plain(
    pixels, latents, cotangent, doc_lengths, latent_offsets, block_deal,
    wq_c, wk_c, wv_c, wo_c, wu_c, wd_c, wq_s, wk_s, wv_s, wo_s, wu_s, wd_s,
    g_in, g_lat, g_cmlp, g_self, g_smlp,
):
    n = lax.axis_size("ctx")
    me = lax.axis_index("ctx")
    rows = latents.shape[1]
    npix = pixels.shape[1]
    c = pixels.shape[2]
    lo, pos = intervals(doc_lengths[0], latent_offsets[0], block_deal)
    own_lo = lax.dynamic_slice_in_dim(lo, me * rows, rows)
    own_pos = lax.dynamic_slice_in_dim(pos, me * rows, rows)
    pix_pos = me * npix + jnp.arange(npix, dtype=jnp.int32)
    mask = (lo[:, None] <= pix_pos[None, :]) & (pix_pos[None, :] <= pos[:, None])
    smask = (own_lo[:, None] <= pos[None, :]) & (pos[None, :] <= own_pos[:, None])

    wq_c, wk_c, wv_c, wo_c = (w.astype(BF) for w in (wq_c, wk_c, wv_c, wo_c))
    wk_all = lax.all_gather(wk_c, "fsdp", axis=1, tiled=True)
    wqk = lax.all_gather(mm_nt(wq_c, wk_all).astype(BF), "fsdp", axis=0, tiled=True)
    wvo = lax.psum(mm(wv_c, wo_c), "fsdp").astype(BF)
    big = jnp.stack([w.astype(BF) for w in (wu_c, wd_c, wq_s, wk_s, wv_s, wo_s, wu_s, wd_s)])
    wu1, wd1, wq, wk, wv, wo, wu3, wd3 = lax.all_gather(big, "fsdp", axis=1, tiled=True)

    xin = pixels[0].astype(F32)
    xn = (norm_parts(xin)[0] * g_in).astype(BF)
    lat = latents[0].astype(F32)
    ln = (norm_parts(lat)[0] * g_lat).astype(BF)
    qk_all = lax.all_gather(mm(ln, wqk).astype(BF), "ctx", axis=0, tiled=True)
    s = jnp.where(mask, mm_nt(qk_all, xn) * CROSS_SCALE, MASKED)
    top = jnp.max(s, axis=1, keepdims=True)
    e = jnp.where(mask, jnp.exp(s - top), 0.0)
    total = jnp.sum(e, axis=1, keepdims=True)
    part = jnp.concatenate([mm(e.astype(BF), xn), top, total], axis=1)
    parts = lax.all_to_all(part.reshape(n, rows, c + 2), "ctx", 0, 0)
    tops = parts[:, :, c : c + 1]
    high = jnp.max(tops, axis=0)
    share = jnp.exp(tops - high[None])
    full = jnp.sum(share * parts[:, :, c + 1 :], axis=0)
    px = jnp.sum(share * parts[:, :, :c], axis=0) / full
    lse = high + jnp.log(full)
    px_low = px.astype(BF)
    h1 = lat + mm(px_low, wvo)
    n1 = (norm_parts(h1)[0] * g_cmlp).astype(BF)
    u1 = mm(n1, wu1)
    z1 = gelu(u1).astype(BF)
    h2 = h1 + mm(z1, wd1)
    n2 = (norm_parts(h2)[0] * g_self).astype(BF)
    q = mm(n2, wq).astype(BF).reshape(rows, HEADS, HEAD)
    kv = jnp.concatenate([mm(n2, wk), mm(n2, wv)], axis=1).astype(BF)
    kv = lax.all_gather(kv, "ctx", axis=0, tiled=True)
    k = kv[:, :D].reshape(n * rows, HEADS, HEAD)
    v = kv[:, D:].reshape(n * rows, HEADS, HEAD)
    ss = jnp.einsum("qhd,khd->hqk", q, k, preferred_element_type=F32) * SELF_SCALE
    ss = jnp.where(smask[None], ss, MASKED)
    se = jnp.exp(ss - jnp.max(ss, axis=-1, keepdims=True))
    ps = se / jnp.sum(se, axis=-1, keepdims=True)
    psl = ps.astype(BF)
    sa = jnp.einsum("hqk,khd->qhd", psl, v, preferred_element_type=F32)
    sa = sa.reshape(rows, D).astype(BF)
    h3 = h2 + mm(sa, wo)
    n3 = (norm_parts(h3)[0] * g_smlp).astype(BF)
    u3 = mm(n3, wu3)
    z3 = gelu(u3).astype(BF)
    layer_out = (h3 + mm(z3, wd3)).astype(BF)

    gy3 = cotangent[0]
    gu3 = (mm_nt(gy3, wd3) * gelu_slope(u3)).astype(BF)
    dx, gg_smlp = norm_back(mm_nt(gu3, wu3), h3, g_smlp)
    dh3 = gy3.astype(F32) + dx
    go3 = dh3.astype(BF)
    gas = mm_nt(go3, wo).astype(BF).reshape(rows, HEADS, HEAD)
    dps = jnp.einsum("qhd,khd->hqk", gas, v, preferred_element_type=F32)
    sdelta = jnp.sum(ps * dps, axis=-1, keepdims=True)
    dss = (ps * (dps - sdelta) * SELF_SCALE).astype(BF)
    dqs = jnp.einsum("hqk,khd->qhd", dss, k, preferred_element_type=F32)
    dqs = dqs.reshape(rows, D).astype(BF)
    dks = jnp.einsum("hqk,qhd->khd", dss, q, preferred_element_type=F32).reshape(n * rows, D)
    dvs = jnp.einsum("hqk,qhd->khd", psl, gas, preferred_element_type=F32).reshape(n * rows, D)
    dkv = lax.psum_scatter(
        jnp.concatenate([dks, dvs], axis=1), "ctx", scatter_dimension=0, tiled=True
    ).astype(BF)
    dks, dvs = dkv[:, :D], dkv[:, D:]
    dn2 = mm_nt(dqs, wq) + mm_nt(dks, wk) + mm_nt(dvs, wv)
    dx, gg_self = norm_back(dn2, h2, g_self)
    dh2 = dh3 + dx
    gy1 = dh2.astype(BF)
    gu1 = (mm_nt(gy1, wd1) * gelu_slope(u1)).astype(BF)
    dx, gg_cmlp = norm_back(mm_nt(gu1, wu1), h1, g_cmlp)
    dh1 = dh2 + dx
    go1 = dh1.astype(BF)
    gv = mm_nt(go1, wvo).astype(BF)
    delta = jnp.sum(px * gv.astype(F32), axis=1, keepdims=True)
    gv_all = lax.all_gather(gv, "ctx", axis=0, tiled=True)
    stat = lax.all_gather(jnp.concatenate([lse, delta], axis=1), "ctx", axis=0, tiled=True)
    p = jnp.where(mask, jnp.exp(s - stat[:, :1]), 0.0)
    ds = (p * (mm_nt(gv_all, xn) - stat[:, 1:]) * CROSS_SCALE).astype(BF)
    dxn = mm_tn(ds, qk_all) + mm_tn(p.astype(BF), gv_all)
    dpix, gg_in = norm_back(dxn, xin, g_in)
    dqk = lax.psum_scatter(mm(ds, xn), "ctx", scatter_dimension=0, tiled=True).astype(BF)
    dx, gg_lat = norm_back(mm_nt(dqk, wqk), lat, g_lat)
    dlat = dh1 + dx

    e_sum = lax.psum_scatter(mm_tn(ln, dqk), "fsdp", scatter_dimension=0, tiled=True)
    e_sum, f_sum = lax.psum((e_sum, lax.psum(mm_tn(px_low, go1), "fsdp")), "ctx")
    e_sum, f_sum = e_sum.astype(BF), f_sum.astype(BF)
    d_wq_c = mm(e_sum, wk_all)
    d_wk_c = lax.psum_scatter(mm_tn(e_sum, wq_c), "fsdp", scatter_dimension=1, tiled=True)
    d_wv_c = mm_nt(f_sum, wo_c)
    d_wo_c = mm_tn(wv_c, f_sum)
    pairs = ((n1, gu1), (z1, gy1), (n2, dqs), (n2, dks), (n2, dvs), (sa, go3), (n3, gu3), (z3, gy3))
    d_big = [
        lax.psum(lax.psum_scatter(mm_tn(a, b), "fsdp", scatter_dimension=0, tiled=True), "ctx")
        for a, b in pairs
    ]
    gains = lax.psum(jnp.concatenate([gg_in, gg_lat, gg_cmlp, gg_self, gg_smlp]), ("ctx", "fsdp"))
    return (
        layer_out[None], dpix[None], dlat[None], d_wq_c, d_wk_c, d_wv_c, d_wo_c, *d_big,
        gains[:c], gains[c : c + D], gains[c + D : c + 2 * D],
        gains[c + 2 * D : c + 3 * D], gains[c + 3 * D :],
    )


def solution(mesh):
    rows, row, col, all_ = P("fsdp", "ctx", None), P("fsdp", None), P(None, "fsdp"), P()
    weights = (row, col, col, *(row,) * 9)
    return jax.shard_map(
        plain,
        mesh=mesh,
        in_specs=(rows, rows, rows, row, row, all_, *weights, *(all_,) * 5),
        out_specs=(rows, rows, rows, *weights, *(all_,) * 5),
        check_vma=False,
    )
```

```python
import math
import types

import jax
import jax.numpy as jnp
from jax import lax
from jax.experimental import pallas as pl
from jax.experimental.pallas import tpu as pltpu
from jax.sharding import PartitionSpec as P

D = 1024
HEADS = 8
HEAD = D // HEADS
STRIDE = 8
LBLK = 64
BF = jnp.bfloat16
F32 = jnp.float32
CROSS_SCALE = 1.0 / math.sqrt(D)
SELF_SCALE = 1.0 / math.sqrt(HEAD)
MASKED = -1e30
GELU_K = math.sqrt(2.0 / math.pi)
GELU_A = 0.044715


def mm(a, b):
    return jnp.dot(a, b, preferred_element_type=F32)


def mm_nt(a, b):
    return lax.dot_general(a, b, (((1,), (1,)), ((), ())), preferred_element_type=F32)


def mm_tn(a, b):
    return lax.dot_general(a, b, (((0,), (0,)), ((), ())), preferred_element_type=F32)


def norm_parts(x):
    center = x - jnp.mean(x, axis=-1, keepdims=True)
    r = lax.rsqrt(jnp.mean(center * center, axis=-1, keepdims=True) + 1e-05)
    return center * r, r


def norm_back(dy, x, gain):
    hat, r = norm_parts(x)
    dhat = dy * gain
    dx = r * (
        dhat
        - jnp.mean(dhat, axis=-1, keepdims=True)
        - hat * jnp.mean(dhat * hat, axis=-1, keepdims=True)
    )
    return dx, jnp.sum(dy * hat, axis=0, keepdims=True)


def gelu(u):
    return 0.5 * u * (1.0 + jnp.tanh(GELU_K * (u + GELU_A * u * u * u)))


def gelu_slope(u):
    t = jnp.tanh(GELU_K * (u + GELU_A * u * u * u))
    return 0.5 * (1.0 + t) + 0.5 * u * (1.0 - t * t) * GELU_K * (1.0 + 3.0 * GELU_A * u * u)


def intervals(lengths, offsets, deal):
    count = lengths.shape[0]
    before = jnp.arange(count)[:, None] > jnp.arange(count)[None, :]
    starts = jnp.sum(jnp.where(before, lengths[None, :], 0), axis=1)
    base = (deal[:, None] * LBLK + jnp.arange(LBLK, dtype=jnp.int32)[None, :]).reshape(-1)
    pos = base * STRIDE + offsets
    lo = jnp.max(jnp.where(starts[None, :] <= pos[:, None], starts[None, :], -1), axis=1)
    return lo, pos


def plain(
    pixels, latents, cotangent, doc_lengths, latent_offsets, block_deal,
    wq_c, wk_c, wv_c, wo_c, wu_c, wd_c, wq_s, wk_s, wv_s, wo_s, wu_s, wd_s,
    g_in, g_lat, g_cmlp, g_self, g_smlp,
):
    n = lax.axis_size("ctx")
    me = lax.axis_index("ctx")
    rows = latents.shape[1]
    npix = pixels.shape[1]
    c = pixels.shape[2]
    lo, pos = intervals(doc_lengths[0], latent_offsets[0], block_deal)
    own_lo = lax.dynamic_slice_in_dim(lo, me * rows, rows)
    own_pos = lax.dynamic_slice_in_dim(pos, me * rows, rows)
    pix_pos = me * npix + jnp.arange(npix, dtype=jnp.int32)
    mask = (lo[:, None] <= pix_pos[None, :]) & (pix_pos[None, :] <= pos[:, None])
    smask = (own_lo[:, None] <= pos[None, :]) & (pos[None, :] <= own_pos[:, None])

    wq_c, wk_c, wv_c, wo_c = (w.astype(BF) for w in (wq_c, wk_c, wv_c, wo_c))
    wk_all = lax.all_gather(wk_c, "fsdp", axis=1, tiled=True)
    wqk = lax.all_gather(mm_nt(wq_c, wk_all).astype(BF), "fsdp", axis=0, tiled=True)
    wvo = lax.psum(mm(wv_c, wo_c), "fsdp").astype(BF)
    big = jnp.stack([w.astype(BF) for w in (wu_c, wd_c, wq_s, wk_s, wv_s, wo_s, wu_s, wd_s)])
    wu1, wd1, wq, wk, wv, wo, wu3, wd3 = lax.all_gather(big, "fsdp", axis=1, tiled=True)

    xin = pixels[0].astype(F32)
    xn = (norm_parts(xin)[0] * g_in).astype(BF)
    lat = latents[0].astype(F32)
    ln = (norm_parts(lat)[0] * g_lat).astype(BF)
    qk_all = lax.all_gather(mm(ln, wqk).astype(BF), "ctx", axis=0, tiled=True)
    s = jnp.where(mask, mm_nt(qk_all, xn) * CROSS_SCALE, MASKED)
    top = jnp.max(s, axis=1, keepdims=True)
    e = lax.optimization_barrier(jnp.where(mask, jnp.exp(s - top), 0.0).astype(BF))
    total = jnp.sum(e.astype(F32), axis=1, keepdims=True)
    part = jnp.concatenate([mm(e, xn), top, total], axis=1)
    parts = lax.all_to_all(part.reshape(n, rows, c + 2), "ctx", 0, 0)
    tops = parts[:, :, c : c + 1]
    high = jnp.max(tops, axis=0)
    share = jnp.exp(tops - high[None])
    full = jnp.sum(share * parts[:, :, c + 1 :], axis=0)
    px = jnp.sum(share * parts[:, :, :c], axis=0) / full
    lse = high + jnp.log(full)
    px_low = px.astype(BF)
    h1 = lat + mm(px_low, wvo)
    n1 = (norm_parts(h1)[0] * g_cmlp).astype(BF)
    u1 = mm(n1, wu1)
    z1 = gelu(u1).astype(BF)
    h2 = h1 + mm(z1, wd1)
    n2 = (norm_parts(h2)[0] * g_self).astype(BF)
    q = mm(n2, wq).astype(BF).reshape(rows, HEADS, HEAD)
    kv = jnp.concatenate([mm(n2, wk), mm(n2, wv)], axis=1).astype(BF)
    kv = lax.all_gather(kv, "ctx", axis=0, tiled=True)
    k = kv[:, :D].reshape(n * rows, HEADS, HEAD)
    v = kv[:, D:].reshape(n * rows, HEADS, HEAD)
    ss = jnp.einsum("qhd,khd->hqk", q, k, preferred_element_type=F32) * SELF_SCALE
    ss = jnp.where(smask[None], ss, MASKED)
    se = jnp.exp(ss - jnp.max(ss, axis=-1, keepdims=True))
    ps = se / jnp.sum(se, axis=-1, keepdims=True)
    psl = ps.astype(BF)
    sa = jnp.einsum("hqk,khd->qhd", psl, v, preferred_element_type=F32)
    sa = sa.reshape(rows, D).astype(BF)
    h3 = h2 + mm(sa, wo)
    n3 = (norm_parts(h3)[0] * g_smlp).astype(BF)
    u3 = mm(n3, wu3)
    z3 = gelu(u3).astype(BF)
    layer_out = (h3 + mm(z3, wd3)).astype(BF)

    gy3 = cotangent[0]
    gu3 = (mm_nt(gy3, wd3) * gelu_slope(u3)).astype(BF)
    dx, gg_smlp = norm_back(mm_nt(gu3, wu3), h3, g_smlp)
    dh3 = gy3.astype(F32) + dx
    go3 = dh3.astype(BF)
    gas = mm_nt(go3, wo).astype(BF).reshape(rows, HEADS, HEAD)
    dps = jnp.einsum("qhd,khd->hqk", gas, v, preferred_element_type=F32)
    sdelta = jnp.sum(ps * dps, axis=-1, keepdims=True)
    dss = (ps * (dps - sdelta) * SELF_SCALE).astype(BF)
    dqs = jnp.einsum("hqk,khd->qhd", dss, k, preferred_element_type=F32)
    dqs = dqs.reshape(rows, D).astype(BF)
    dks = jnp.einsum("hqk,qhd->khd", dss, q, preferred_element_type=F32).reshape(n * rows, D)
    dvs = jnp.einsum("hqk,qhd->khd", psl, gas, preferred_element_type=F32).reshape(n * rows, D)
    dkv = lax.psum_scatter(
        jnp.concatenate([dks, dvs], axis=1), "ctx", scatter_dimension=0, tiled=True
    ).astype(BF)
    dks, dvs = dkv[:, :D], dkv[:, D:]
    dn2 = mm_nt(dqs, wq) + mm_nt(dks, wk) + mm_nt(dvs, wv)
    dx, gg_self = norm_back(dn2, h2, g_self)
    dh2 = dh3 + dx
    gy1 = dh2.astype(BF)
    gu1 = (mm_nt(gy1, wd1) * gelu_slope(u1)).astype(BF)
    dx, gg_cmlp = norm_back(mm_nt(gu1, wu1), h1, g_cmlp)
    dh1 = dh2 + dx
    go1 = dh1.astype(BF)
    gv = lax.optimization_barrier(mm_nt(go1, wvo).astype(BF))
    delta = jnp.sum(px * gv.astype(F32), axis=1, keepdims=True)
    gv_all = lax.all_gather(gv, "ctx", axis=0, tiled=True)
    stat = lax.all_gather(jnp.concatenate([lse, delta], axis=1), "ctx", axis=0, tiled=True)
    p = jnp.where(mask, jnp.exp(s - stat[:, :1]), 0.0)
    ds = (p * (mm_nt(gv_all, xn) - stat[:, 1:]) * CROSS_SCALE).astype(BF)
    dxn = mm_tn(ds, qk_all) + mm_tn(p.astype(BF), gv_all)
    dpix, gg_in = norm_back(dxn, xin, g_in)
    dqk = lax.psum_scatter(mm(ds, xn), "ctx", scatter_dimension=0, tiled=True).astype(BF)
    dx, gg_lat = norm_back(mm_nt(dqk, wqk), lat, g_lat)
    dlat = dh1 + dx

    e_sum = lax.psum_scatter(mm_tn(ln, dqk), "fsdp", scatter_dimension=0, tiled=True)
    e_sum, f_sum = lax.psum((e_sum, lax.psum(mm_tn(px_low, go1), "fsdp")), "ctx")
    e_sum, f_sum = e_sum.astype(BF), f_sum.astype(BF)
    d_wq_c = mm(e_sum, wk_all)
    d_wk_c = lax.psum_scatter(mm_tn(e_sum, wq_c), "fsdp", scatter_dimension=1, tiled=True)
    d_wv_c = mm_nt(f_sum, wo_c)
    d_wo_c = mm_tn(wv_c, f_sum)
    pairs = ((n1, gu1), (z1, gy1), (n2, dqs), (n2, dks), (n2, dvs), (sa, go3), (n3, gu3), (z3, gy3))
    d_big = [
        lax.psum(lax.psum_scatter(mm_tn(a, b), "fsdp", scatter_dimension=0, tiled=True), "ctx")
        for a, b in pairs
    ]
    gains = lax.psum(jnp.concatenate([gg_in[0], gg_lat[0], gg_cmlp[0], gg_self[0], gg_smlp[0]]), ("ctx", "fsdp"))
    return (
        layer_out[None], dpix[None], dlat[None], d_wq_c, d_wk_c, d_wv_c, d_wo_c, *d_big,
        gains[:c], gains[c : c + D], gains[c + D : c + 2 * D],
        gains[c + 2 * D : c + 3 * D], gains[c + 3 * D :],
    )


CP = 384
CR = 288
PARITY_ROWS = 4 * 128


def fused(
    pix, lat, cot, span, pos_r, g_in, g_lat, g_cmlp, g_self, g_smlp,
    wq_c, wk_c, wv_c, wo_c, wu_1, wd_1, wq_s, wk_s, wv_s, wo_s, wu_3, wd_3,
    layer_out, d_pix, d_lat, d_wq, d_wk, d_wv, d_wo, d_big, d_gain,
    *scratch,
):
    s = types.SimpleNamespace(**dict(zip(SCRATCH, scratch)))
    c, z = lax.axis_index("ctx"), lax.axis_index("fsdp")
    k, p = lax.rem(c, 2), lax.div(c, 2)
    k2 = 1 - k

    def flip(v, d):
        low, high = lax.rem(v, 2), lax.div(v, 2)
        return (1 - low if d & 1 else low) + 2 * (1 - high if d & 2 else high)

    chip = {d: flip(p, d) for d in (1, 2, 3)}
    plane = {d: flip(z, d) for d in (1, 2, 3)}
    sib = {"ctx": 2 * p + k2}

    def peer(d):
        return {"ctx": 2 * chip[d] + k}

    def level(d):
        return {"fsdp": plane[d]}

    used = [0, 0]
    sends = []

    def make(src, dst, target, slot=None):
        if slot is None:
            slot = used[0]
            used[0] += 1
        send = used[1]
        used[1] += 1
        return pltpu.make_async_remote_copy(
            src_ref=src, dst_ref=dst, send_sem=s.ssem.at[send], recv_sem=s.rsem.at[slot],
            device_id=target, device_id_type=pl.DeviceIdType.MESH,
        )

    def put(src, dst, target):
        copy = make(src, dst, target)
        copy.start()
        sends.append((None, copy))
        return copy

    def sent(copies):
        for copy in copies.values() if isinstance(copies, dict) else copies:
            copy.wait_send()
            sends[:] = [pair for pair in sends if pair[1] is not copy]

    def to_peers(src_of, dst_of, order=(3, 1, 2)):
        return {d: put(src_of(d), dst_of(d), peer(d)) for d in order}

    def to_planes(src_of, dst_of):
        return {d: put(src_of(d), dst_of(d), level(d)) for d in (1, 2, 3)}

    def arrived(copies):
        for copy in copies.values() if isinstance(copies, dict) else copies:
            copy.wait_recv()

    locals_ = [0]

    def fetch(src, dst):
        copy = pltpu.make_async_copy(src, dst, s.lsem.at[locals_[0]])
        locals_[0] += 1
        copy.start()
        return copy

    def gather(slot_of, first=()):
        copies = to_peers(lambda d: slot_of(c), lambda d: slot_of(c))
        own = put(slot_of(c), slot_of(c), sib)
        return copies, own

    def pass_on(slot_of, state):
        copies, own = state
        on = []
        for d in (1, 2, 3):
            copies[d].wait_recv()
            there = slot_of(2 * chip[d] + k)
            on.append(put(there, there, sib))
        return [own, *on]

    for j in range(4):
        s.wk[j, 256:CP, :] = jnp.zeros((CP - 256, 256), BF)
    s.wv_z[256:CP, :] = jnp.zeros((CP - 256, 256), BF)
    for j in range(8):
        s.wvo[j, CR:CP, :] = jnp.zeros((CP - CR, 128), BF)
        s.fag[j, CR:CP, :] = jnp.zeros((CP - CR, 128), BF)
    barrier = pltpu.get_barrier_semaphore()
    for target in (sib, *(peer(d) for d in (1, 2, 3)), *(level(d) for d in (1, 2, 3))):
        pl.semaphore_signal(barrier, inc=1, device_id=target, device_id_type=pl.DeviceIdType.MESH)
    lanes = pl.ds(pl.multiple_of(c * 128, 128), 128)
    quarter = pl.ds(pl.multiple_of(k * 128 + p * 32, 32), 32)
    f_wk = [fetch(wk_c.at[0:256], s.u1.at[0]), fetch(wk_c.at[256:261], s.u1.at[1, 0:5])]
    f_wq = [fetch(wq_c.at[128 * i : 128 * (i + 1)], s.hpa.at[i]) for i in range(2)]
    f_wv = [fetch(wv_c.at[0:256], s.u3.at[0]), fetch(wv_c.at[256:261], s.u3.at[1, 0:5])]
    f_wo = [fetch(wo_c.at[128 * i : 128 * (i + 1)], s.hpb.at[i]) for i in range(2)]

    def early(i):
        return (s.dh if i < 8 else s.tmp).at[:, 128 * (i % 8) : 128 * (i % 8) + 128]

    f_u = [
        fetch(w.at[128 * j : 128 * (j + 1), lanes], early(2 * i + j))
        for i, w in enumerate((wu_1, wu_3, wq_s, wk_s, wv_s))
        for j in range(2)
    ]
    f_d = [fetch(w.at[quarter, :], s.h3.at[32 * i : 32 * (i + 1)]) for i, w in enumerate((wd_1, wd_3))]
    f_os = fetch(wo_s.at[pl.ds(pl.multiple_of(k * 128, 128), 128), :], s.hxa)
    pl.semaphore_wait(barrier, 7)

    for copy in f_wk:
        copy.wait()
    s.wk[z, 0:256, :] = s.u1[0].astype(BF)
    s.wk[z, 256:261, :] = s.u1[1, 0:5, :].astype(BF)
    half = pl.ds(pl.multiple_of(k * 144, 16), 144)
    wk_z = to_planes(lambda d: s.wk.at[z, half], lambda d: s.wk.at[z, half])
    s.cpair[k] = cot[...]
    x_cot = put(s.cpair.at[k], s.cpair.at[k], sib)

    def norm_pixels(i, carry):
        rows = pl.ds(pl.multiple_of(i * 256, 256), 256)
        s.xn2[k, rows, 256:CP] = jnp.zeros((256, CP - 256), BF)
        s.xn2[k, rows, 0:261] = (norm_parts(pix[rows, :].astype(F32))[0] * g_in[...]).astype(BF)
        return carry

    lax.fori_loop(0, 4, norm_pixels, 0)
    ln = (norm_parts(lat[...].astype(F32))[0] * g_lat[...]).astype(BF)
    s.ln[...] = ln
    for i in range(2):
        f_wq[i].wait()
        s.wq_z[128 * i : 128 * (i + 1), :] = s.hpa[i].astype(BF)
    wk_s_in = []
    for d in (1, 2, 3):
        wk_z[d].wait_recv()
        there = s.wk.at[plane[d], half]
        wk_s_in.append(put(there, there, sib))
    for copy in f_wv:
        copy.wait()
    s.wv_z[0:256, :] = s.u3[0].astype(BF)
    s.wv_z[256:261, :] = s.u3[1, 0:5, :].astype(BF)
    for i in range(2):
        f_wo[i].wait()
        s.wo_z[128 * i : 128 * (i + 1), :] = s.hpb[i].astype(BF)
    wvo_part = mm(s.wv_z[...], s.wo_z[:, lanes])
    s.wvz[0] = wvo_part[:CR].astype(BF)
    arrived(wk_s_in)
    own_rows = pl.ds(pl.multiple_of(k * 128, 128), 128)
    part = jnp.zeros((128, CP), F32)
    for j in range(4):
        part += mm_nt(s.wq_z[own_rows, 256 * j : 256 * (j + 1)], s.wk[j])
    s.wqk[z, k] = part.astype(BF)
    wqk_z = to_planes(lambda d: s.wqk.at[z, k], lambda d: s.wqk.at[z, k])
    wqk_s = [put(s.wqk.at[z, k], s.wqk.at[z, k], sib)]
    wvo_z = to_planes(lambda d: s.wvz.at[0], lambda d: s.wvz.at[d])
    x_xn = put(s.xn2.at[k], s.xn2.at[k], sib)

    for copy in f_u:
        copy.wait()
    for copy in f_d:
        copy.wait()
    own_z = pl.ds(pl.multiple_of(z * 256, 256), 256)
    for j in range(2):
        half_z = pl.ds(pl.multiple_of(z * 256 + 128 * j, 128), 128)
        s.wu1[p, half_z, :] = early(j)[...].astype(BF)
        s.wu3[p, half_z, :] = early(2 + j)[...].astype(BF)
        for i in range(3):
            s.wqkv[i, k, half_z, :] = early(4 + 2 * i + j)[...].astype(BF)
    s.wd1[z, p] = s.h3[0:32, :].astype(BF)
    s.wd3[z, p] = s.h3[32:64, :].astype(BF)
    f_os.wait()

    @pl.when(z == p)
    def _():
        s.wo[k] = s.hxa[...].astype(BF)

    for d in (1, 2, 3):
        wqk_z[d].wait_recv()
        there = s.wqk.at[plane[d], k]
        wqk_s.append(put(there, there, sib))
    wu1_z = to_planes(lambda d: s.wu1.at[p, own_z], lambda d: s.wu1.at[p, own_z])
    wd1_z = to_planes(lambda d: s.wd1.at[z, p], lambda d: s.wd1.at[z, p])
    arrived(wqk_s)
    wqk = s.wqk[...].reshape(D, CP)
    s.qk[p] = mm(ln, wqk).astype(BF)
    qk_in = to_peers(lambda d: s.qk.at[p], lambda d: s.qk.at[p])
    arrived(wvo_z)
    s.wvo[c, 0:CR, :] = sum(s.wvz[d].astype(F32) for d in range(4)).astype(BF)

    def wvo_slot(i):
        return s.wvo.at[i, 0:CR]

    wvo_in = gather(wvo_slot)
    qkv_z = to_planes(lambda d: s.wqkv.at[:, k, own_z], lambda d: s.wqkv.at[:, k, own_z])

    wo_slot = used[0]
    used[0] += 1
    wo_out = [make(s.wo.at[k], s.wo.at[k], level(d), wo_slot) for d in (1, 2, 3)]

    @pl.when(z == p)
    def _():
        for copy in wo_out:
            copy.start()

    sends.extend((z == p, copy) for copy in wo_out)
    wu3_z = to_planes(lambda d: s.wu3.at[p, own_z], lambda d: s.wu3.at[p, own_z])
    wd3_z = to_planes(lambda d: s.wd3.at[z, p], lambda d: s.wd3.at[z, p])
    x_xn.wait_recv()

    wide = lax.broadcasted_iota(jnp.int32, (128, 1024), 1)
    lane = lax.broadcasted_iota(jnp.int32, (128, CP), 1)

    def cross_block(q):
        rows = pl.ds(pl.multiple_of((2 * q + k) * 128, 128), 128)
        low, high = span[rows, 0:1], span[rows, 1:2]
        scores = []
        for h in range(2):
            at = wide + (2 * p + h) * 1024
            sc = mm_nt(s.qk[q], s.xn2[h]) * CROSS_SCALE
            scores.append(jnp.where((at >= low) & (at <= high), sc, MASKED))
        top = jnp.maximum(*(jnp.max(sc, axis=1, keepdims=True) for sc in scores))
        total = jnp.zeros((128, 1), F32)
        acc = jnp.zeros((128, CP), F32)
        for h in range(2):
            e = jnp.where(scores[h] > 0.5 * MASKED, jnp.exp(scores[h] - top), 0.0).astype(BF)
            s.ee[2 * q + h] = e
            total += jnp.sum(e.astype(F32), axis=1, keepdims=True)
            acc += mm(e, s.xn2[h])
        s.tops[q] = jnp.broadcast_to(top, (128, 128))
        s.pxs[q] = tag(acc, lane, top, total)

    cross_block(p)
    for d in (1, 2):
        qk_in[d].wait_recv()
    qk_in[3].wait_recv()
    px_in = {}
    for d in (3, 1, 2):
        cross_block(chip[d])
        px_in[d] = put(s.pxs.at[chip[d]], s.pxr.at[d - 1], peer(d))
    wvo_s = pass_on(wvo_slot, wvo_in)
    arrived(wu1_z)
    wu1_in = to_peers(lambda d: s.wu1.at[p], lambda d: s.wu1.at[p])
    arrived(wd1_z)
    wd1_in = to_peers(lambda d: s.wd1.at[:, p], lambda d: s.wd1.at[:, p])
    arrived(px_in)
    found = [untag(s.pxs[p], lane)] + [untag(s.pxr[i], lane) for i in range(3)]
    high = found[0][1]
    for f in found[1:]:
        high = jnp.maximum(high, f[1])
    px, total = jnp.zeros((128, CP), F32), jnp.zeros((128, 1), F32)
    for val, top, tot in found:
        share = jnp.exp(top - high)
        px += share * val
        total += share * tot
    px = px / total
    s.px[...] = px
    lse = high + jnp.log(total)
    s.pxl[...] = px.astype(BF)
    arrived(wvo_s)
    lat_f = lat[...].astype(F32)
    pxl = s.pxl[...]
    for j in range(4):
        cols = slice(256 * j, 256 * (j + 1))
        w = jnp.concatenate([s.wvo[2 * j], s.wvo[2 * j + 1]], axis=1)
        s.h1[:, cols] = lat[:, cols].astype(F32) + mm(pxl, w)

    def mlp_start(h_ref, gain, npair):
        npair[k] = (norm_parts(h_ref[...])[0] * gain[...]).astype(BF)
        return put(npair.at[k], npair.at[k], sib)

    def mlp_up(npair, wu, u, zb):
        rows = npair[...].reshape(256, D)
        for j in range(2):
            w = jnp.concatenate([wu[2 * j], wu[2 * j + 1]], axis=1)
            hidden = mm(rows, w)
            u[j] = hidden
            zb[j] = gelu(hidden).astype(BF)

    def mlp_down(zb, wd, hp, hx):
        for t in range(4):
            cols = slice(256 * t, 256 * (t + 1))
            acc = mm(zb[0], wd[0:2, :, :, cols].reshape(256, 256))
            acc += mm(zb[1], wd[2:4, :, :, cols].reshape(256, 256))
            hp[:, :, cols] = acc.reshape(2, 128, 256)
        return put(hp.at[k2], hx, sib)

    def mlp_back(gpair, wu, wd, u, gub, hp, hx):
        rows = gpair[...].reshape(256, D)
        for j in range(2):
            gz = mm_nt(rows, wd[2 * j : 2 * j + 2].reshape(256, D))
            gub[j] = (gz * gelu_slope(u[j])).astype(BF)
        for t in range(4):
            cols = slice(256 * t, 256 * (t + 1))
            acc = jnp.zeros((256, 256), F32)
            for j in range(2):
                w = jnp.concatenate([wu[2 * j, cols, :], wu[2 * j + 1, cols, :]], axis=1)
                acc += mm_nt(gub[j], w)
            hp[:, :, cols] = acc.reshape(2, 128, 256)
        return put(hp.at[k2], hx, sib)

    def mlp_grads(npair, gpair, zb, gub):
        for j in range(2):
            for t in range(4):
                cols = slice(256 * t, 256 * (t + 1))
                g = mm_tn(npair[:, :, cols].reshape(256, 256), gub[j]).astype(BF)
                s.gsu[2 * j, cols, :] = g[:, :128]
                s.gsu[2 * j + 1, cols, :] = g[:, 128:]
        up = to_peers(lambda d: s.gsu.at[chip[d]], lambda d: s.gru.at[d - 1])
        for j in range(2):
            for t in range(4):
                cols = slice(256 * t, 256 * (t + 1))
                g = mm_tn(zb[j], gpair[:, :, cols].reshape(256, 256)).astype(BF)
                s.gsd[2 * j : 2 * j + 2, :, :, cols] = g.reshape(2, 4, 32, 256)
        down = to_peers(lambda d: s.gsd.at[:, chip[d]], lambda d: s.grd.at[d - 1])
        return up, down

    def up_to_planes(up, zs, zr):
        arrived(up)
        total = s.gsu[p].astype(F32)
        for i in range(3):
            total += s.gru[i].astype(F32)
        zs[...] = total.astype(BF)
        return to_planes(
            lambda d: zs.at[pl.ds(pl.multiple_of(plane[d] * 256, 256), 256)], lambda d: zr.at[d - 1]
        )

    def down_to_planes(down, zs, zr):
        arrived(down)
        total = s.gsd[:, p].astype(F32)
        for i in range(3):
            total += s.grd[i].astype(F32)
        zs[...] = total.astype(BF)
        return to_planes(lambda d: zs.at[plane[d]], lambda d: zr.at[d - 1])

    def up_total(copies, zs, zr, ag):
        arrived(copies)
        total = zs[own_z, :].astype(F32)
        for i in range(3):
            total += zr[i].astype(F32)
        ag[c] = total.astype(BF)
        return gather(lambda i: ag.at[i])

    def row_slot(ag):
        return lambda i: ag.at[lax.rem(i, 2), lax.div(i, 2)]

    def down_total(copies, zs, zr, ag):
        arrived(copies)
        total = zs[z].astype(F32)
        for i in range(3):
            total += zr[i].astype(F32)
        ag[k, p] = total.astype(BF)
        return gather(row_slot(ag))

    outs = []

    def out_cols(ag, w):
        for j in range(8):
            outs.append(fetch(ag.at[j], d_big.at[w, :, 128 * j : 128 * (j + 1)]))

    def out_rows(ag, w):
        for kk in range(2):
            for q in range(4):
                at = 128 * kk + 32 * q
                outs.append(fetch(ag.at[kk, q], d_big.at[w, at : at + 32, :]))

    x_n1 = mlp_start(s.h1, g_cmlp, s.n1)
    arrived(wu1_in)
    x_n1.wait_recv()
    mlp_up(s.n1, s.wu1, s.u1, s.z1)
    arrived(wd1_in)
    x_h1 = mlp_down(s.z1, s.wd1, s.hpa, s.hxa)
    arrived(qkv_z)
    x_qkv = put(s.wqkv.at[:, k], s.wqkv.at[:, k], sib)
    x_h1.wait_recv()
    s.h2[...] = s.h1[...] + s.hpa[k] + s.hxa[...]

    s.n2[p] = (norm_parts(s.h2[...])[0] * g_self[...]).astype(BF)
    n2_in = to_peers(lambda d: s.n2.at[p], lambda d: s.n2.at[p])
    x_qkv.wait_recv()

    @pl.when(z != p)
    def _():
        wo_out[0].wait_recv()

    x_wo = put(s.wo.at[k], s.wo.at[k], sib)

    def project(q):
        rows = s.n2[q]
        for i in range(3):
            w = jnp.concatenate([s.wqkv[i, 0], s.wqkv[i, 1]], axis=1)
            s.pair[...] = mm(rows, w).astype(BF).reshape(128, 256)
            for h in range(2):
                s.heads[h, q, i] = s.pair[:, 128 * h : 128 * (h + 1)]
        s.mine[2 * q + k] = s.heads[k, q]
        return put(s.heads.at[k2, q], s.mine.at[2 * q + k], sib)

    qkv_in = [project(p)]
    for d in (1, 2, 3):
        n2_in[d].wait_recv()
        qkv_in.append(project(chip[d]))
    arrived(wu3_z)
    wu3_in = to_peers(lambda d: s.wu3.at[p], lambda d: s.wu3.at[p])
    arrived(wd3_z)
    wd3_in = to_peers(lambda d: s.wd3.at[:, p], lambda d: s.wd3.at[:, p])
    arrived(qkv_in)

    def attend(b):
        rows = pl.ds(pl.multiple_of(b * 128, 128), 128)
        keys = s.mine[:, 1].reshape(D, 128)
        sc = mm_nt(s.mine[b, 0], keys) * SELF_SCALE
        at = pos_r[...]
        sc = jnp.where((at >= span[rows, 0:1]) & (at <= span[rows, 1:2]), sc, MASKED)
        e = jnp.exp(sc - jnp.max(sc, axis=1, keepdims=True))
        low = (e / jnp.sum(e, axis=1, keepdims=True)).astype(BF)
        s.a1[b] = low
        return mm(low, s.mine[:, 2].reshape(D, 128)).astype(BF)

    def other_rows(q, carry):
        s.send[q] = attend(2 * q + k2)
        return carry

    def own_parity(q, carry):
        s.aspar[q, k] = attend(2 * q + k)
        return carry

    lax.fori_loop(0, 4, other_rows, 0)
    x_as = put(s.send, s.aspar.at[:, k], sib)
    lax.fori_loop(0, 4, own_parity, 0)
    x_wo.wait_recv()
    x_as.wait_recv()

    def both(ref, q):
        return jnp.concatenate([ref[q, 0], ref[q, 1]], axis=1)

    out_in = {}
    for d in (3, 1, 2):
        s.outp[d - 1] = mm(both(s.aspar, chip[d]), s.wo[...].reshape(256, D)).astype(BF)
        out_in[d] = put(s.outp.at[d - 1], s.outr.at[d - 1], peer(d))
    s.h3[...] = s.h2[...] + mm(both(s.aspar, p), s.wo[...].reshape(256, D))
    arrived(out_in)
    s.h3[...] += sum(s.outr[i].astype(F32) for i in range(3))

    x_n3 = mlp_start(s.h3, g_smlp, s.n3)
    arrived(wu3_in)
    x_n3.wait_recv()
    mlp_up(s.n3, s.wu3, s.u3, s.z3)
    arrived(wd3_in)
    x_cot.wait_recv()
    sent([x_h1])
    x_d3 = mlp_back(s.cpair, s.wu3, s.wd3, s.u3, s.gu3, s.hpa, s.hxa)
    x_h3 = mlp_down(s.z3, s.wd3, s.hpb, s.hxb)
    x_d3.wait_recv()
    dx, gg_smlp = norm_back(s.hpa[k] + s.hxa[...], s.h3[...], g_smlp[...])
    dh3 = cot[...].astype(F32) + dx
    s.dh[...] = dh3
    s.go[p] = dh3.astype(BF)
    go_in = to_peers(lambda d: s.go.at[p], lambda d: s.go.at[p])
    g3 = mlp_grads(s.n3, s.cpair, s.z3, s.gu3)
    x_h3.wait_recv()
    layer_out[...] = (s.h3[...] + s.hpb[k] + s.hxb[...]).astype(BF)

    def pull_out(q):
        g = mm_nt(s.go[q], s.wo[...].reshape(256, D)).astype(BF)
        s.pair[...] = g
        for h in range(2):
            s.gheads[h, q] = s.pair[:, 128 * h : 128 * (h + 1)]
        s.gmine[2 * q + k] = s.gheads[k, q]
        return put(s.gheads.at[k2, q], s.gmine.at[2 * q + k], sib)

    gas_in = [pull_out(p)]
    for d in (1, 2, 3):
        go_in[d].wait_recv()
        gas_in.append(pull_out(chip[d]))
    arrived(gas_in)

    def attend_back(b, carry):
        dps = mm_nt(s.gmine[b], s.mine[:, 2].reshape(D, 128))
        probs = s.a1[b].astype(F32)
        delta = jnp.sum(probs * dps, axis=1, keepdims=True) / jnp.sum(probs, axis=1, keepdims=True)
        dss = (probs * (dps - delta) * SELF_SCALE).astype(BF)
        s.a2[b] = dss
        s.heads[lax.div(b, 4), lax.rem(b, 4), 0] = mm(dss, s.mine[:, 1].reshape(D, 128)).astype(BF)
        return carry

    sent(qkv_in)
    lax.fori_loop(0, 8, attend_back, 0)
    for t in range(4):
        cols = slice(256 * t, 256 * (t + 1))
        dk = mm_tn(s.a2[:, :, cols].reshape(D, 256), s.mine[:, 0].reshape(D, 128))
        dv = mm_tn(s.a1[:, :, cols].reshape(D, 256), s.gmine[...].reshape(D, 128))
        two = slice(2 * (t % 2), 2 * (t % 2) + 2)
        s.heads[t // 2, two, 1] = dk.astype(BF).reshape(2, 128, 128)
        s.heads[t // 2, two, 2] = dv.astype(BF).reshape(2, 128, 128)

    def sort(q, carry):
        high, low = lax.div(q, 2), 2 * lax.rem(q, 2)
        s.dsend[q] = s.heads[high, low + k2]
        for i in range(3):
            s.dpar[q, i, k] = s.heads[high, low + k, i]
        return carry

    lax.fori_loop(0, 4, sort, 0)
    x_dp = put(s.dsend, s.dpar.at[:, :, k], sib)
    g3u_z = up_to_planes(g3[0], s.su3, s.zu3)
    g3d_z = down_to_planes(g3[1], s.sd3, s.zd3)
    x_dp.wait_recv()

    def pull_in(q, write):
        for t in range(4):
            cols = slice(256 * t, 256 * (t + 1))
            acc = jnp.zeros((128, 256), F32)
            for i in range(3):
                w = jnp.concatenate([s.wqkv[i, 0, cols, :], s.wqkv[i, 1, cols, :]], axis=1)
                acc += mm_nt(jnp.concatenate([s.dpar[q, i, 0], s.dpar[q, i, 1]], axis=1), w)
            write(cols, acc)

    sent(out_in)
    dn_in = {}
    for d in (3, 1, 2):

        def write(cols, acc):
            s.outp[d - 1, :, cols] = acc.astype(BF)

        pull_in(chip[d], write)
        dn_in[d] = put(s.outp.at[d - 1], s.outr.at[d - 1], peer(d))

    def write(cols, acc):
        s.tmp[:, cols] = acc

    pull_in(p, write)
    for i in range(3):
        g = jnp.concatenate([s.dpar[:, i, 0].reshape(PARITY_ROWS, 128), s.dpar[:, i, 1].reshape(PARITY_ROWS, 128)], axis=1)
        for t in range(4):
            cols = slice(256 * t, 256 * (t + 1))
            w = mm_tn(s.n2[:, :, cols].reshape(PARITY_ROWS, 256), g).astype(BF)
            for h in range(2):
                s.pg[i, h, cols, :] = w[:, 128 * h : 128 * (h + 1)]
    x_pg = put(s.pg.at[:, k2], s.pgr, sib)
    g = jnp.concatenate([s.aspar[:, 0].reshape(PARITY_ROWS, 128), s.aspar[:, 1].reshape(PARITY_ROWS, 128)], axis=1)
    for t in range(4):
        cols = slice(256 * t, 256 * (t + 1))
        w = mm_tn(g, s.go[:, :, cols].reshape(PARITY_ROWS, 256)).astype(BF)
        s.pgo[:, :, cols] = w.reshape(2, 128, 256)
    x_pgo = put(s.pgo.at[k2], s.pgor, sib)
    arrived(dn_in)
    dn2 = s.tmp[...] + sum(s.outr[i].astype(F32) for i in range(3))
    dx, gg_self = norm_back(dn2, s.h2[...], g_self[...])
    s.dh[...] += dx

    sent([x_cot])
    s.cpair[k] = s.dh[...].astype(BF)
    x_g = put(s.cpair.at[k], s.cpair.at[k], sib)
    x_pg.wait_recv()
    for i in range(3):
        s.pg[i, k] = (s.pg[i, k].astype(F32) + s.pgr[i].astype(F32)).astype(BF)
    pg_z = to_planes(
        lambda d: s.pg.at[:, k, pl.ds(pl.multiple_of(plane[d] * 256, 256), 256)],
        lambda d: s.zq.at[d - 1],
    )
    x_g.wait_recv()
    sent([x_d3])
    x_d1 = mlp_back(s.cpair, s.wu1, s.wd1, s.u1, s.gu1, s.hpa, s.hxa)
    x_pgo.wait_recv()
    s.pgo[k] = (s.pgo[k].astype(F32) + s.pgor[...].astype(F32)).astype(BF)
    pgo_z = {d: make(s.pgo.at[k], s.zo.at[d - 1], level(d)) for d in (1, 2, 3)}
    for d in (1, 2, 3):
        pl.when(plane[d] == p)(pgo_z[d].start)
        sends.append((plane[d] == p, pgo_z[d]))
    x_d1.wait_recv()
    dx, gg_cmlp = norm_back(s.hpa[k] + s.hxa[...], s.h1[...], g_cmlp[...])
    dh1 = s.dh[...] + dx
    s.dh[...] = dh1

    go1 = dh1.astype(BF)
    gv = jnp.zeros((128, CP), F32)
    for j in range(4):
        w = jnp.concatenate([s.wvo[2 * j], s.wvo[2 * j + 1]], axis=1)
        gv += mm_nt(go1[:, 256 * j : 256 * (j + 1)], w)
    gv = gv.astype(BF).astype(F32)
    delta = jnp.sum(jnp.where(lane < 261, s.px[...] * gv, 0.0), axis=1, keepdims=True)
    s.gv[p] = tag(gv, lane, lse, delta)
    gv_in = to_peers(lambda d: s.gv.at[p], lambda d: s.gv.at[p])
    sent(g3[0])
    sent(g3[1])
    g1 = mlp_grads(s.n1, s.cpair, s.z1, s.gu1)
    for j in range(4):
        f_part = mm_tn(s.pxl[...], go1[:, 256 * j : 256 * (j + 1)])[:CR].astype(BF)
        s.fst[j, 0] = f_part[:, :128]
        s.fst[j, 1] = f_part[:, 128:]
    x_f = put(s.fst.at[:, k2], s.fsr, sib)

    def cross_back(q):
        val, last, delta = untag(s.gv[q], lane)
        ratio = jnp.exp(s.tops[q][:, 0:1] - last)
        s.gvr[q] = (val * ratio).astype(BF)
        acc = jnp.zeros((128, CP), F32)
        for h in range(2):
            dp = mm_nt(s.gv[q], s.xn2[h])
            ds = (s.ee[2 * q + h].astype(F32) * ((dp - delta) * (ratio * CROSS_SCALE))).astype(BF)
            s.a2[2 * q + h] = ds
            acc += mm(ds, s.xn2[h])
        s.pxs[q] = acc.astype(BF)
        return acc

    sent(px_in)
    s.dqk[...] = cross_back(p)
    dq_in = {}
    for d in (1, 2, 3):
        gv_in[d].wait_recv()
        cross_back(chip[d])
        dq_in[d] = put(s.pxs.at[chip[d]], s.pxr.at[d - 1], peer(d))

    def pixel_rows(h, t):
        cols = slice(256 * t, 256 * (t + 1))
        ds = jnp.concatenate([s.a2[2 * q + h, :, cols] for q in range(4)], axis=0)
        e = jnp.concatenate([s.ee[2 * q + h, :, cols] for q in range(4)], axis=0)
        return mm_tn(ds, s.qk[...].reshape(PARITY_ROWS, CP)) + mm_tn(e, s.gvr[...].reshape(PARITY_ROWS, CP))

    for t in range(4):
        s.dxs[256 * t : 256 * (t + 1), :] = pixel_rows(k2, t).astype(BF)
    x_dx = put(s.dxs, s.dxr, sib)
    arrived(dq_in)
    dqk = (s.dqk[...] + sum(s.pxr[i].astype(F32) for i in range(3))).astype(BF)
    for j in range(8):
        e = mm_tn(s.ln[:, 128 * j : 128 * (j + 1)], dqk).astype(BF)
        s.est[j // 2, 2 * (j % 2) : 2 * (j % 2) + 2] = e.reshape(2, 2, 32, CP)
    x_e = put(s.est.at[:, :, k2], s.esr, sib)
    dx, gg_lat = norm_back(mm_nt(dqk, s.wqk[...].reshape(D, CP)), lat[...].astype(F32), g_lat[...])
    s.dh[...] += dx
    outs.append(fetch(s.dh, d_lat))
    x_e.wait_recv()
    s.est[:, :, k] = (s.est[:, :, k].astype(F32) + s.esr[...].astype(F32)).astype(BF)
    e_in = to_peers(lambda d: s.est.at[:, chip[d], k], lambda d: s.epr.at[d - 1])
    x_f.wait_recv()
    s.fst[:, k] = (s.fst[:, k].astype(F32) + s.fsr[...].astype(F32)).astype(BF)
    f_in = to_peers(lambda d: s.fst.at[chip[d], k], lambda d: s.fpr.at[d - 1])

    x_dx.wait_recv()
    gg_in = jnp.zeros((1, 261), F32)
    for t in range(4):
        rows = slice(256 * t, 256 * (t + 1))
        dxn = pixel_rows(k, t) + s.dxr[rows, :].astype(F32)
        dx, gg = norm_back(dxn[:, :261], pix[rows, :].astype(F32), g_in[...])
        d_pix[rows, :] = dx
        gg_in += gg
    s.ga[k] = jnp.zeros((8, D), F32)
    s.ga[k, 0:1, 0:261] = gg_in
    for i, gg in enumerate((gg_lat, gg_cmlp, gg_self, gg_smlp)):
        s.ga[k, i + 1 : i + 2, :] = gg
    x_ga = put(s.ga.at[k], s.ga.at[k], sib)

    arrived(e_in)
    total = s.est[:, p, k].astype(F32)
    for i in range(3):
        total += s.epr[i].astype(F32)
    s.ez[...] = total.astype(BF)
    e_z = to_planes(lambda d: s.ez.at[plane[d]], lambda d: s.ezr.at[d - 1])
    x_ga.wait_recv()
    s.gb[p] = s.ga[0] + s.ga[1]
    gb_in = to_peers(lambda d: s.gb.at[p], lambda d: s.gb.at[p])
    arrived(f_in)
    total = s.fst[p, k].astype(F32)
    for i in range(3):
        total += s.fpr[i].astype(F32)
    s.fz[0] = total.astype(BF)
    f_z = to_planes(lambda d: s.fz.at[0], lambda d: s.fz.at[d])
    arrived(e_z)
    total = s.ez[z].astype(F32)
    for i in range(3):
        total += s.ezr[i].astype(F32)
    s.eag[c] = total.astype(BF)
    e_ag = gather(lambda i: s.eag.at[i])
    arrived(gb_in)
    s.gc[z] = s.gb[0] + s.gb[1] + s.gb[2] + s.gb[3]
    gc_in = to_planes(lambda d: s.gc.at[z], lambda d: s.gc.at[z])
    arrived(f_z)
    s.fag[c, 0:CR, :] = sum(s.fz[d].astype(F32) for d in range(4)).astype(BF)

    def f_slot(i):
        return s.fag.at[i, 0:CR]

    f_ag = gather(f_slot)
    e_s = pass_on(lambda i: s.eag.at[i], e_ag)
    g1u_z = up_to_planes(g1[0], s.su1, s.zu1)
    g1d_z = down_to_planes(g1[1], s.sd1, s.zd1)
    arrived(e_s)
    e_all = s.eag[...].reshape(256, CP)
    for j in range(4):
        s.gks[j] = mm_tn(e_all, s.wq_z[:, 256 * j : 256 * (j + 1)])[:CR].astype(BF)
    gk_z = to_planes(lambda d: s.gks.at[plane[d], half], lambda d: s.gkr.at[d - 1])
    sent([x_d1])
    for j in range(4):
        s.hpa[:, :, 256 * j : 256 * (j + 1)] = mm(e_all, s.wk[j]).reshape(2, 128, 256)
    outs.extend(fetch(s.hpa.at[i], d_wq.at[128 * i : 128 * (i + 1)]) for i in range(2))
    g3u_ag = up_total(g3u_z, s.su3, s.zu3, s.agu3)
    g3d_ag = down_total(g3d_z, s.sd3, s.zd3, s.agd3)
    f_s = pass_on(f_slot, f_ag)

    arrived(pg_z)
    for i in range(3):
        total = s.pg[i, k, own_z, :].astype(F32)
        for d in range(3):
            total += s.zq[d, i].astype(F32)
        s.agq[c, i] = total.astype(BF)
    q_ag = gather(lambda i: s.agq.at[i])

    o_recv = {d: make(s.ago.at[k], s.ago.at[k], peer(d)) for d in (1, 2, 3)}

    @pl.when(z == p)
    def _():
        total = s.pgo[k].astype(F32)
        for d in (1, 2, 3):
            pgo_z[d].wait_recv()
            total += s.zo[d - 1].astype(F32)
        s.ago[k] = total.astype(BF)
        for d in (1, 2, 3):
            o_recv[d].start()

    sends.extend((z == p, copy) for copy in o_recv.values())
    for d in (1, 2, 3):
        pl.when(chip[d] == z)(o_recv[d].wait_recv)
    x_o = put(s.ago.at[k], s.ago.at[k], sib)

    arrived(gk_z)
    total = s.gks[z, half, :].astype(F32)
    for i in range(3):
        total += s.gkr[i].astype(F32)
    s.gkh[half, :] = total
    x_gk = put(s.gkh.at[half], s.gkh.at[half], sib)
    g1u_ag = up_total(g1u_z, s.su1, s.zu1, s.agu1)
    g1d_ag = down_total(g1d_z, s.sd1, s.zd1, s.agd1)
    arrived(f_s)
    sent([x_h3])
    acc = jnp.zeros((CP, 256), F32)
    for j in range(4):
        f_two = jnp.concatenate([s.fag[2 * j], s.fag[2 * j + 1]], axis=1)
        acc += mm_nt(f_two, s.wo_z[:, 256 * j : 256 * (j + 1)])
        s.hpb[:, :, 256 * j : 256 * (j + 1)] = mm_tn(s.wv_z[...], f_two).reshape(2, 128, 256)
    d_wv[...] = acc[:261]
    outs.extend(fetch(s.hpb.at[i], d_wo.at[128 * i : 128 * (i + 1)]) for i in range(2))
    arrived(gc_in)
    d_gain[...] = s.gc[0] + s.gc[1] + s.gc[2] + s.gc[3]

    g3u_s = pass_on(lambda i: s.agu3.at[i], g3u_ag)
    g3d_s = pass_on(row_slot(s.agd3), g3d_ag)
    q_s = pass_on(lambda i: s.agq.at[i], q_ag)
    g1u_s = pass_on(lambda i: s.agu1.at[i], g1u_ag)
    g1d_s = pass_on(row_slot(s.agd1), g1d_ag)
    x_gk.wait_recv()
    d_wk[...] = s.gkh[0:261, :]
    arrived(g3u_s)
    out_cols(s.agu3, 6)
    arrived(g3d_s)
    out_rows(s.agd3, 7)
    arrived(q_s)
    for i in range(3):
        for j in range(8):
            outs.append(fetch(s.agq.at[j, i], d_big.at[2 + i, :, 128 * j : 128 * (j + 1)]))
    x_o.wait_recv()
    for h in range(2):
        outs.append(fetch(s.ago.at[h], d_big.at[5, 128 * h : 128 * (h + 1), :]))
    arrived(g1u_s)
    out_cols(s.agu1, 0)
    arrived(g1d_s)
    out_rows(s.agd1, 1)
    for copy in outs:
        copy.wait()
    for when, copy in sends:
        if when is None:
            copy.wait_send()
        else:
            pl.when(when)(copy.wait_send)


def tag(val, lane, one, two):
    for i, x in enumerate((one, two)):
        for j in range(3):
            part = x.astype(BF).astype(F32)
            val = jnp.where(lane == 261 + 3 * i + j, part, val)
            x = x - part
    return val.astype(BF)


def untag(low, lane):
    val = low.astype(F32)

    def column(i):
        here = (lane >= 261 + 3 * i) & (lane < 264 + 3 * i)
        return jnp.sum(jnp.where(here, val, 0.0), axis=1, keepdims=True)

    return jnp.where(lane < 261, val, 0.0), column(0), column(1)


SCRATCH = {
    "ssem": 400, "rsem": 400, "lsem": 96,

    "wk": ((4, CP, 256), BF), "wqk": ((4, 2, 128, CP), BF), "wq_z": ((256, 1024), BF), "wo_z": ((256, 1024), BF),
    "wv_z": ((CP, 256), BF), "wvz": ((4, CR, 128), BF), "wvo": ((8, CP, 128), BF),
    "wu1": ((4, 1024, 128), BF), "wu3": ((4, 1024, 128), BF), "wd1": ((4, 4, 32, 1024), BF), "wd3": ((4, 4, 32, 1024), BF),
    "wqkv": ((3, 2, 1024, 128), BF), "wo": ((2, 128, 1024), BF),
    "xn2": ((2, 1024, CP), BF), "ln": ((128, 1024), BF), "qk": ((4, 128, CP), BF),
    "pxs": ((4, 128, CP), BF), "pxr": ((3, 128, CP), BF), "px": ((128, CP), F32), "pxl": ((128, CP), BF),
    "cpair": ((2, 128, 1024), BF), "n1": ((2, 128, 1024), BF), "n3": ((2, 128, 1024), BF),
    "u1": ((2, 256, 256), F32), "u3": ((2, 256, 256), F32), "z1": ((2, 256, 256), BF), "z3": ((2, 256, 256), BF),
    "gu1": ((2, 256, 256), BF), "gu3": ((2, 256, 256), BF),


    "h1": ((128, 1024), F32), "h2": ((128, 1024), F32), "h3": ((128, 1024), F32), "dh": ((128, 1024), F32), "tmp": ((128, 1024), F32),
    "n2": ((4, 128, 1024), BF), "go": ((4, 128, 1024), BF), "pair": ((128, 256), BF),
    "heads": ((2, 4, 3, 128, 128), BF), "mine": ((8, 3, 128, 128), BF),
    "a1": ((8, 128, 1024), BF), "a2": ((8, 128, 1024), BF), "send": ((4, 128, 128), BF), "aspar": ((4, 2, 128, 128), BF),
    "outp": ((3, 128, 1024), BF), "outr": ((3, 128, 1024), BF),
    "gheads": ((2, 4, 128, 128), BF), "gmine": ((8, 128, 128), BF),
    "dsend": ((4, 3, 128, 128), BF), "dpar": ((4, 3, 2, 128, 128), BF),


    "zu1": ((3, 256, 128), BF), "zu3": ((3, 256, 128), BF), "zd1": ((3, 32, 1024), BF), "zd3": ((3, 32, 1024), BF),
    "agu1": ((8, 256, 128), BF), "agu3": ((8, 256, 128), BF), "agd1": ((2, 4, 32, 1024), BF), "agd3": ((2, 4, 32, 1024), BF),
    "pg": ((3, 2, 1024, 128), BF), "pgr": ((3, 1024, 128), BF), "zq": ((3, 3, 256, 128), BF), "agq": ((8, 3, 256, 128), BF),
    "pgo": ((2, 128, 1024), BF), "pgor": ((128, 1024), BF), "zo": ((3, 128, 1024), BF), "ago": ((2, 128, 1024), BF),
    "gv": ((4, 128, CP), BF), "dqk": ((128, CP), F32),
    "dxs": ((1024, CP), BF), "dxr": ((1024, CP), BF),
    "fst": ((4, 2, CR, 128), BF), "fsr": ((4, CR, 128), BF), "fpr": ((3, CR, 128), BF), "fz": ((4, CR, 128), BF), "fag": ((8, CP, 128), BF),
    "est": ((4, 4, 2, 32, CP), BF), "esr": ((4, 4, 32, CP), BF), "epr": ((3, 4, 32, CP), BF), "ez": ((4, 32, CP), BF),
    "ezr": ((3, 32, CP), BF), "eag": ((8, 32, CP), BF),
    "gks": ((4, CR, 256), BF), "gkr": ((3, 144, 256), BF), "gkh": ((CR, 256), F32),
    "ga": ((2, 8, 1024), F32), "gb": ((4, 8, 1024), F32), "gc": ((4, 8, 1024), F32),
    "hpa": ((2, 128, 1024), F32), "hpb": ((2, 128, 1024), F32), "hxa": ((128, 1024), F32), "hxb": ((128, 1024), F32),
    "ee": ((8, 128, 1024), BF), "tops": ((4, 128, 128), F32), "gvr": ((4, 128, CP), BF),
    "gsu": ((4, 1024, 128), BF), "gsd": ((4, 4, 32, 1024), BF), "gru": ((3, 1024, 128), BF), "grd": ((3, 4, 32, 1024), BF),
    "su1": ((1024, 128), BF), "su3": ((1024, 128), BF), "sd1": ((4, 32, 1024), BF), "sd3": ((4, 32, 1024), BF),
}


def one_kernel(
    pixels, latents, cotangent, doc_lengths, latent_offsets, block_deal,
    wq_c, wk_c, wv_c, wo_c, wu_c, wd_c, wq_s, wk_s, wv_s, wo_s, wu_s, wd_s,
    g_in, g_lat, g_cmlp, g_self, g_smlp,
):
    lo, pos = intervals(doc_lengths[0], latent_offsets[0], block_deal)
    vmem, hbm = pl.BlockSpec(memory_space=pltpu.VMEM), pl.BlockSpec(memory_space=pl.ANY)

    def shape(dims, kind=F32):
        return jax.ShapeDtypeStruct(dims, kind)

    outs = pl.pallas_call(
        fused,
        out_shape=(
            shape((128, D), BF), shape((1024, 261)), shape((128, D)), shape((256, D)), shape((261, 256)),
            shape((261, 256)), shape((256, D)), shape((8, 256, D), BF), shape((8, D)),
        ),
        in_specs=[vmem] * 10 + [hbm] * 12,
        out_specs=(vmem, vmem, hbm, hbm, vmem, vmem, hbm, hbm, vmem),
        scratch_shapes=[
            pltpu.SemaphoreType.DMA((what,)) if isinstance(what, int) else pltpu.VMEM(*what)
            for what in SCRATCH.values()
        ],
        compiler_params=pltpu.CompilerParams(
            collective_id=0, has_side_effects=True, vmem_limit_bytes=VMEM_BYTES
        ),
        cost_estimate=pl.CostEstimate(flops=26 * 10**9, bytes_accessed=40 * 10**6, transcendentals=10**7),
    )(
        pixels[0], latents[0], cotangent[0], jnp.stack([lo, pos], axis=1), pos[None, :],
        g_in[None], g_lat[None], g_cmlp[None], g_self[None], g_smlp[None],
        wq_c, wk_c, wv_c, wo_c, wu_c, wd_c, wq_s, wk_s, wv_s, wo_s, wu_s, wd_s,
    )
    layer_out, d_pix, d_lat, d_wq, d_wk, d_wv, d_wo, big, gains = outs
    return (
        layer_out[None], d_pix[None], d_lat[None], d_wq, d_wk, d_wv, d_wo,
        *(big[i].astype(F32) for i in range(8)), gains[0, :261], *(gains[i] for i in range(1, 5)),
    )


VMEM_BYTES = 65472 * 2**10


def solution(mesh):
    rows, row, col, all_ = P("fsdp", "ctx", None), P("fsdp", None), P(None, "fsdp"), P()
    weights = (row, col, col, *(row,) * 9)
    small = mesh.shape["ctx"] == 8 and mesh.shape["fsdp"] == 4
    return jax.shard_map(
        one_kernel if small else plain,
        mesh=mesh,
        in_specs=(rows, rows, rows, row, row, all_, *weights, *(all_,) * 5),
        out_specs=(rows, rows, rows, *weights, *(all_,) * 5),
        check_vma=False,
    )
```

```python
import math
import types

import jax
import jax.numpy as jnp
from jax import lax
from jax.experimental import pallas as pl
from jax.experimental.pallas import tpu as pltpu
from jax.sharding import PartitionSpec as P

D = 1024
HEADS = 8
HEAD = D // HEADS
STRIDE = 8
LBLK = 64
BF = jnp.bfloat16
F32 = jnp.float32
CROSS_SCALE = 1.0 / math.sqrt(D)
SELF_SCALE = 1.0 / math.sqrt(HEAD)
MASKED = -1e30
GELU_K = math.sqrt(2.0 / math.pi)
GELU_A = 0.044715


def mm(a, b):
    return jnp.dot(a, b, preferred_element_type=F32)


def mm_nt(a, b):
    return lax.dot_general(a, b, (((1,), (1,)), ((), ())), preferred_element_type=F32)


def mm_tn(a, b):
    return lax.dot_general(a, b, (((0,), (0,)), ((), ())), preferred_element_type=F32)


def norm_parts(x):
    center = x - jnp.mean(x, axis=-1, keepdims=True)
    r = lax.rsqrt(jnp.mean(center * center, axis=-1, keepdims=True) + 1e-05)
    return center * r, r


def norm_back(dy, x, gain):
    hat, r = norm_parts(x)
    dhat = dy * gain
    dx = r * (
        dhat
        - jnp.mean(dhat, axis=-1, keepdims=True)
        - hat * jnp.mean(dhat * hat, axis=-1, keepdims=True)
    )
    return dx, jnp.sum(dy * hat, axis=0, keepdims=True)


def gelu(u):
    return 0.5 * u * (1.0 + jnp.tanh(GELU_K * (u + GELU_A * u * u * u)))


def gelu_slope(u):
    t = jnp.tanh(GELU_K * (u + GELU_A * u * u * u))
    return 0.5 * (1.0 + t) + 0.5 * u * (1.0 - t * t) * GELU_K * (1.0 + 3.0 * GELU_A * u * u)


def intervals(lengths, offsets, deal):
    count = lengths.shape[0]
    before = jnp.arange(count)[:, None] > jnp.arange(count)[None, :]
    starts = jnp.sum(jnp.where(before, lengths[None, :], 0), axis=1)
    base = (deal[:, None] * LBLK + jnp.arange(LBLK, dtype=jnp.int32)[None, :]).reshape(-1)
    pos = base * STRIDE + offsets
    lo = jnp.max(jnp.where(starts[None, :] <= pos[:, None], starts[None, :], -1), axis=1)
    return lo, pos


def plain(
    pixels, latents, cotangent, doc_lengths, latent_offsets, block_deal,
    wq_c, wk_c, wv_c, wo_c, wu_c, wd_c, wq_s, wk_s, wv_s, wo_s, wu_s, wd_s,
    g_in, g_lat, g_cmlp, g_self, g_smlp,
):
    n = lax.axis_size("ctx")
    me = lax.axis_index("ctx")
    rows = latents.shape[1]
    npix = pixels.shape[1]
    c = pixels.shape[2]
    lo, pos = intervals(doc_lengths[0], latent_offsets[0], block_deal)
    own_lo = lax.dynamic_slice_in_dim(lo, me * rows, rows)
    own_pos = lax.dynamic_slice_in_dim(pos, me * rows, rows)
    pix_pos = me * npix + jnp.arange(npix, dtype=jnp.int32)
    mask = (lo[:, None] <= pix_pos[None, :]) & (pix_pos[None, :] <= pos[:, None])
    smask = (own_lo[:, None] <= pos[None, :]) & (pos[None, :] <= own_pos[:, None])

    wq_c, wk_c, wv_c, wo_c = (w.astype(BF) for w in (wq_c, wk_c, wv_c, wo_c))
    wk_all = lax.all_gather(wk_c, "fsdp", axis=1, tiled=True)
    wqk = lax.all_gather(mm_nt(wq_c, wk_all).astype(BF), "fsdp", axis=0, tiled=True)
    wvo = lax.psum(mm(wv_c, wo_c), "fsdp").astype(BF)
    big = jnp.stack([w.astype(BF) for w in (wu_c, wd_c, wq_s, wk_s, wv_s, wo_s, wu_s, wd_s)])
    wu1, wd1, wq, wk, wv, wo, wu3, wd3 = lax.all_gather(big, "fsdp", axis=1, tiled=True)

    xin = pixels[0].astype(F32)
    xn = (norm_parts(xin)[0] * g_in).astype(BF)
    lat = latents[0].astype(F32)
    ln = (norm_parts(lat)[0] * g_lat).astype(BF)
    qk_all = lax.all_gather(mm(ln, wqk).astype(BF), "ctx", axis=0, tiled=True)
    s = jnp.where(mask, mm_nt(qk_all, xn) * CROSS_SCALE, MASKED)
    top = jnp.max(s, axis=1, keepdims=True)
    e = lax.optimization_barrier(jnp.where(mask, jnp.exp(s - top), 0.0).astype(BF))
    total = jnp.sum(e.astype(F32), axis=1, keepdims=True)
    part = jnp.concatenate([mm(e, xn), top, total], axis=1)
    parts = lax.all_to_all(part.reshape(n, rows, c + 2), "ctx", 0, 0)
    tops = parts[:, :, c : c + 1]
    high = jnp.max(tops, axis=0)
    share = jnp.exp(tops - high[None])
    full = jnp.sum(share * parts[:, :, c + 1 :], axis=0)
    px = jnp.sum(share * parts[:, :, :c], axis=0) / full
    lse = high + jnp.log(full)
    px_low = px.astype(BF)
    h1 = lat + mm(px_low, wvo)
    n1 = (norm_parts(h1)[0] * g_cmlp).astype(BF)
    u1 = mm(n1, wu1)
    z1 = gelu(u1).astype(BF)
    h2 = h1 + mm(z1, wd1)
    n2 = (norm_parts(h2)[0] * g_self).astype(BF)
    q = mm(n2, wq).astype(BF).reshape(rows, HEADS, HEAD)
    kv = jnp.concatenate([mm(n2, wk), mm(n2, wv)], axis=1).astype(BF)
    kv = lax.all_gather(kv, "ctx", axis=0, tiled=True)
    k = kv[:, :D].reshape(n * rows, HEADS, HEAD)
    v = kv[:, D:].reshape(n * rows, HEADS, HEAD)
    ss = jnp.einsum("qhd,khd->hqk", q, k, preferred_element_type=F32) * SELF_SCALE
    ss = jnp.where(smask[None], ss, MASKED)
    se = jnp.exp(ss - jnp.max(ss, axis=-1, keepdims=True))
    ps = se / jnp.sum(se, axis=-1, keepdims=True)
    psl = ps.astype(BF)
    sa = jnp.einsum("hqk,khd->qhd", psl, v, preferred_element_type=F32)
    sa = sa.reshape(rows, D).astype(BF)
    h3 = h2 + mm(sa, wo)
    n3 = (norm_parts(h3)[0] * g_smlp).astype(BF)
    u3 = mm(n3, wu3)
    z3 = gelu(u3).astype(BF)
    layer_out = (h3 + mm(z3, wd3)).astype(BF)

    gy3 = cotangent[0]
    gu3 = (mm_nt(gy3, wd3) * gelu_slope(u3)).astype(BF)
    dx, gg_smlp = norm_back(mm_nt(gu3, wu3), h3, g_smlp)
    dh3 = gy3.astype(F32) + dx
    go3 = dh3.astype(BF)
    gas = mm_nt(go3, wo).astype(BF).reshape(rows, HEADS, HEAD)
    dps = jnp.einsum("qhd,khd->hqk", gas, v, preferred_element_type=F32)
    sdelta = jnp.sum(ps * dps, axis=-1, keepdims=True)
    dss = (ps * (dps - sdelta) * SELF_SCALE).astype(BF)
    dqs = jnp.einsum("hqk,khd->qhd", dss, k, preferred_element_type=F32)
    dqs = dqs.reshape(rows, D).astype(BF)
    dks = jnp.einsum("hqk,qhd->khd", dss, q, preferred_element_type=F32).reshape(n * rows, D)
    dvs = jnp.einsum("hqk,qhd->khd", psl, gas, preferred_element_type=F32).reshape(n * rows, D)
    dkv = lax.psum_scatter(
        jnp.concatenate([dks, dvs], axis=1), "ctx", scatter_dimension=0, tiled=True
    ).astype(BF)
    dks, dvs = dkv[:, :D], dkv[:, D:]
    dn2 = mm_nt(dqs, wq) + mm_nt(dks, wk) + mm_nt(dvs, wv)
    dx, gg_self = norm_back(dn2, h2, g_self)
    dh2 = dh3 + dx
    gy1 = dh2.astype(BF)
    gu1 = (mm_nt(gy1, wd1) * gelu_slope(u1)).astype(BF)
    dx, gg_cmlp = norm_back(mm_nt(gu1, wu1), h1, g_cmlp)
    dh1 = dh2 + dx
    go1 = dh1.astype(BF)
    gv = lax.optimization_barrier(mm_nt(go1, wvo).astype(BF))
    delta = jnp.sum(px * gv.astype(F32), axis=1, keepdims=True)
    gv_all = lax.all_gather(gv, "ctx", axis=0, tiled=True)
    stat = lax.all_gather(jnp.concatenate([lse, delta], axis=1), "ctx", axis=0, tiled=True)
    p = jnp.where(mask, jnp.exp(s - stat[:, :1]), 0.0)
    ds = (p * (mm_nt(gv_all, xn) - stat[:, 1:]) * CROSS_SCALE).astype(BF)
    dxn = mm_tn(ds, qk_all) + mm_tn(p.astype(BF), gv_all)
    dpix, gg_in = norm_back(dxn, xin, g_in)
    dqk = lax.psum_scatter(mm(ds, xn), "ctx", scatter_dimension=0, tiled=True).astype(BF)
    dx, gg_lat = norm_back(mm_nt(dqk, wqk), lat, g_lat)
    dlat = dh1 + dx

    e_sum = lax.psum_scatter(mm_tn(ln, dqk), "fsdp", scatter_dimension=0, tiled=True)
    e_sum, f_sum = lax.psum((e_sum, lax.psum(mm_tn(px_low, go1), "fsdp")), "ctx")
    e_sum, f_sum = e_sum.astype(BF), f_sum.astype(BF)
    d_wq_c = mm(e_sum, wk_all)
    d_wk_c = lax.psum_scatter(mm_tn(e_sum, wq_c), "fsdp", scatter_dimension=1, tiled=True)
    d_wv_c = mm_nt(f_sum, wo_c)
    d_wo_c = mm_tn(wv_c, f_sum)
    pairs = ((n1, gu1), (z1, gy1), (n2, dqs), (n2, dks), (n2, dvs), (sa, go3), (n3, gu3), (z3, gy3))
    d_big = [
        lax.psum(lax.psum_scatter(mm_tn(a, b), "fsdp", scatter_dimension=0, tiled=True), "ctx")
        for a, b in pairs
    ]
    gains = lax.psum(jnp.concatenate([gg_in[0], gg_lat[0], gg_cmlp[0], gg_self[0], gg_smlp[0]]), ("ctx", "fsdp"))
    return (
        layer_out[None], dpix[None], dlat[None], d_wq_c, d_wk_c, d_wv_c, d_wo_c, *d_big,
        gains[:c], gains[c : c + D], gains[c + D : c + 2 * D],
        gains[c + 2 * D : c + 3 * D], gains[c + 3 * D :],
    )


CP = 384
CR = 288
CX = 272
PARITY_ROWS = 4 * 128


def fused(
    pix, lat, cot, lengths, offsets, deal, g_in, g_lat, g_cmlp, g_self, g_smlp,
    wq_c, wk_c, wv_c, wo_c, wu_1, wd_1, wq_s, wk_s, wv_s, wo_s, wu_3, wd_3,
    layer_out, d_pix, d_lat, d_big, d_wk, d_wv, d_gain,
    *scratch,
):
    s = types.SimpleNamespace(**dict(zip(SCRATCH, scratch)))
    c, z = lax.axis_index("ctx"), lax.axis_index("fsdp")
    k, p = lax.rem(c, 2), lax.div(c, 2)
    k2 = 1 - k

    def flip(v, d):
        low, high = lax.rem(v, 2), lax.div(v, 2)
        return (1 - low if d & 1 else low) + 2 * (1 - high if d & 2 else high)

    chip = {d: flip(p, d) for d in (1, 2, 3)}
    plane = {d: flip(z, d) for d in (1, 2, 3)}
    sib = {"ctx": 2 * p + k2}

    def peer(d):
        return {"ctx": 2 * chip[d] + k}

    def across(d):
        return {"ctx": 2 * chip[d] + k2}

    def level(d):
        return {"fsdp": plane[d]}

    used = [0, 0]
    sends = []

    def make(src, dst, target, slot=None):
        if slot is None:
            slot = used[0]
            used[0] += 1
        send = used[1]
        used[1] += 1
        return pltpu.make_async_remote_copy(
            src_ref=src, dst_ref=dst, send_sem=s.ssem.at[send], recv_sem=s.rsem.at[slot],
            device_id=target, device_id_type=pl.DeviceIdType.MESH,
        )

    def put(src, dst, target):
        copy = make(src, dst, target)
        copy.start()
        sends.append((None, copy))
        return copy

    def sent(copies):
        for copy in copies.values() if isinstance(copies, dict) else copies:
            copy.wait_send()
            sends[:] = [pair for pair in sends if pair[1] is not copy]

    def to_peers(src_of, dst_of, order=(3, 1, 2)):
        return {d: put(src_of(d), dst_of(d), peer(d)) for d in order}

    def to_planes(src_of, dst_of):
        return {d: put(src_of(d), dst_of(d), level(d)) for d in (1, 2, 3)}

    def arrived(copies):
        for copy in copies.values() if isinstance(copies, dict) else copies:
            copy.wait_recv()

    locals_ = [0]

    def fetch(src, dst):
        copy = pltpu.make_async_copy(src, dst, s.lsem.at[locals_[0]])
        locals_[0] += 1
        copy.start()
        return copy

    def spread(part_of):
        mine = [part_of(p, h) for h in range(2)]
        copies = {(d, h): put(mine[h], mine[h], peer(d)) for d, h in ((1, 0), (2, 1), (1, 1), (2, 0))}
        return part_of, copies, []

    def relay(state):
        part_of, copies, on = state
        for d, h in ((1, 0), (2, 1)):
            copies[d, h].wait_recv()
            part = part_of(chip[d], h)
            on.append(put(part, part, peer(3 - d)))

    def near(state, d):
        state[1][d, 2 - d].wait_recv()

    def far(state):
        arrived(state[2])

    def all_of(state):
        near(state, 1)
        near(state, 2)
        far(state)

    def fold(part_of, into):
        first = [put(part_of(3, h), into(0, h), peer(1 + h)) for h in range(2)]
        near_ = [put(part_of(1 + h, h), into(1, h), peer(1 + h)) for h in range(2)]
        return part_of, into, first, near_

    def fold_on(state):
        part_of, into, first, near_ = state
        for h in range(2):
            first[h].wait_recv()
            part = part_of(2 - h, h)
            part[...] = (part[...].astype(F32) + into(0, h)[...].astype(F32)).astype(BF)
            near_.append(put(part, into(2, h), peer(2 - h)))

    def gather(slot_of, half_of=None):
        own = put(slot_of(c), slot_of(c), sib)
        if half_of is None:
            return slot_of, to_peers(lambda d: slot_of(c), lambda d: slot_of(c)), [own]
        return slot_of, spread(lambda q, h: half_of(2 * q + k, h)), [own]

    def pass_on(state):
        slot_of, copies, to_sib = state
        if not isinstance(copies, dict):
            all_of(copies)
        for d in (1, 2, 3):
            if isinstance(copies, dict):
                copies[d].wait_recv()
            there = slot_of(2 * chip[d] + k)
            to_sib.append(put(there, there, sib))
        return to_sib

    def to_plane(part):
        return [put(part, part, to) for to in (*(peer(d) for d in (1, 2, 3)), *(across(d) for d in (1, 2, 3)), sib)]

    for j in range(4):
        s.wk[j, 256:CP, :] = jnp.zeros((CP - 256, 256), BF)
    s.wv_z[256:CP, :] = jnp.zeros((CP - 256, 256), BF)
    for j in range(2):
        s.xt[j, 256:CP, :] = jnp.zeros((CP - 256, 1024), BF)
    for j in range(8):
        s.wvo[j, CR:CP, :] = jnp.zeros((CP - CR, 128), BF)
    barrier = pltpu.get_barrier_semaphore()
    near_by = (sib, *(across(d) for d in (1, 2, 3)), *(peer(d) for d in (1, 2, 3)))
    for target in (*near_by, *(level(d) for d in (1, 2, 3))):
        pl.semaphore_signal(barrier, inc=1, device_id=target, device_id_type=pl.DeviceIdType.MESH)
    lanes = pl.ds(pl.multiple_of(c * 128, 128), 128)
    quarter = pl.ds(pl.multiple_of(k * 128 + p * 32, 32), 32)
    f_wk = [fetch(wk_c.at[0:256], s.u1.at[0]), fetch(wk_c.at[256:261], s.u1.at[1, 0:5])]
    f_wq = [fetch(wq_c.at[128 * i : 128 * (i + 1)], s.hpa.at[i]) for i in range(2)]
    f_wv = [fetch(wv_c.at[0:256], s.u3.at[0]), fetch(wv_c.at[256:261], s.u3.at[1, 0:5])]
    f_wo = [fetch(wo_c.at[128 * i : 128 * (i + 1)], s.hpb.at[i]) for i in range(2)]

    def early(i):
        return (s.dh if i < 8 else s.hxb).at[:, 128 * (i % 8) : 128 * (i % 8) + 128]

    f_u = [
        fetch(w.at[128 * j : 128 * (j + 1), lanes], early(2 * i + j))
        for i, w in enumerate((wu_1, wu_3, wq_s, wk_s, wv_s))
        for j in range(2)
    ]
    f_d = [fetch(w.at[quarter, :], s.h3.at[32 * i : 32 * (i + 1)]) for i, w in enumerate((wd_1, wo_s))]
    f_d3 = fetch(wd_3.at[pl.ds(pl.multiple_of(k * 128, 128), 128), :], s.hxa)
    pl.semaphore_wait(barrier, 10)

    for copy in f_wk:
        copy.wait()
    s.wk[z, 0:256, :] = s.u1[0].astype(BF)
    s.wk[z, 256:261, :] = s.u1[1, 0:5, :].astype(BF)
    half = pl.ds(pl.multiple_of(k * 144, 16), 144)
    wk_z = to_planes(lambda d: s.wk.at[z, half], lambda d: s.wk.at[z, half])
    for copy in f_u:
        copy.wait()
    own_z = pl.ds(pl.multiple_of(z * 256, 256), 256)
    for j in range(2):
        half_z = pl.ds(pl.multiple_of(z * 256 + 128 * j, 128), 128)
        s.wu1[p, half_z, :] = early(j)[...].astype(BF)
    wu1_z = to_planes(lambda d: s.wu1.at[p, own_z], lambda d: s.wu1.at[p, own_z])
    s.cpair[k] = cot[...]
    x_cot = put(s.cpair.at[k], s.cpair.at[k], sib)

    order = lax.broadcasted_iota(jnp.int32, (8, D), 1)
    block = lax.div(order, LBLK)
    base = jnp.zeros((8, D), jnp.int32)
    for i in range(D // LBLK):
        base = jnp.where(block == i, deal[i], base)
    pos_r = (base * LBLK + lax.rem(order, LBLK)) * STRIDE + offsets[...]
    lo_r = jnp.zeros((8, D), jnp.int32)
    start = lengths[0, 0]
    for i in range(1, lengths.shape[1]):
        lo_r = jnp.where(start <= pos_r, start, lo_r)
        start = start + lengths[0, i]
    s.pos[...] = pos_r
    top_row = lax.broadcasted_iota(jnp.int32, (128, 128), 0) == 0
    for b in range(8):
        cols = slice(128 * b, 128 * (b + 1))
        both_rows = jnp.where(top_row, lo_r[0:1, cols], pos_r[0:1, cols]).astype(F32)
        s.span[cols, :] = both_rows.T.astype(jnp.int32)
    s.row[0:1, 0:256] = g_in[0:256].reshape(1, 256)
    s.row[0:1, 256:261] = g_in[256:261].reshape(1, 5)
    s.gcol[...] = jnp.broadcast_to(s.row[0:1, :], (128, CP)).T

    def norm_pixels(t):
        cols = slice(256 * t, 256 * (t + 1))
        normed = (norm_cols(pix[:, cols].astype(F32))[0] * s.gcol[0:261, 0:1]).astype(BF)
        s.xt[k, 0:256, cols] = normed[0:256]
        s.xt[k, 256:261, cols] = normed[256:261]

    for t in range(4):
        norm_pixels(t)
    ln = (norm_parts(lat[...].astype(F32))[0] * g_lat[...]).astype(BF)
    s.ln[...] = ln
    for i in range(2):
        f_wq[i].wait()
        s.wq_z[128 * i : 128 * (i + 1), :] = s.hpa[i].astype(BF)
    wk_s_in = []
    for d in (1, 2, 3):
        wk_z[d].wait_recv()
        there = s.wk.at[plane[d], half]
        wk_s_in.append(put(there, there, sib))
    for copy in f_wv:
        copy.wait()
    s.wv_z[0:256, :] = s.u3[0].astype(BF)
    s.wv_z[256:261, :] = s.u3[1, 0:5, :].astype(BF)
    for i in range(2):
        f_wo[i].wait()
        s.wo_z[128 * i : 128 * (i + 1), :] = s.hpb[i].astype(BF)
    wvo_part = mm(s.wv_z[...], s.wo_z[:, lanes])
    s.wvz[0] = wvo_part[:CR].astype(BF)
    arrived(wk_s_in)
    own_rows = pl.ds(pl.multiple_of(k * 128, 128), 128)
    part = jnp.zeros((128, CP), F32)
    for j in range(4):
        part += mm_nt(s.wq_z[own_rows, 256 * j : 256 * (j + 1)], s.wk[j])
    s.wqk[z, k] = part.astype(BF)
    wqk_z = to_planes(lambda d: s.wqk.at[z, k], lambda d: s.wqk.at[z, k])
    wqk_s = [put(s.wqk.at[z, k], s.wqk.at[z, k], sib)]
    wvo_z = to_planes(lambda d: s.wvz.at[0], lambda d: s.wvz.at[d])
    x_xn = put(s.xt.at[k, 0:CX], s.xt.at[k, 0:CX], sib)
    for copy in f_d:
        copy.wait()
    s.wd1[z, p] = s.h3[0:32, :].astype(BF)
    wd1_z = to_planes(lambda d: s.wd1.at[z, p], lambda d: s.wd1.at[z, p])

    for j in range(2):
        half_z = pl.ds(pl.multiple_of(z * 256 + 128 * j, 128), 128)
        s.wu3[p, half_z, :] = early(2 + j)[...].astype(BF)
        for i in range(3):
            s.wqkv[i, k, half_z, :] = early(4 + 2 * i + j)[...].astype(BF)
    s.woz[z] = s.h3[32:64, :].astype(BF)
    f_d3.wait()
    s.wd3[z] = s.hxa[...].astype(BF).reshape(4, 32, D)
    arrived(wu1_z)
    wu1_in = spread(lambda q, h: s.wu1.at[q, 512 * h : 512 * h + 512])
    for d in (1, 2, 3):
        wqk_z[d].wait_recv()
        there = s.wqk.at[plane[d], k]
        wqk_s.append(put(there, there, sib))
    relay(wu1_in)
    arrived(wqk_s)
    wqk = s.wqk[...].reshape(D, CP)
    s.qk[p] = mm(ln, wqk).astype(BF)
    qk_in = to_peers(lambda d: s.qk.at[p], lambda d: s.qk.at[p])
    arrived(wvo_z)
    s.wvo[c, 0:CR, :] = sum(s.wvz[d].astype(F32) for d in range(4)).astype(BF)

    def wvo_slot(i):
        return s.wvo.at[i, 0:CR]

    wvo_in = gather(wvo_slot)
    wu3_z = to_planes(lambda d: s.wu3.at[p, own_z], lambda d: s.wu3.at[p, own_z])
    qkv_z = to_planes(lambda d: s.wqkv.at[:, k, own_z], lambda d: s.wqkv.at[:, k, own_z])
    wo_z = to_planes(lambda d: s.woz.at[z], lambda d: s.woz.at[z])
    wd3_z = to_planes(lambda d: s.wd3.at[z], lambda d: s.wd3.at[z])
    x_xn.wait_recv()

    wide = lax.broadcasted_iota(jnp.int32, (128, 1024), 1)
    lane = lax.broadcasted_iota(jnp.int32, (128, CP), 1)

    def cross_block(q):
        rows = pl.ds(pl.multiple_of((2 * q + k) * 128, 128), 128)
        low, high = s.span[rows, 0:1], s.span[rows, 1:2]
        scores = []
        for h in range(2):
            at = wide + (2 * p + h) * 1024
            sc = mm(s.qk[q], s.xt[h]) * CROSS_SCALE
            scores.append(jnp.where((at >= low) & (at <= high), sc, MASKED))
        top = jnp.maximum(*(jnp.max(sc, axis=1, keepdims=True) for sc in scores))
        total = jnp.zeros((128, 1), F32)
        acc = jnp.zeros((128, CP), F32)
        for h in range(2):
            e = jnp.where(scores[h] > 0.5 * MASKED, jnp.exp(scores[h] - top), 0.0).astype(BF)
            s.ee[2 * q + h] = e
            total += jnp.sum(e.astype(F32), axis=1, keepdims=True)
            acc += mm_nt(e, s.xt[h])
        s.tops[q] = jnp.broadcast_to(top, (128, 128))
        s.pxs[q] = tag(acc, lane, top, total)

    cross_block(p)
    px_in = {}
    for d in (1, 2, 3):
        qk_in[d].wait_recv()
        cross_block(chip[d])
        px_in[d] = put(s.pxs.at[chip[d]], s.pxr.at[d - 1], peer(d))
    wvo_s = pass_on(wvo_in)
    arrived(wd1_z)
    wd1_in = spread(lambda q, h: s.wd1.at[2 * h : 2 * h + 2, q])
    arrived(px_in)
    found = [untag(s.pxs[p], lane)] + [untag(s.pxr[i], lane) for i in range(3)]
    high = found[0][1]
    for f in found[1:]:
        high = jnp.maximum(high, f[1])
    px, total = jnp.zeros((128, CP), F32), jnp.zeros((128, 1), F32)
    for val, top, tot in found:
        share = jnp.exp(top - high)
        px += share * val
        total += share * tot
    px = px / total
    s.px[...] = px
    lse = high + jnp.log(total)
    s.pxl[...] = px.astype(BF)
    relay(wd1_in)
    arrived(wvo_s)
    lat_f = lat[...].astype(F32)
    pxl = s.pxl[...]
    for j in range(4):
        cols = slice(256 * j, 256 * (j + 1))
        w = jnp.concatenate([s.wvo[2 * j], s.wvo[2 * j + 1]], axis=1)
        s.h1[:, cols] = lat[:, cols].astype(F32) + mm(pxl, w)

    def mlp_start(h_ref, gain, npair):
        npair[k] = (norm_parts(h_ref[...])[0] * gain[...]).astype(BF)
        return put(npair.at[k], npair.at[k], sib)

    def mlp_up(npair, wu, u, zb):
        rows = npair[...].reshape(256, D)
        for j in range(2):
            w = jnp.concatenate([wu[2 * j], wu[2 * j + 1]], axis=1)
            hidden = mm(rows, w)
            u[j] = hidden
            zb[j] = gelu(hidden).astype(BF)

    def mlp_down(zb, wd, hp, hx):
        for t in range(4):
            cols = slice(256 * t, 256 * (t + 1))
            acc = mm(zb[0], wd[0:2, :, :, cols].reshape(256, 256))
            acc += mm(zb[1], wd[2:4, :, :, cols].reshape(256, 256))
            hp[:, :, cols] = acc.reshape(2, 128, 256)
        return put(hp.at[k2], hx, sib)

    def mlp_back(gpair, wu, wd, u, gub, hp, hx):
        rows = gpair[...].reshape(256, D)
        for j in range(2):
            gz = mm_nt(rows, wd[2 * j : 2 * j + 2].reshape(256, D))
            gub[j] = (gz * gelu_slope(u[j])).astype(BF)
        for t in range(4):
            cols = slice(256 * t, 256 * (t + 1))
            acc = jnp.zeros((256, 256), F32)
            for j in range(2):
                w = jnp.concatenate([wu[2 * j, cols, :], wu[2 * j + 1, cols, :]], axis=1)
                acc += mm_nt(gub[j], w)
            hp[:, :, cols] = acc.reshape(2, 128, 256)
        return put(hp.at[k2], hx, sib)

    def up_partial(npair, gub):
        for j in range(2):
            for t in range(4):
                cols = slice(256 * t, 256 * (t + 1))
                g = mm_tn(npair[:, :, cols].reshape(256, 256), gub[j]).astype(BF)
                s.gsu[2 * j, cols, :] = g[:, :128]
                s.gsu[2 * j + 1, cols, :] = g[:, 128:]

    def up_fold():
        return fold(
            lambda d, h: s.gsu.at[chip[d], 512 * h : 512 * h + 512],
            lambda i, h: s.gru.at[i, 512 * h : 512 * h + 512],
        )

    def down_partial(zb, gpair):
        for j in range(2):
            for t in range(4):
                cols = slice(256 * t, 256 * (t + 1))
                g = mm_tn(zb[j], gpair[:, :, cols].reshape(256, 256)).astype(BF)
                s.gsd[2 * j : 2 * j + 2, :, :, cols] = g.reshape(2, 4, 32, 256)

    def down_fold():
        return fold(
            lambda d, h: s.gsd.at[2 * h : 2 * h + 2, chip[d]],
            lambda i, h: s.grd.at[i, 2 * h : 2 * h + 2],
        )

    def up_to_planes(up, zs, zr):
        arrived(up[3])
        total = s.gsu[p].astype(F32)
        for i in (1, 2):
            total += s.gru[i].astype(F32)
        zs[...] = total.astype(BF)
        return to_planes(
            lambda d: zs.at[pl.ds(pl.multiple_of(plane[d] * 256, 256), 256)], lambda d: zr.at[d - 1]
        )

    def down_to_planes(down, zs, zr):
        arrived(down[3])
        total = s.gsd[:, p].astype(F32)
        for i in (1, 2):
            total += s.grd[i].astype(F32)
        zs[...] = total.astype(BF)
        return to_planes(lambda d: zs.at[plane[d]], lambda d: zr.at[d - 1])

    def up_total(copies, zs, zr, ag):
        arrived(copies)
        total = zs[own_z, :].astype(F32)
        for i in range(3):
            total += zr[i].astype(F32)
        ag[c] = total.astype(BF)
        return gather(lambda i: ag.at[i], lambda i, h: ag.at[i, 128 * h : 128 * h + 128])

    def row_slot(ag):
        return lambda i: ag.at[lax.rem(i, 2), lax.div(i, 2)]

    def row_half(ag):
        return lambda i, h: ag.at[lax.rem(i, 2), lax.div(i, 2), 16 * h : 16 * h + 16]

    def down_total(copies, zs, zr, ag):
        arrived(copies)
        total = zs[z].astype(F32)
        for i in range(3):
            total += zr[i].astype(F32)
        ag[k, p] = total.astype(BF)
        return gather(row_slot(ag), row_half(ag))

    outs = []

    def out_cols(ag, w):
        for j in range(8):
            outs.append(fetch(ag.at[j], d_big.at[w, :, 128 * j : 128 * (j + 1)]))

    def out_rows(ag, w):
        for kk in range(2):
            for q in range(4):
                at = 128 * kk + 32 * q
                outs.append(fetch(ag.at[kk, q], d_big.at[w, at : at + 32, :]))

    x_n1 = mlp_start(s.h1, g_cmlp, s.n1)
    arrived(wu3_z)
    wu3_in = spread(lambda q, h: s.wu3.at[q, 512 * h : 512 * h + 512])
    all_of(wu1_in)
    x_n1.wait_recv()
    mlp_up(s.n1, s.wu1, s.u1, s.z1)
    all_of(wd1_in)
    x_h1 = mlp_down(s.z1, s.wd1, s.hpa, s.hxa)
    relay(wu3_in)
    arrived(qkv_z)
    x_qkv = put(s.wqkv.at[:, k], s.wqkv.at[:, k], sib)
    x_h1.wait_recv()
    s.h2[...] = s.h1[...] + s.hpa[k] + s.hxa[...]

    s.n2[p] = (norm_parts(s.h2[...])[0] * g_self[...]).astype(BF)
    n2_in = spread(lambda q, h: s.n2.at[q, 64 * h : 64 * h + 64])
    x_qkv.wait_recv()

    def project(q):
        rows = s.n2[q]
        for i in range(3):
            w = jnp.concatenate([s.wqkv[i, 0], s.wqkv[i, 1]], axis=1)
            s.pair[...] = mm(rows, w).astype(BF).reshape(128, 256)
            for h in range(2):
                s.heads[h, q, i] = s.pair[:, 128 * h : 128 * (h + 1)]
        s.mine[2 * q + k] = s.heads[k, q]
        return put(s.heads.at[k2, q], s.mine.at[2 * q + k], sib)

    qkv_in = [project(p)]
    relay(n2_in)
    for d in (1, 2):
        near(n2_in, d)
        qkv_in.append(project(chip[d]))
    far(n2_in)
    qkv_in.append(project(chip[3]))
    arrived(wo_z)
    piece = pl.ds(pl.multiple_of(32 * p, 32), 32)
    s.wo[k, piece, :] = s.woz[p]
    wo_in = to_peers(lambda d: s.woz.at[chip[d]], lambda d: s.wo.at[k, piece])
    arrived(qkv_in)

    def attend(b):
        rows = pl.ds(pl.multiple_of(b * 128, 128), 128)
        keys = s.mine[:, 1].reshape(D, 128)
        sc = mm_nt(s.mine[b, 0], keys) * SELF_SCALE
        at = s.pos[0:1, :]
        sc = jnp.where((at >= s.span[rows, 0:1]) & (at <= s.span[rows, 1:2]), sc, MASKED)
        e = jnp.exp(sc - jnp.max(sc, axis=1, keepdims=True))
        low = (e / jnp.sum(e, axis=1, keepdims=True)).astype(BF)
        s.a1[b] = low
        return mm(low, s.mine[:, 2].reshape(D, 128)).astype(BF)

    def other_rows(q, carry):
        s.send[q] = attend(2 * q + k2)
        return carry

    def own_parity(q, carry):
        s.aspar[q, k] = attend(2 * q + k)
        return carry

    lax.fori_loop(0, 4, other_rows, 0)
    x_as = put(s.send, s.aspar.at[:, k], sib)
    arrived(wo_in)
    x_wo = put(s.wo.at[k], s.wo.at[k], sib)
    lax.fori_loop(0, 4, own_parity, 0)
    x_wo.wait_recv()
    x_as.wait_recv()

    def both(ref, q):
        return jnp.concatenate([ref[q, 0], ref[q, 1]], axis=1)

    for d in (3, 1, 2):
        s.outp[d - 1] = mm(both(s.aspar, chip[d]), s.wo[...].reshape(256, D)).astype(BF)

    def rows_out(d, h):
        return s.outp.at[d - 1, 64 * h : 64 * h + 64]

    def rows_in(i, h):
        return s.outr.at[i, 64 * h : 64 * h + 64]

    out_in = fold(rows_out, rows_in)
    s.h3[...] = s.h2[...] + mm(both(s.aspar, p), s.wo[...].reshape(256, D))
    fold_on(out_in)
    arrived(out_in[3])
    s.h3[...] += s.outr[1].astype(F32) + s.outr[2].astype(F32)

    x_n3 = mlp_start(s.h3, g_smlp, s.n3)
    all_of(wu3_in)
    x_n3.wait_recv()
    mlp_up(s.n3, s.wu3, s.u3, s.z3)
    arrived(wd3_z)
    x_cot.wait_recv()
    sent([x_h1])
    x_d3 = mlp_back(s.cpair, s.wu3, s.wd3, s.u3, s.gu3, s.hpa, s.hxa)
    x_h3 = mlp_down(s.z3, s.wd3, s.hpb, s.hxb)
    x_d3.wait_recv()
    dx, gg_smlp = norm_back(s.hpa[k] + s.hxa[...], s.h3[...], g_smlp[...])
    dh3 = cot[...].astype(F32) + dx
    s.dh[...] = dh3
    s.go[p] = dh3.astype(BF)
    go_in = spread(lambda q, h: s.go.at[q, 64 * h : 64 * h + 64])
    x_h3.wait_recv()
    layer_out[...] = (s.h3[...] + s.hpb[k] + s.hxb[...]).astype(BF)

    def pull_out(q):
        g = mm_nt(s.go[q], s.wo[...].reshape(256, D)).astype(BF)
        s.pair[...] = g
        for h in range(2):
            s.gheads[h, q] = s.pair[:, 128 * h : 128 * (h + 1)]
        s.gmine[2 * q + k] = s.gheads[k, q]
        return put(s.gheads.at[k2, q], s.gmine.at[2 * q + k], sib)

    gas_in = [pull_out(p)]
    relay(go_in)
    up_partial(s.n3, s.gu3)
    g3u_z = to_planes(
        lambda d: s.gsu.at[:, pl.ds(pl.multiple_of(plane[d] * 256, 256), 256)], lambda d: s.zg.at[d - 1]
    )
    for d in (1, 2):
        near(go_in, d)
        gas_in.append(pull_out(chip[d]))
    far(go_in)
    gas_in.append(pull_out(chip[3]))
    down_partial(s.z3, s.cpair)
    g3d = down_fold()
    arrived(gas_in)

    def attend_back(b, carry):
        dps = mm_nt(s.gmine[b], s.mine[:, 2].reshape(D, 128))
        probs = s.a1[b].astype(F32)
        delta = jnp.sum(probs * dps, axis=1, keepdims=True) / jnp.sum(probs, axis=1, keepdims=True)
        dss = (probs * (dps - delta) * SELF_SCALE).astype(BF)
        s.a2[b] = dss
        s.heads[lax.div(b, 4), lax.rem(b, 4), 0] = mm(dss, s.mine[:, 1].reshape(D, 128)).astype(BF)
        return carry

    sent(qkv_in)
    lax.fori_loop(0, 8, attend_back, 0)
    fold_on(g3d)
    for t in range(4):
        cols = slice(256 * t, 256 * (t + 1))
        dk = mm_tn(s.a2[:, :, cols].reshape(D, 256), s.mine[:, 0].reshape(D, 128))
        dv = mm_tn(s.a1[:, :, cols].reshape(D, 256), s.gmine[...].reshape(D, 128))
        two = slice(2 * (t % 2), 2 * (t % 2) + 2)
        s.heads[t // 2, two, 1] = dk.astype(BF).reshape(2, 128, 128)
        s.heads[t // 2, two, 2] = dv.astype(BF).reshape(2, 128, 128)

    def sort(q, carry):
        high, low = lax.div(q, 2), 2 * lax.rem(q, 2)
        s.dsend[q] = s.heads[high, low + k2]
        for i in range(3):
            s.dpar[q, i, k] = s.heads[high, low + k, i]
        return carry

    lax.fori_loop(0, 4, sort, 0)
    x_dp = put(s.dsend, s.dpar.at[:, :, k], sib)
    g3d_z = down_to_planes(g3d, s.sd3, s.zd3)
    x_dp.wait_recv()

    def pull_in(q, write):
        for t in range(4):
            cols = slice(256 * t, 256 * (t + 1))
            acc = jnp.zeros((128, 256), F32)
            for i in range(3):
                w = jnp.concatenate([s.wqkv[i, 0, cols, :], s.wqkv[i, 1, cols, :]], axis=1)
                acc += mm_nt(jnp.concatenate([s.dpar[q, i, 0], s.dpar[q, i, 1]], axis=1), w)
            write(cols, acc)

    sent(out_in[2])
    sent(out_in[3])
    for d in (3, 1, 2):

        def write(cols, acc):
            s.outp[d - 1, :, cols] = acc.astype(BF)

        pull_in(chip[d], write)
    dn_in = fold(rows_out, rows_in)

    def write(cols, acc):
        s.hxb[:, cols] = acc

    pull_in(p, write)
    fold_on(dn_in)
    for i in range(3):
        g = jnp.concatenate([s.dpar[:, i, 0].reshape(PARITY_ROWS, 128), s.dpar[:, i, 1].reshape(PARITY_ROWS, 128)], axis=1)
        for t in range(4):
            cols = slice(256 * t, 256 * (t + 1))
            w = mm_tn(s.n2[:, :, cols].reshape(PARITY_ROWS, 256), g).astype(BF)
            for h in range(2):
                s.pg[i, h, cols, :] = w[:, 128 * h : 128 * (h + 1)]
    x_pg = put(s.pg.at[:, k2], s.pgr, sib)
    g = jnp.concatenate([s.aspar[:, 0].reshape(PARITY_ROWS, 128), s.aspar[:, 1].reshape(PARITY_ROWS, 128)], axis=1)
    for t in range(4):
        cols = slice(256 * t, 256 * (t + 1))
        w = mm_tn(g, s.go[:, :, cols].reshape(PARITY_ROWS, 256)).astype(BF)
        s.pgo[:, :, cols] = w.reshape(2, 128, 256)
    x_pgo = put(s.pgo.at[k2], s.pgor, sib)
    arrived(dn_in[3])
    dn2 = s.hxb[...] + s.outr[1].astype(F32) + s.outr[2].astype(F32)
    dx, gg_self = norm_back(dn2, s.h2[...], g_self[...])
    s.dh[...] += dx

    s.gpair[k] = s.dh[...].astype(BF)
    x_g = put(s.gpair.at[k], s.gpair.at[k], sib)
    x_pg.wait_recv()
    for i in range(3):
        s.pg[i, k] = (s.pg[i, k].astype(F32) + s.pgr[i].astype(F32)).astype(BF)
    pg_z = to_planes(
        lambda d: s.pg.at[:, k, pl.ds(pl.multiple_of(plane[d] * 256, 256), 256)],
        lambda d: s.zq.at[d - 1],
    )
    arrived(g3u_z)
    s.zs[...] = (s.gsu[:, own_z, :].astype(F32) + sum(s.zg[i].astype(F32) for i in range(3))).astype(BF)
    g3u_in = to_peers(lambda d: s.zs.at[chip[d]], lambda d: s.zu3.at[d - 1])
    g3d_ag = down_total(g3d_z, s.sd3, s.zd3, s.agd3)
    x_g.wait_recv()
    sent([x_d3])
    x_d1 = mlp_back(s.gpair, s.wu1, s.wd1, s.u1, s.gu1, s.hpa, s.hxa)
    sent(g3d[2])
    sent(g3d[3])
    down_partial(s.z1, s.gpair)
    g1d = down_fold()
    x_pgo.wait_recv()
    s.pgo[k] = (s.pgo[k].astype(F32) + s.pgor[...].astype(F32)).astype(BF)
    s.wz[p] = s.pgo[k, piece, :]
    pgo_in = to_peers(
        lambda d: s.pgo.at[k, pl.ds(pl.multiple_of(32 * chip[d], 32), 32)], lambda d: s.wz.at[p]
    )
    x_d1.wait_recv()
    dx, gg_cmlp = norm_back(s.hpa[k] + s.hxa[...], s.h1[...], g_cmlp[...])
    dh1 = s.dh[...] + dx
    s.dh[...] = dh1

    go1 = dh1.astype(BF)
    gv = jnp.zeros((128, CP), F32)
    for j in range(4):
        w = jnp.concatenate([s.wvo[2 * j], s.wvo[2 * j + 1]], axis=1)
        gv += mm_nt(go1[:, 256 * j : 256 * (j + 1)], w)
    gv = gv.astype(BF).astype(F32)
    delta = jnp.sum(jnp.where(lane < 261, s.px[...] * gv, 0.0), axis=1, keepdims=True)
    s.gv[p] = tag(gv, lane, lse, delta)
    gv_in = to_peers(lambda d: s.gv.at[p], lambda d: s.gv.at[p])
    relay(g3d_ag[1])
    fold_on(g1d)
    sent(g3u_z)
    up_partial(s.n1, s.gu1)
    g1u = up_fold()
    for j in range(4):
        f_part = mm_tn(s.pxl[...], go1[:, 256 * j : 256 * (j + 1)])[:CR].astype(BF)
        s.fst[j, 0] = f_part[:, :128]
        s.fst[j, 1] = f_part[:, 128:]
    sent(wvo_in[1])
    sent(wvo_s)
    x_f = put(s.fst.at[:, k2], s.fsr, sib)

    arrived(g3u_in)
    s.agu3[c] = (s.zs[p].astype(F32) + sum(s.zu3[i].astype(F32) for i in range(3))).astype(BF)
    g3u_ag = gather(lambda i: s.agu3.at[i], lambda i, h: s.agu3.at[i, 128 * h : 128 * h + 128])
    arrived(pgo_in)
    pgo_z = to_planes(lambda d: s.wz.at[plane[d]], lambda d: s.zo.at[d - 1])
    def cross_back(q):
        val, last, delta = untag(s.gv[q], lane)
        ratio = jnp.exp(s.tops[q][:, 0:1] - last)
        s.gvr[q] = (val * ratio).astype(BF)
        acc = jnp.zeros((128, CP), F32)
        for h in range(2):
            dp = mm(s.gv[q], s.xt[h])
            ds = (s.ee[2 * q + h].astype(F32) * ((dp - delta) * (ratio * CROSS_SCALE))).astype(BF)
            s.a2[2 * q + h] = ds
            acc += mm_nt(ds, s.xt[h])
        s.pxs[q] = acc.astype(BF)
        return acc

    sent(px_in)
    s.dqk[...] = cross_back(p)
    dq_in = {}
    for d in (1, 2, 3):
        gv_in[d].wait_recv()
        cross_back(chip[d])
        dq_in[d] = put(s.pxs.at[chip[d]], s.pxr.at[d - 1], peer(d))

    fold_on(g1u)
    relay(g3u_ag[1])
    for q in range(4):
        for j in range(3):
            cols = slice(128 * j, 128 * (j + 1))
            s.a1[j, :, 128 * q : 128 * (q + 1)] = s.qk[q, :, cols].T
            s.a1[j, :, 512 + 128 * q : 512 + 128 * (q + 1)] = s.gvr[q, :, cols].T

    def pixel_cols(h, t):
        cols = slice(256 * t, 256 * (t + 1))
        parts = [s.a2[2 * q + h, :, cols] for q in range(4)] + [s.ee[2 * q + h, :, cols] for q in range(4)]
        return mm(s.a1[0:3].reshape(CP, 1024), jnp.concatenate(parts, axis=0))

    for t in range(4):
        s.dxs[:, 256 * t : 256 * (t + 1)] = pixel_cols(k2, t)[:CX].astype(BF)
    x_dx = put(s.dxs, s.dxr, sib)
    arrived(dq_in)
    dqk = (s.dqk[...] + sum(s.pxr[i].astype(F32) for i in range(3))).astype(BF)
    for j in range(8):
        e = mm_tn(s.ln[:, 128 * j : 128 * (j + 1)], dqk).astype(BF)
        s.est[j // 2, 2 * (j % 2) : 2 * (j % 2) + 2] = e.reshape(2, 2, 32, CP)
    x_e = put(s.est.at[:, :, k2], s.esr, sib)
    dx, gg_lat = norm_back(mm_nt(dqk, s.wqk[...].reshape(D, CP)), lat[...].astype(F32), g_lat[...])
    s.dh[...] += dx
    outs.append(fetch(s.dh, d_lat))
    x_e.wait_recv()
    s.est[:, :, k] = (s.est[:, :, k].astype(F32) + s.esr[...].astype(F32)).astype(BF)
    e_in = to_peers(lambda d: s.est.at[:, chip[d], k], lambda d: s.epr.at[d - 1])
    x_f.wait_recv()
    s.fst[:, k] = (s.fst[:, k].astype(F32) + s.fsr[...].astype(F32)).astype(BF)
    f_in = to_peers(lambda d: s.fst.at[chip[d], k], lambda d: s.fpr.at[d - 1])

    x_dx.wait_recv()
    gg_in = jnp.zeros((261, 1), F32)
    for t in range(4):
        cols = slice(256 * t, 256 * (t + 1))
        dxn = (pixel_cols(k, t)[:CX] + s.dxr[:, cols].astype(F32))[:261]
        hat, r = norm_cols(pix[:, cols].astype(F32))
        dhat = dxn * s.gcol[0:261, 0:1]
        even = jnp.mean(dhat, axis=0, keepdims=True)
        tilt = jnp.mean(dhat * hat, axis=0, keepdims=True)
        d_pix[:, cols] = r * (dhat - even - hat * tilt)
        gg_in += jnp.sum(dxn * hat, axis=1, keepdims=True)
    s.gcol[0:261, :] = jnp.broadcast_to(gg_in, (261, 128))
    s.ga[k] = jnp.zeros((8, D), F32)
    s.ga[k, 0:1, 0:CP] = s.gcol[...].T[0:1, :]
    for i, gg in enumerate((gg_lat, gg_cmlp, gg_self, gg_smlp)):
        s.ga[k, i + 1 : i + 2, :] = gg
    x_ga = put(s.ga.at[k], s.ga.at[k], sib)

    arrived(e_in)
    total = s.est[:, p, k].astype(F32)
    for i in range(3):
        total += s.epr[i].astype(F32)
    s.ez[...] = total.astype(BF)
    e_z = to_planes(lambda d: s.ez.at[plane[d]], lambda d: s.ezr.at[d - 1])
    x_ga.wait_recv()
    s.gb[p] = s.ga[0] + s.ga[1]
    gb_in = to_peers(lambda d: s.gb.at[p], lambda d: s.gb.at[p])
    arrived(f_in)
    total = s.fst[p, k].astype(F32)
    for i in range(3):
        total += s.fpr[i].astype(F32)
    s.fz[0] = total.astype(BF)
    f_z = to_planes(lambda d: s.fz.at[0], lambda d: s.fz.at[d])
    arrived(e_z)
    total = s.ez[z].astype(F32)
    for i in range(3):
        total += s.ezr[i].astype(F32)
    s.eag[c] = total.astype(BF)
    e_s = to_plane(s.eag.at[c])
    arrived(gb_in)
    s.gc[z] = s.gb[0] + s.gb[1] + s.gb[2] + s.gb[3]
    gc_in = to_planes(lambda d: s.gc.at[z], lambda d: s.gc.at[z])
    arrived(f_z)
    s.wvo[c, 0:CR, :] = sum(s.fz[d].astype(F32) for d in range(4)).astype(BF)

    def f_slot(i):
        return s.wvo.at[i, 0:CR]

    f_ag = gather(f_slot)
    g1u_z = up_to_planes(g1u, s.su1, s.zu1)
    g1d_z = down_to_planes(g1d, s.sd1, s.zd1)
    eighth = pl.ds(pl.multiple_of(c * 48, 16), 48)
    arrived(e_s)
    e_all = s.eag[...].reshape(256, CP)
    for j in range(4):
        s.gks[j] = mm_tn(e_all, s.wq_z[:, 256 * j : 256 * (j + 1)]).astype(BF)
    gk_z = to_planes(lambda d: s.gks.at[plane[d], eighth], lambda d: s.gkr.at[d - 1])
    sent([x_n3])
    for j in range(4):
        s.n3[:, :, 256 * j : 256 * (j + 1)] = mm(e_all, s.wk[j]).astype(BF).reshape(2, 128, 256)
    outs.extend(fetch(s.n3.at[i], d_big.at[8, 128 * i : 128 * (i + 1)]) for i in range(2))
    f_s = pass_on(f_ag)

    arrived(pg_z)
    for i in range(3):
        total = s.pg[i, k, own_z, :].astype(F32)
        for d in range(3):
            total += s.zq[d, i].astype(F32)
        s.agq[c, i] = total.astype(BF)
    q_ag = gather(lambda i: s.agq.at[i], lambda i, h: s.agq.at[i, :, 128 * h : 128 * h + 128])

    wo_ag = down_total(pgo_z, s.wz, s.zo, s.ago)
    relay(q_ag[1])
    arrived(gk_z)
    total = s.gks[z, eighth, :].astype(F32)
    for i in range(3):
        total += s.gkr[i].astype(F32)
    s.gkh[eighth, :] = total.astype(BF)
    x_gk = to_plane(s.gkh.at[eighth])
    g1u_ag = up_total(g1u_z, s.su1, s.zu1, s.agu1)
    g1d_ag = down_total(g1d_z, s.sd1, s.zd1, s.agd1)
    arrived(f_s)
    sent([x_n1])
    acc = jnp.zeros((CP, 256), F32)
    for j in range(4):
        f_two = jnp.concatenate([s.wvo[2 * j], s.wvo[2 * j + 1]], axis=1)
        acc += mm_nt(f_two, s.wo_z[:, 256 * j : 256 * (j + 1)])
        s.n1[:, :, 256 * j : 256 * (j + 1)] = mm_tn(s.wv_z[...], f_two).astype(BF).reshape(2, 128, 256)
    d_wv[...] = acc[:261]
    outs.extend(fetch(s.n1.at[i], d_big.at[9, 128 * i : 128 * (i + 1)]) for i in range(2))
    arrived(gc_in)
    d_gain[...] = s.gc[0] + s.gc[1] + s.gc[2] + s.gc[3]

    g3u_s = pass_on(g3u_ag)
    g3d_s = pass_on(g3d_ag)
    q_s = pass_on(q_ag)
    relay(wo_ag[1])
    wo_s_ = pass_on(wo_ag)
    relay(g1u_ag[1])
    relay(g1d_ag[1])
    g1u_s = pass_on(g1u_ag)
    g1d_s = pass_on(g1d_ag)
    arrived(x_gk)
    d_wk[...] = s.gkh[...].astype(F32)[0:261]
    arrived(g3u_s)
    out_cols(s.agu3, 6)
    arrived(g3d_s)
    out_rows(s.agd3, 7)
    arrived(q_s)
    for i in range(3):
        for j in range(8):
            outs.append(fetch(s.agq.at[j, i], d_big.at[2 + i, :, 128 * j : 128 * (j + 1)]))
    arrived(wo_s_)
    out_rows(s.ago, 5)
    arrived(g1u_s)
    out_cols(s.agu1, 0)
    arrived(g1d_s)
    out_rows(s.agd1, 1)
    for copy in outs:
        copy.wait()
    for when, copy in sends:
        if when is None:
            copy.wait_send()
        else:
            pl.when(when)(copy.wait_send)


def norm_cols(x):
    center = x - jnp.mean(x, axis=0, keepdims=True)
    r = lax.rsqrt(jnp.mean(center * center, axis=0, keepdims=True) + 1e-05)
    return center * r, r


def tag(val, lane, one, two):
    for i, x in enumerate((one, two)):
        for j in range(3):
            part = x.astype(BF).astype(F32)
            val = jnp.where(lane == 261 + 3 * i + j, part, val)
            x = x - part
    return val.astype(BF)


def untag(low, lane):
    val = low.astype(F32)

    def column(i):
        here = (lane >= 261 + 3 * i) & (lane < 264 + 3 * i)
        return jnp.sum(jnp.where(here, val, 0.0), axis=1, keepdims=True)

    return jnp.where(lane < 261, val, 0.0), column(0), column(1)


SCRATCH = {
    "ssem": 400, "rsem": 400, "lsem": 96,

    "wk": ((4, CP, 256), BF), "wqk": ((4, 2, 128, CP), BF), "wq_z": ((256, 1024), BF), "wo_z": ((256, 1024), BF),
    "wv_z": ((CP, 256), BF), "wvz": ((4, CR, 128), BF), "wvo": ((8, CP, 128), BF),
    "wu1": ((4, 1024, 128), BF), "wu3": ((4, 1024, 128), BF), "wd1": ((4, 4, 32, 1024), BF), "wd3": ((4, 4, 32, 1024), BF),
    "wqkv": ((3, 2, 1024, 128), BF), "wo": ((2, 128, 1024), BF),
    "xt": ((2, CP, 1024), BF), "span": ((1024, 128), jnp.int32), "pos": ((8, 1024), jnp.int32), "row": ((8, CP), F32), "gcol": ((CP, 128), F32), "ln": ((128, 1024), BF), "qk": ((4, 128, CP), BF),
    "pxs": ((4, 128, CP), BF), "pxr": ((3, 128, CP), BF), "px": ((128, CP), F32), "pxl": ((128, CP), BF),
    "cpair": ((2, 128, 1024), BF), "n1": ((2, 128, 1024), BF), "n3": ((2, 128, 1024), BF),
    "u1": ((2, 256, 256), F32), "u3": ((2, 256, 256), F32), "z1": ((2, 256, 256), BF), "z3": ((2, 256, 256), BF),
    "gu1": ((2, 256, 256), BF), "gu3": ((2, 256, 256), BF),


    "h1": ((128, 1024), F32), "h2": ((128, 1024), F32), "h3": ((128, 1024), F32), "dh": ((128, 1024), F32),
    "n2": ((4, 128, 1024), BF), "go": ((4, 128, 1024), BF), "pair": ((128, 256), BF),
    "heads": ((2, 4, 3, 128, 128), BF), "mine": ((8, 3, 128, 128), BF),
    "a1": ((8, 128, 1024), BF), "a2": ((8, 128, 1024), BF), "send": ((4, 128, 128), BF), "aspar": ((4, 2, 128, 128), BF),
    "outp": ((3, 128, 1024), BF), "outr": ((3, 128, 1024), BF),
    "gheads": ((2, 4, 128, 128), BF), "gmine": ((8, 128, 128), BF),
    "dsend": ((4, 3, 128, 128), BF), "dpar": ((4, 3, 2, 128, 128), BF),


    "zu1": ((3, 256, 128), BF), "zu3": ((3, 256, 128), BF), "zd1": ((3, 32, 1024), BF), "zd3": ((3, 32, 1024), BF),
    "agu1": ((8, 256, 128), BF), "agu3": ((8, 256, 128), BF), "agd1": ((2, 4, 32, 1024), BF), "agd3": ((2, 4, 32, 1024), BF),
    "pg": ((3, 2, 1024, 128), BF), "pgr": ((3, 1024, 128), BF), "zq": ((3, 3, 256, 128), BF), "agq": ((8, 3, 256, 128), BF),
    "pgo": ((2, 128, 1024), BF), "pgor": ((128, 1024), BF), "zo": ((3, 32, 1024), BF), "ago": ((2, 4, 32, 1024), BF), "woz": ((4, 32, 1024), BF), "wz": ((4, 32, 1024), BF),
    "gv": ((4, 128, CP), BF), "dqk": ((128, CP), F32),
    "dxs": ((CX, 1024), BF), "dxr": ((CX, 1024), BF),
    "fst": ((4, 2, CR, 128), BF), "fsr": ((4, CR, 128), BF), "fpr": ((3, CR, 128), BF), "fz": ((4, CR, 128), BF),
    "est": ((4, 4, 2, 32, CP), BF), "esr": ((4, 4, 32, CP), BF), "epr": ((3, 4, 32, CP), BF), "ez": ((4, 32, CP), BF),
    "ezr": ((3, 32, CP), BF), "eag": ((8, 32, CP), BF),
    "gks": ((4, CP, 256), BF), "gkr": ((3, 48, 256), BF), "gkh": ((CP, 256), BF), "gpair": ((2, 128, 1024), BF), "zg": ((3, 4, 256, 128), BF), "zs": ((4, 256, 128), BF),
    "ga": ((2, 8, 1024), F32), "gb": ((4, 8, 1024), F32), "gc": ((4, 8, 1024), F32),
    "hpa": ((2, 128, 1024), F32), "hpb": ((2, 128, 1024), F32), "hxa": ((128, 1024), F32), "hxb": ((128, 1024), F32),
    "ee": ((8, 128, 1024), BF), "tops": ((4, 128, 128), F32), "gvr": ((4, 128, CP), BF),
    "gsu": ((4, 1024, 128), BF), "gsd": ((4, 4, 32, 1024), BF), "gru": ((3, 1024, 128), BF), "grd": ((3, 4, 32, 1024), BF),
    "su1": ((1024, 128), BF), "sd1": ((4, 32, 1024), BF), "sd3": ((4, 32, 1024), BF),
}


def unpack(layer_in, lat_in, big_in, wk_in, wv_in, gain_in, pix_in, layer_out, d_lat, *rest):
    big = rest[:10]
    wk_out, wv_out, gains, first, pix_out = rest[10], rest[11], rest[12:16], rest[16], rest[17]
    low, wide, pix_rows, sem_in, sem_out = rest[18:]
    loads = [pltpu.make_async_copy(big_in.at[i], low.at[i], sem_in.at[i]) for i in range(10)]
    for copy in loads:
        copy.start()
    pairs = ((layer_in, layer_out), (lat_in, d_lat), (wk_in, wk_out), (wv_in, wv_out))
    stores = [pltpu.make_async_copy(a, b, sem_out.at[i]) for i, (a, b) in enumerate(pairs)]
    for copy in stores:
        copy.start()
    for i in range(10):
        loads[i].wait()
        wide[i] = low[i].astype(F32)
        stores.append(pltpu.make_async_copy(wide.at[i], big[i], sem_out.at[4 + i]))
        stores[-1].start()
    pix_rows[...] = pix_in[...].reshape(261, 1, 1024)
    stores.append(pltpu.make_async_copy(pix_rows, pix_out, sem_out.at[18]))
    stores[-1].start()
    first[...] = gain_in[0:1, 0:261].reshape(261)
    for i in range(4):
        stores.append(pltpu.make_async_copy(gain_in.at[i + 1 : i + 2], gains[i], sem_out.at[14 + i]))
        stores[-1].start()
    for copy in stores:
        copy.wait()


def one_kernel(
    pixels, latents, cotangent, doc_lengths, latent_offsets, block_deal,
    wq_c, wk_c, wv_c, wo_c, wu_c, wd_c, wq_s, wk_s, wv_s, wo_s, wu_s, wd_s,
    g_in, g_lat, g_cmlp, g_self, g_smlp,
):
    vmem, hbm = pl.BlockSpec(memory_space=pltpu.VMEM), pl.BlockSpec(memory_space=pl.ANY)
    smem = pl.BlockSpec(memory_space=pltpu.SMEM)

    def shape(dims, kind=F32):
        return jax.ShapeDtypeStruct(dims, kind)

    layer_out, d_pix, d_lat, big, d_wk, d_wv, gains = pl.pallas_call(
        fused,
        out_shape=(
            shape((128, D), BF), shape((261, 1024)), shape((128, D)), shape((10, 256, D), BF),
            shape((261, 256)), shape((261, 256)), shape((8, D)),
        ),
        in_specs=[vmem, vmem, vmem, smem, vmem, smem] + [vmem] * 5 + [hbm] * 12,
        out_specs=(vmem, vmem, hbm, hbm, vmem, vmem, vmem),
        scratch_shapes=[
            pltpu.SemaphoreType.DMA((what,)) if isinstance(what, int) else pltpu.VMEM(*what)
            for what in SCRATCH.values()
        ],
        compiler_params=pltpu.CompilerParams(
            collective_id=0, has_side_effects=True, vmem_limit_bytes=VMEM_BYTES
        ),
        cost_estimate=pl.CostEstimate(flops=26 * 10**9, bytes_accessed=40 * 10**6, transcendentals=10**7),
    )(
        pixels[0].T, latents[0], cotangent[0], doc_lengths, latent_offsets, block_deal,
        g_in, g_lat[None], g_cmlp[None], g_self[None], g_smlp[None],
        wq_c, wk_c, wv_c, wo_c, wu_c, wd_c, wq_s, wk_s, wv_s, wo_s, wu_s, wd_s,
    )
    outs = pl.pallas_call(
        unpack,
        out_shape=(
            shape((128, D), BF), shape((128, D)), *[shape((256, D))] * 10, *[shape((261, 256))] * 2, *[shape((1, D))] * 4,
            shape((261,)), shape((261, 1, 1024)),
        ),
        in_specs=[vmem, vmem, hbm, vmem, vmem, vmem, vmem],
        out_specs=(*[hbm] * 18, vmem, hbm),
        scratch_shapes=[
            pltpu.VMEM((10, 256, D), BF), pltpu.VMEM((10, 256, D), F32), pltpu.VMEM((261, 1, 1024), F32),
            pltpu.SemaphoreType.DMA((10,)), pltpu.SemaphoreType.DMA((19,)),
        ],
        compiler_params=pltpu.CompilerParams(vmem_limit_bytes=VMEM_BYTES),
        cost_estimate=pl.CostEstimate(flops=0, bytes_accessed=18 * 10**6, transcendentals=0),
    )(layer_out, d_lat, big, d_wk, d_wv, gains, d_pix)
    layer_out, d_lat, d_big, d_wk, d_wv, d_gain = outs[0], outs[1], outs[2:12], outs[12], outs[13], outs[14:18]
    return (
        layer_out[None], outs[19].transpose(1, 2, 0), d_lat[None], d_big[8], d_wk, d_wv, d_big[9], *d_big[:8],
        outs[18], *(g[0] for g in d_gain),
    )


VMEM_BYTES = 65472 * 2**10


def solution(mesh):
    rows, row, col, all_ = P("fsdp", "ctx", None), P("fsdp", None), P(None, "fsdp"), P()
    weights = (row, col, col, *(row,) * 9)
    small = mesh.shape["ctx"] == 8 and mesh.shape["fsdp"] == 4
    return jax.shard_map(
        one_kernel if small else plain,
        mesh=mesh,
        in_specs=(rows, rows, rows, row, row, all_, *weights, *(all_,) * 5),
        out_specs=(rows, rows, rows, *weights, *(all_,) * 5),
        check_vma=False,
    )
```

```python
import math
import types

import jax
import jax.numpy as jnp
from jax import lax
from jax.experimental import pallas as pl
from jax.experimental.pallas import tpu as pltpu
from jax.sharding import PartitionSpec as P

D = 1024
HEADS = 8
HEAD = D // HEADS
STRIDE = 8
LBLK = 64
BF = jnp.bfloat16
F32 = jnp.float32
CROSS_SCALE = 1.0 / math.sqrt(D)
SELF_SCALE = 1.0 / math.sqrt(HEAD)
MASKED = -1e30
GELU_K = math.sqrt(2.0 / math.pi)
GELU_A = 0.044715


def mm(a, b):
    return jnp.dot(a, b, preferred_element_type=F32)


def mm_nt(a, b):
    return lax.dot_general(a, b, (((1,), (1,)), ((), ())), preferred_element_type=F32)


def mm_tn(a, b):
    return lax.dot_general(a, b, (((0,), (0,)), ((), ())), preferred_element_type=F32)


def norm_parts(x):
    center = x - jnp.mean(x, axis=-1, keepdims=True)
    r = lax.rsqrt(jnp.mean(center * center, axis=-1, keepdims=True) + 1e-05)
    return center * r, r


def norm_back(dy, x, gain):
    hat, r = norm_parts(x)
    dhat = dy * gain
    dx = r * (
        dhat
        - jnp.mean(dhat, axis=-1, keepdims=True)
        - hat * jnp.mean(dhat * hat, axis=-1, keepdims=True)
    )
    return dx, jnp.sum(dy * hat, axis=0, keepdims=True)


def gelu(u):
    return 0.5 * u * (1.0 + jnp.tanh(GELU_K * (u + GELU_A * u * u * u)))


def gelu_slope(u):
    t = jnp.tanh(GELU_K * (u + GELU_A * u * u * u))
    return 0.5 * (1.0 + t) + 0.5 * u * (1.0 - t * t) * GELU_K * (1.0 + 3.0 * GELU_A * u * u)


def intervals(lengths, offsets, deal):
    count = lengths.shape[0]
    before = jnp.arange(count)[:, None] > jnp.arange(count)[None, :]
    starts = jnp.sum(jnp.where(before, lengths[None, :], 0), axis=1)
    base = (deal[:, None] * LBLK + jnp.arange(LBLK, dtype=jnp.int32)[None, :]).reshape(-1)
    pos = base * STRIDE + offsets
    lo = jnp.max(jnp.where(starts[None, :] <= pos[:, None], starts[None, :], -1), axis=1)
    return lo, pos


def plain(
    pixels, latents, cotangent, doc_lengths, latent_offsets, block_deal,
    wq_c, wk_c, wv_c, wo_c, wu_c, wd_c, wq_s, wk_s, wv_s, wo_s, wu_s, wd_s,
    g_in, g_lat, g_cmlp, g_self, g_smlp,
):
    n = lax.axis_size("ctx")
    me = lax.axis_index("ctx")
    rows = latents.shape[1]
    npix = pixels.shape[1]
    c = pixels.shape[2]
    lo, pos = intervals(doc_lengths[0], latent_offsets[0], block_deal)
    own_lo = lax.dynamic_slice_in_dim(lo, me * rows, rows)
    own_pos = lax.dynamic_slice_in_dim(pos, me * rows, rows)
    pix_pos = me * npix + jnp.arange(npix, dtype=jnp.int32)
    mask = (lo[:, None] <= pix_pos[None, :]) & (pix_pos[None, :] <= pos[:, None])
    smask = (own_lo[:, None] <= pos[None, :]) & (pos[None, :] <= own_pos[:, None])

    wq_c, wk_c, wv_c, wo_c = (w.astype(BF) for w in (wq_c, wk_c, wv_c, wo_c))
    wk_all = lax.all_gather(wk_c, "fsdp", axis=1, tiled=True)
    wqk = lax.all_gather(mm_nt(wq_c, wk_all).astype(BF), "fsdp", axis=0, tiled=True)
    wvo = lax.psum(mm(wv_c, wo_c), "fsdp").astype(BF)
    big = jnp.stack([w.astype(BF) for w in (wu_c, wd_c, wq_s, wk_s, wv_s, wo_s, wu_s, wd_s)])
    wu1, wd1, wq, wk, wv, wo, wu3, wd3 = lax.all_gather(big, "fsdp", axis=1, tiled=True)

    xin = pixels[0].astype(F32)
    xn = (norm_parts(xin)[0] * g_in).astype(BF)
    lat = latents[0].astype(F32)
    ln = (norm_parts(lat)[0] * g_lat).astype(BF)
    qk_all = lax.all_gather(mm(ln, wqk).astype(BF), "ctx", axis=0, tiled=True)
    s = jnp.where(mask, mm_nt(qk_all, xn) * CROSS_SCALE, MASKED)
    top = jnp.max(s, axis=1, keepdims=True)
    e = lax.optimization_barrier(jnp.where(mask, jnp.exp(s - top), 0.0).astype(BF))
    total = jnp.sum(e.astype(F32), axis=1, keepdims=True)
    part = jnp.concatenate([mm(e, xn), top, total], axis=1)
    parts = lax.all_to_all(part.reshape(n, rows, c + 2), "ctx", 0, 0)
    tops = parts[:, :, c : c + 1]
    high = jnp.max(tops, axis=0)
    share = jnp.exp(tops - high[None])
    full = jnp.sum(share * parts[:, :, c + 1 :], axis=0)
    px = jnp.sum(share * parts[:, :, :c], axis=0) / full
    lse = high + jnp.log(full)
    px_low = px.astype(BF)
    h1 = lat + mm(px_low, wvo)
    n1 = (norm_parts(h1)[0] * g_cmlp).astype(BF)
    u1 = mm(n1, wu1)
    z1 = gelu(u1).astype(BF)
    h2 = h1 + mm(z1, wd1)
    n2 = (norm_parts(h2)[0] * g_self).astype(BF)
    q = mm(n2, wq).astype(BF).reshape(rows, HEADS, HEAD)
    kv = jnp.concatenate([mm(n2, wk), mm(n2, wv)], axis=1).astype(BF)
    kv = lax.all_gather(kv, "ctx", axis=0, tiled=True)
    k = kv[:, :D].reshape(n * rows, HEADS, HEAD)
    v = kv[:, D:].reshape(n * rows, HEADS, HEAD)
    ss = jnp.einsum("qhd,khd->hqk", q, k, preferred_element_type=F32) * SELF_SCALE
    ss = jnp.where(smask[None], ss, MASKED)
    se = jnp.exp(ss - jnp.max(ss, axis=-1, keepdims=True))
    ps = se / jnp.sum(se, axis=-1, keepdims=True)
    psl = ps.astype(BF)
    sa = jnp.einsum("hqk,khd->qhd", psl, v, preferred_element_type=F32)
    sa = sa.reshape(rows, D).astype(BF)
    h3 = h2 + mm(sa, wo)
    n3 = (norm_parts(h3)[0] * g_smlp).astype(BF)
    u3 = mm(n3, wu3)
    z3 = gelu(u3).astype(BF)
    layer_out = (h3 + mm(z3, wd3)).astype(BF)

    gy3 = cotangent[0]
    gu3 = (mm_nt(gy3, wd3) * gelu_slope(u3)).astype(BF)
    dx, gg_smlp = norm_back(mm_nt(gu3, wu3), h3, g_smlp)
    dh3 = gy3.astype(F32) + dx
    go3 = dh3.astype(BF)
    gas = mm_nt(go3, wo).astype(BF).reshape(rows, HEADS, HEAD)
    dps = jnp.einsum("qhd,khd->hqk", gas, v, preferred_element_type=F32)
    sdelta = jnp.sum(ps * dps, axis=-1, keepdims=True)
    dss = (ps * (dps - sdelta) * SELF_SCALE).astype(BF)
    dqs = jnp.einsum("hqk,khd->qhd", dss, k, preferred_element_type=F32)
    dqs = dqs.reshape(rows, D).astype(BF)
    dks = jnp.einsum("hqk,qhd->khd", dss, q, preferred_element_type=F32).reshape(n * rows, D)
    dvs = jnp.einsum("hqk,qhd->khd", psl, gas, preferred_element_type=F32).reshape(n * rows, D)
    dkv = lax.psum_scatter(
        jnp.concatenate([dks, dvs], axis=1), "ctx", scatter_dimension=0, tiled=True
    ).astype(BF)
    dks, dvs = dkv[:, :D], dkv[:, D:]
    dn2 = mm_nt(dqs, wq) + mm_nt(dks, wk) + mm_nt(dvs, wv)
    dx, gg_self = norm_back(dn2, h2, g_self)
    dh2 = dh3 + dx
    gy1 = dh2.astype(BF)
    gu1 = (mm_nt(gy1, wd1) * gelu_slope(u1)).astype(BF)
    dx, gg_cmlp = norm_back(mm_nt(gu1, wu1), h1, g_cmlp)
    dh1 = dh2 + dx
    go1 = dh1.astype(BF)
    gv = lax.optimization_barrier(mm_nt(go1, wvo).astype(BF))
    delta = jnp.sum(px * gv.astype(F32), axis=1, keepdims=True)
    gv_all = lax.all_gather(gv, "ctx", axis=0, tiled=True)
    stat = lax.all_gather(jnp.concatenate([lse, delta], axis=1), "ctx", axis=0, tiled=True)
    p = jnp.where(mask, jnp.exp(s - stat[:, :1]), 0.0)
    ds = (p * (mm_nt(gv_all, xn) - stat[:, 1:]) * CROSS_SCALE).astype(BF)
    dxn = mm_tn(ds, qk_all) + mm_tn(p.astype(BF), gv_all)
    dpix, gg_in = norm_back(dxn, xin, g_in)
    dqk = lax.psum_scatter(mm(ds, xn), "ctx", scatter_dimension=0, tiled=True).astype(BF)
    dx, gg_lat = norm_back(mm_nt(dqk, wqk), lat, g_lat)
    dlat = dh1 + dx

    e_sum = lax.psum_scatter(mm_tn(ln, dqk), "fsdp", scatter_dimension=0, tiled=True)
    e_sum, f_sum = lax.psum((e_sum, lax.psum(mm_tn(px_low, go1), "fsdp")), "ctx")
    e_sum, f_sum = e_sum.astype(BF), f_sum.astype(BF)
    d_wq_c = mm(e_sum, wk_all)
    d_wk_c = lax.psum_scatter(mm_tn(e_sum, wq_c), "fsdp", scatter_dimension=1, tiled=True)
    d_wv_c = mm_nt(f_sum, wo_c)
    d_wo_c = mm_tn(wv_c, f_sum)
    pairs = ((n1, gu1), (z1, gy1), (n2, dqs), (n2, dks), (n2, dvs), (sa, go3), (n3, gu3), (z3, gy3))
    d_big = [
        lax.psum(lax.psum_scatter(mm_tn(a, b), "fsdp", scatter_dimension=0, tiled=True), "ctx")
        for a, b in pairs
    ]
    gains = lax.psum(jnp.concatenate([gg_in[0], gg_lat[0], gg_cmlp[0], gg_self[0], gg_smlp[0]]), ("ctx", "fsdp"))
    return (
        layer_out[None], dpix[None], dlat[None], d_wq_c, d_wk_c, d_wv_c, d_wo_c, *d_big,
        gains[:c], gains[c : c + D], gains[c + D : c + 2 * D],
        gains[c + 2 * D : c + 3 * D], gains[c + 3 * D :],
    )


CP = 384
CR = 288
CX = 272
PARITY_ROWS = 4 * 128


def fused(
    pix, lat, cot, lengths, offsets, deal, g_in, g_lat, g_cmlp, g_self, g_smlp,
    wq_c, wk_c, wv_c, wo_c, wu_1, wd_1, wq_s, wk_s, wv_s, wo_s, wu_3, wd_3,
    layer_out, d_pix, d_lat, d_big, d_wk, d_wv, d_gain,
    *scratch,
):
    s = types.SimpleNamespace(**dict(zip(SCRATCH, scratch)))
    c, z = lax.axis_index("ctx"), lax.axis_index("fsdp")
    k, p = lax.rem(c, 2), lax.div(c, 2)
    k2 = 1 - k

    def flip(v, d):
        low, high = lax.rem(v, 2), lax.div(v, 2)
        return (1 - low if d & 1 else low) + 2 * (1 - high if d & 2 else high)

    chip = {d: flip(p, d) for d in (1, 2, 3)}
    plane = {d: flip(z, d) for d in (1, 2, 3)}
    sib = {"ctx": 2 * p + k2}

    def peer(d):
        return {"ctx": 2 * chip[d] + k}

    def across(d):
        return {"ctx": 2 * chip[d] + k2}

    def level(d):
        return {"fsdp": plane[d]}

    used = [0, 0]
    sends = []

    def make(src, dst, target, slot=None):
        if slot is None:
            slot = used[0]
            used[0] += 1
        send = used[1]
        used[1] += 1
        return pltpu.make_async_remote_copy(
            src_ref=src, dst_ref=dst, send_sem=s.ssem.at[send], recv_sem=s.rsem.at[slot],
            device_id=target, device_id_type=pl.DeviceIdType.MESH,
        )

    def put(src, dst, target):
        copy = make(src, dst, target)
        copy.start()
        sends.append((None, copy))
        return copy

    def sent(copies):
        for copy in copies.values() if isinstance(copies, dict) else copies:
            copy.wait_send()
            sends[:] = [pair for pair in sends if pair[1] is not copy]

    def to_peers(src_of, dst_of, order=(3, 1, 2)):
        return {d: put(src_of(d), dst_of(d), peer(d)) for d in order}

    def to_planes(src_of, dst_of):
        return {d: put(src_of(d), dst_of(d), level(d)) for d in (1, 2, 3)}

    def arrived(copies):
        for copy in copies.values() if isinstance(copies, dict) else copies:
            copy.wait_recv()

    locals_ = [0]

    def fetch(src, dst):
        copy = pltpu.make_async_copy(src, dst, s.lsem.at[locals_[0]])
        locals_[0] += 1
        copy.start()
        return copy

    def spread(part_of):
        mine = [part_of(p, h) for h in range(2)]
        copies = {(d, h): put(mine[h], mine[h], peer(d)) for d, h in ((1, 0), (2, 1), (1, 1), (2, 0))}
        return part_of, copies, []

    def relay(state):
        part_of, copies, on = state
        for d, h in ((1, 0), (2, 1)):
            copies[d, h].wait_recv()
            part = part_of(chip[d], h)
            on.append(put(part, part, peer(3 - d)))

    def near(state, d):
        state[1][d, 2 - d].wait_recv()

    def far(state):
        arrived(state[2])

    def all_of(state):
        near(state, 1)
        near(state, 2)
        far(state)

    def fold(part_of, into):
        first = [put(part_of(3, h), into(0, h), peer(1 + h)) for h in range(2)]
        near_ = [put(part_of(1 + h, h), into(1, h), peer(1 + h)) for h in range(2)]
        return part_of, into, first, near_

    def fold_on(state):
        part_of, into, first, near_ = state
        for h in range(2):
            first[h].wait_recv()
            part = part_of(2 - h, h)
            part[...] = (part[...].astype(F32) + into(0, h)[...].astype(F32)).astype(BF)
            near_.append(put(part, into(2, h), peer(2 - h)))

    def gather(slot_of, half_of=None):
        own = put(slot_of(c), slot_of(c), sib)
        if half_of is None:
            return slot_of, to_peers(lambda d: slot_of(c), lambda d: slot_of(c)), [own]
        return slot_of, spread(lambda q, h: half_of(2 * q + k, h)), [own]

    def pass_on(state):
        slot_of, copies, to_sib = state
        if not isinstance(copies, dict):
            all_of(copies)
        for d in (1, 2, 3):
            if isinstance(copies, dict):
                copies[d].wait_recv()
            there = slot_of(2 * chip[d] + k)
            to_sib.append(put(there, there, sib))
        return to_sib

    def to_plane(part):
        return [put(part, part, to) for to in (*(peer(d) for d in (1, 2, 3)), *(across(d) for d in (1, 2, 3)), sib)]

    for j in range(4):
        s.wk[j, 256:CP, :] = jnp.zeros((CP - 256, 256), BF)
    s.wv_z[256:CP, :] = jnp.zeros((CP - 256, 256), BF)
    for j in range(2):
        s.xt[j, 256:CP, :] = jnp.zeros((CP - 256, 1024), BF)
    for j in range(8):
        s.wvo[j, CR:CP, :] = jnp.zeros((CP - CR, 128), BF)
    barrier = pltpu.get_barrier_semaphore()
    near_by = (sib, *(across(d) for d in (1, 2, 3)), *(peer(d) for d in (1, 2, 3)))
    for target in (*near_by, *(level(d) for d in (1, 2, 3))):
        pl.semaphore_signal(barrier, inc=1, device_id=target, device_id_type=pl.DeviceIdType.MESH)
    lanes = pl.ds(pl.multiple_of(c * 128, 128), 128)
    quarter = pl.ds(pl.multiple_of(k * 128 + p * 32, 32), 32)
    f_wk = [fetch(wk_c.at[0:256], s.u1.at[0]), fetch(wk_c.at[256:261], s.u1.at[1, 0:5])]
    f_wq = [fetch(wq_c.at[128 * i : 128 * (i + 1)], s.hpa.at[i]) for i in range(2)]
    f_wv = [fetch(wv_c.at[0:256], s.u3.at[0]), fetch(wv_c.at[256:261], s.u3.at[1, 0:5])]
    f_wo = [fetch(wo_c.at[128 * i : 128 * (i + 1)], s.hpb.at[i]) for i in range(2)]

    def early(i):
        return (s.dh if i < 8 else s.hxb).at[:, 128 * (i % 8) : 128 * (i % 8) + 128]

    f_u = [
        fetch(w.at[128 * j : 128 * (j + 1), lanes], early(2 * i + j))
        for i, w in enumerate((wu_1, wu_3, wq_s, wk_s, wv_s))
        for j in range(2)
    ]
    f_d = [fetch(w.at[quarter, :], s.h3.at[32 * i : 32 * (i + 1)]) for i, w in enumerate((wd_1, wo_s))]
    f_d3 = fetch(wd_3.at[pl.ds(pl.multiple_of(k * 128, 128), 128), :], s.hxa)
    pl.semaphore_wait(barrier, 10)

    for copy in f_wk:
        copy.wait()
    s.wk[z, 0:256, :] = s.u1[0].astype(BF)
    s.wk[z, 256:261, :] = s.u1[1, 0:5, :].astype(BF)
    half = pl.ds(pl.multiple_of(k * 144, 16), 144)
    wk_z = to_planes(lambda d: s.wk.at[z, half], lambda d: s.wk.at[z, half])
    for copy in f_u:
        copy.wait()
    own_z = pl.ds(pl.multiple_of(z * 256, 256), 256)
    for j in range(2):
        half_z = pl.ds(pl.multiple_of(z * 256 + 128 * j, 128), 128)
        s.wu1[p, half_z, :] = early(j)[...].astype(BF)
    wu1_z = to_planes(lambda d: s.wu1.at[p, own_z], lambda d: s.wu1.at[p, own_z])
    s.cpair[k] = cot[...]
    x_cot = put(s.cpair.at[k], s.cpair.at[k], sib)

    order = lax.broadcasted_iota(jnp.int32, (8, D), 1)
    block = lax.div(order, LBLK)
    base = jnp.zeros((8, D), jnp.int32)
    for i in range(D // LBLK):
        base = jnp.where(block == i, deal[i], base)
    pos_r = (base * LBLK + lax.rem(order, LBLK)) * STRIDE + offsets[...]
    lo_r = jnp.zeros((8, D), jnp.int32)
    start = lengths[0, 0]
    for i in range(1, lengths.shape[1]):
        lo_r = jnp.where(start <= pos_r, start, lo_r)
        start = start + lengths[0, i]
    s.pos[...] = pos_r
    top_row = lax.broadcasted_iota(jnp.int32, (128, 128), 0) == 0
    for b in range(8):
        cols = slice(128 * b, 128 * (b + 1))
        both_rows = jnp.where(top_row, lo_r[0:1, cols], pos_r[0:1, cols]).astype(F32)
        s.span[cols, :] = both_rows.T.astype(jnp.int32)
    s.row[0:1, 0:256] = g_in[0:256].reshape(1, 256)
    s.row[0:1, 256:261] = g_in[256:261].reshape(1, 5)
    s.gcol[...] = jnp.broadcast_to(s.row[0:1, :], (128, CP)).T

    def norm_pixels(t):
        cols = slice(256 * t, 256 * (t + 1))
        normed = (norm_cols(pix[:, cols].astype(F32))[0] * s.gcol[0:261, 0:1]).astype(BF)
        s.xt[k, 0:256, cols] = normed[0:256]
        s.xt[k, 256:261, cols] = normed[256:261]

    for t in range(4):
        norm_pixels(t)
    ln = (norm_parts(lat[...].astype(F32))[0] * g_lat[...]).astype(BF)
    s.lnp[p] = ln
    ln_in = spread(lambda q, h: s.lnp.at[q, 64 * h : 64 * h + 64])
    for i in range(2):
        f_wq[i].wait()
        s.wq_z[128 * i : 128 * (i + 1), :] = s.hpa[i].astype(BF)
    wk_s_in = []
    for d in (1, 2, 3):
        wk_z[d].wait_recv()
        there = s.wk.at[plane[d], half]
        wk_s_in.append(put(there, there, sib))
    relay(ln_in)
    for copy in f_wv:
        copy.wait()
    s.wv_z[0:256, :] = s.u3[0].astype(BF)
    s.wv_z[256:261, :] = s.u3[1, 0:5, :].astype(BF)
    for i in range(2):
        f_wo[i].wait()
        s.wo_z[128 * i : 128 * (i + 1), :] = s.hpb[i].astype(BF)
    wvo_part = mm(s.wv_z[...], s.wo_z[:, lanes])
    s.wvz[0] = wvo_part[:CR].astype(BF)
    arrived(wk_s_in)
    own_rows = pl.ds(pl.multiple_of(k * 128, 128), 128)
    part = jnp.zeros((128, CP), F32)
    for j in range(4):
        part += mm_nt(s.wq_z[own_rows, 256 * j : 256 * (j + 1)], s.wk[j])
    s.wqk[z, k] = part.astype(BF)
    wqk_z = to_planes(lambda d: s.wqk.at[z, k], lambda d: s.wqk.at[z, k])
    wqk_s = [put(s.wqk.at[z, k], s.wqk.at[z, k], sib)]
    wvo_z = to_planes(lambda d: s.wvz.at[0], lambda d: s.wvz.at[d])
    x_xn = put(s.xt.at[k, 0:CX], s.xt.at[k, 0:CX], sib)
    for copy in f_d:
        copy.wait()
    s.wd1[z, p] = s.h3[0:32, :].astype(BF)
    wd1_z = to_planes(lambda d: s.wd1.at[z, p], lambda d: s.wd1.at[z, p])

    for j in range(2):
        half_z = pl.ds(pl.multiple_of(z * 256 + 128 * j, 128), 128)
        s.wu3[p, half_z, :] = early(2 + j)[...].astype(BF)
        for i in range(3):
            s.wqkv[i, k, half_z, :] = early(4 + 2 * i + j)[...].astype(BF)
    s.woz[z] = s.h3[32:64, :].astype(BF)
    f_d3.wait()
    s.wd3[z] = s.hxa[...].astype(BF).reshape(4, 32, D)
    arrived(wu1_z)
    wu1_in = spread(lambda q, h: s.wu1.at[q, 512 * h : 512 * h + 512])
    for d in (1, 2, 3):
        wqk_z[d].wait_recv()
        there = s.wqk.at[plane[d], k]
        wqk_s.append(put(there, there, sib))
    relay(wu1_in)
    arrived(wqk_s)
    wqk = s.wqk[...].reshape(D, CP)
    s.qk[p] = mm(ln, wqk).astype(BF)
    qk_in = to_peers(lambda d: s.qk.at[p], lambda d: s.qk.at[p])
    arrived(wvo_z)
    s.wvo[c, 0:CR, :] = sum(s.wvz[d].astype(F32) for d in range(4)).astype(BF)

    def wvo_slot(i):
        return s.wvo.at[i, 0:CR]

    wvo_in = gather(wvo_slot)
    wu3_z = to_planes(lambda d: s.wu3.at[p, own_z], lambda d: s.wu3.at[p, own_z])
    qkv_z = to_planes(lambda d: s.wqkv.at[:, k, own_z], lambda d: s.wqkv.at[:, k, own_z])
    wo_z = to_planes(lambda d: s.woz.at[z], lambda d: s.woz.at[z])
    wd3_z = to_planes(lambda d: s.wd3.at[z], lambda d: s.wd3.at[z])
    x_xn.wait_recv()

    wide = lax.broadcasted_iota(jnp.int32, (128, 1024), 1)
    lane = lax.broadcasted_iota(jnp.int32, (128, CP), 1)

    def cross_block(q):
        rows = pl.ds(pl.multiple_of((2 * q + k) * 128, 128), 128)
        low, high = s.span[rows, 0:1], s.span[rows, 1:2]
        scores = []
        for h in range(2):
            at = wide + (2 * p + h) * 1024
            sc = mm(s.qk[q], s.xt[h]) * CROSS_SCALE
            scores.append(jnp.where((at >= low) & (at <= high), sc, MASKED))
        top = jnp.maximum(*(jnp.max(sc, axis=1, keepdims=True) for sc in scores))
        total = jnp.zeros((128, 1), F32)
        acc = jnp.zeros((128, CP), F32)
        for h in range(2):
            e = jnp.where(scores[h] > 0.5 * MASKED, jnp.exp(scores[h] - top), 0.0).astype(BF)
            s.ee[2 * q + h] = e
            total += jnp.sum(e.astype(F32), axis=1, keepdims=True)
            acc += mm_nt(e, s.xt[h])
        s.tops[q] = jnp.broadcast_to(top, (128, 128))
        s.pxs[q] = tag(acc, lane, top, total)

    cross_block(p)
    px_in = {}
    for d in (1, 2, 3):
        qk_in[d].wait_recv()
        cross_block(chip[d])
        px_in[d] = put(s.pxs.at[chip[d]], s.pxr.at[d - 1], peer(d))
    wvo_s = pass_on(wvo_in)
    arrived(wd1_z)
    wd1_in = spread(lambda q, h: s.wd1.at[2 * h : 2 * h + 2, q])
    arrived(px_in)
    found = [untag(s.pxs[p], lane)] + [untag(s.pxr[i], lane) for i in range(3)]
    high = found[0][1]
    for f in found[1:]:
        high = jnp.maximum(high, f[1])
    px, total = jnp.zeros((128, CP), F32), jnp.zeros((128, 1), F32)
    for val, top, tot in found:
        share = jnp.exp(top - high)
        px += share * val
        total += share * tot
    px = px / total
    s.px[...] = px
    lse = high + jnp.log(total)
    s.pxl[...] = px.astype(BF)
    relay(wd1_in)
    arrived(wvo_s)
    lat_f = lat[...].astype(F32)
    pxl = s.pxl[...]
    for j in range(4):
        cols = slice(256 * j, 256 * (j + 1))
        w = jnp.concatenate([s.wvo[2 * j], s.wvo[2 * j + 1]], axis=1)
        s.h1[:, cols] = lat[:, cols].astype(F32) + mm(pxl, w)

    def mlp_start(h_ref, gain, npair):
        npair[k] = (norm_parts(h_ref[...])[0] * gain[...]).astype(BF)
        return put(npair.at[k], npair.at[k], sib)

    def mlp_up(npair, wu, u, zb):
        rows = npair[...].reshape(256, D)
        for j in range(2):
            w = jnp.concatenate([wu[2 * j], wu[2 * j + 1]], axis=1)
            hidden = mm(rows, w)
            u[j] = hidden
            zb[j] = gelu(hidden).astype(BF)

    def mlp_down(zb, wd, hp, hx):
        for t in range(4):
            cols = slice(256 * t, 256 * (t + 1))
            acc = mm(zb[0], wd[0:2, :, :, cols].reshape(256, 256))
            acc += mm(zb[1], wd[2:4, :, :, cols].reshape(256, 256))
            hp[:, :, cols] = acc.reshape(2, 128, 256)
        return put(hp.at[k2], hx, sib)

    def mlp_back(gpair, wu, wd, u, gub, hp, hs, hx):
        rows = gpair[...].reshape(256, D)
        for j in range(2):
            gz = mm_nt(rows, wd[2 * j : 2 * j + 2].reshape(256, D))
            gub[j] = (gz * gelu_slope(u[j])).astype(BF)
        for t in range(4):
            cols = slice(256 * t, 256 * (t + 1))
            acc = jnp.zeros((256, 256), F32)
            for j in range(2):
                w = jnp.concatenate([wu[2 * j, cols, :], wu[2 * j + 1, cols, :]], axis=1)
                acc += mm_nt(gub[j], w)
            hp[:, :, cols] = acc.reshape(2, 128, 256)
        hs[...] = hp[k2].astype(BF)
        return put(hs, hx, sib)

    def up_partial(npair, gub):
        for j in range(2):
            for t in range(4):
                cols = slice(256 * t, 256 * (t + 1))
                g = mm_tn(npair[:, :, cols].reshape(256, 256), gub[j]).astype(BF)
                s.gsu[2 * j, cols, :] = g[:, :128]
                s.gsu[2 * j + 1, cols, :] = g[:, 128:]

    def up_fold():
        return fold(
            lambda d, h: s.gsu.at[chip[d], 512 * h : 512 * h + 512],
            lambda i, h: s.gru.at[i, 512 * h : 512 * h + 512],
        )

    def down_partial(zb, gpair):
        for j in range(2):
            for t in range(4):
                cols = slice(256 * t, 256 * (t + 1))
                g = mm_tn(zb[j], gpair[:, :, cols].reshape(256, 256)).astype(BF)
                s.gsd[2 * j : 2 * j + 2, :, :, cols] = g.reshape(2, 4, 32, 256)

    def down_fold():
        return fold(
            lambda d, h: s.gsd.at[2 * h : 2 * h + 2, chip[d]],
            lambda i, h: s.grd.at[i, 2 * h : 2 * h + 2],
        )

    def up_to_planes(up, zs, zr):
        arrived(up[3])
        total = s.gsu[p].astype(F32)
        for i in (1, 2):
            total += s.gru[i].astype(F32)
        zs[...] = total.astype(BF)
        return to_planes(
            lambda d: zs.at[pl.ds(pl.multiple_of(plane[d] * 256, 256), 256)], lambda d: zr.at[d - 1]
        )

    def down_to_planes(down, zs, zr):
        arrived(down[3])
        total = s.gsd[:, p].astype(F32)
        for i in (1, 2):
            total += s.grd[i].astype(F32)
        zs[...] = total.astype(BF)
        return to_planes(lambda d: zs.at[plane[d]], lambda d: zr.at[d - 1])

    def up_total(copies, zs, zr, ag):
        arrived(copies)
        total = zs[own_z, :].astype(F32)
        for i in range(3):
            total += zr[i].astype(F32)
        ag[c] = total.astype(BF)
        return gather(lambda i: ag.at[i], lambda i, h: ag.at[i, 128 * h : 128 * h + 128])

    def row_slot(ag):
        return lambda i: ag.at[lax.rem(i, 2), lax.div(i, 2)]

    def row_half(ag):
        return lambda i, h: ag.at[lax.rem(i, 2), lax.div(i, 2), 16 * h : 16 * h + 16]

    def down_total(copies, zs, zr, ag):
        arrived(copies)
        total = zs[z].astype(F32)
        for i in range(3):
            total += zr[i].astype(F32)
        ag[k, p] = total.astype(BF)
        return gather(row_slot(ag), row_half(ag))

    outs = []

    def out_cols(ag, w):
        for j in range(8):
            outs.append(fetch(ag.at[j], d_big.at[w, :, 128 * j : 128 * (j + 1)]))

    def out_rows(ag, w):
        for kk in range(2):
            for q in range(4):
                at = 128 * kk + 32 * q
                outs.append(fetch(ag.at[kk, q], d_big.at[w, at : at + 32, :]))

    x_n1 = mlp_start(s.h1, g_cmlp, s.n1)
    arrived(wu3_z)
    wu3_in = spread(lambda q, h: s.wu3.at[q, 512 * h : 512 * h + 512])
    all_of(wu1_in)
    x_n1.wait_recv()
    mlp_up(s.n1, s.wu1, s.u1, s.z1)
    all_of(wd1_in)
    x_h1 = mlp_down(s.z1, s.wd1, s.hpa, s.hxa)
    relay(wu3_in)
    arrived(qkv_z)
    x_qkv = put(s.wqkv.at[:, k], s.wqkv.at[:, k], sib)
    x_h1.wait_recv()
    s.h2[...] = s.h1[...] + s.hpa[k] + s.hxa[...]

    s.n2[p] = (norm_parts(s.h2[...])[0] * g_self[...]).astype(BF)
    n2_in = spread(lambda q, h: s.n2.at[q, 64 * h : 64 * h + 64])
    x_qkv.wait_recv()

    def project(q):
        rows = s.n2[q]
        for i in range(3):
            w = jnp.concatenate([s.wqkv[i, 0], s.wqkv[i, 1]], axis=1)
            s.pair[...] = mm(rows, w).astype(BF).reshape(128, 256)
            for h in range(2):
                s.heads[h, q, i] = s.pair[:, 128 * h : 128 * (h + 1)]
        s.mine[2 * q + k] = s.heads[k, q]
        return put(s.heads.at[k2, q], s.mine.at[2 * q + k], sib)

    qkv_in = [project(p)]
    relay(n2_in)
    for d in (1, 2):
        near(n2_in, d)
        qkv_in.append(project(chip[d]))
    far(n2_in)
    qkv_in.append(project(chip[3]))
    arrived(wo_z)
    piece = pl.ds(pl.multiple_of(32 * p, 32), 32)
    s.wo[k, piece, :] = s.woz[p]
    wo_in = to_peers(lambda d: s.woz.at[chip[d]], lambda d: s.wo.at[k, piece])
    arrived(qkv_in)

    def attend(b):
        rows = pl.ds(pl.multiple_of(b * 128, 128), 128)
        keys = s.mine[:, 1].reshape(D, 128)
        sc = mm_nt(s.mine[b, 0], keys) * SELF_SCALE
        at = s.pos[0:1, :]
        sc = jnp.where((at >= s.span[rows, 0:1]) & (at <= s.span[rows, 1:2]), sc, MASKED)
        e = jnp.exp(sc - jnp.max(sc, axis=1, keepdims=True))
        low = (e / jnp.sum(e, axis=1, keepdims=True)).astype(BF)
        s.a1[b] = low
        return mm(low, s.mine[:, 2].reshape(D, 128)).astype(BF)

    def other_rows(q, carry):
        s.send[q] = attend(2 * q + k2)
        return carry

    def own_parity(q, carry):
        s.aspar[q, k] = attend(2 * q + k)
        return carry

    lax.fori_loop(0, 4, other_rows, 0)
    x_as = put(s.send, s.aspar.at[:, k], sib)
    arrived(wo_in)
    x_wo = put(s.wo.at[k], s.wo.at[k], sib)
    lax.fori_loop(0, 4, own_parity, 0)
    x_wo.wait_recv()
    x_as.wait_recv()

    def both(ref, q):
        return jnp.concatenate([ref[q, 0], ref[q, 1]], axis=1)

    for d in (3, 1, 2):
        s.outp[d - 1] = mm(both(s.aspar, chip[d]), s.wo[...].reshape(256, D)).astype(BF)

    def rows_out(d, h):
        return s.outp.at[d - 1, 64 * h : 64 * h + 64]

    def rows_in(i, h):
        return s.outr.at[i, 64 * h : 64 * h + 64]

    out_in = fold(rows_out, rows_in)
    s.h3[...] = s.h2[...] + mm(both(s.aspar, p), s.wo[...].reshape(256, D))
    fold_on(out_in)
    arrived(out_in[3])
    s.h3[...] += s.outr[1].astype(F32) + s.outr[2].astype(F32)

    x_n3 = mlp_start(s.h3, g_smlp, s.n3)
    all_of(wu3_in)
    x_n3.wait_recv()
    mlp_up(s.n3, s.wu3, s.u3, s.z3)
    arrived(wd3_z)
    x_cot.wait_recv()
    sent([x_h1])
    x_d3 = mlp_back(s.cpair, s.wu3, s.wd3, s.u3, s.gu3, s.hpa, s.hs, s.hr)
    x_h3 = mlp_down(s.z3, s.wd3, s.hpb, s.hxb)
    x_d3.wait_recv()
    dx, gg_smlp = norm_back(s.hpa[k] + s.hr[...].astype(F32), s.h3[...], g_smlp[...])
    dh3 = cot[...].astype(F32) + dx
    s.dh[...] = dh3
    s.go[p] = dh3.astype(BF)
    go_in = spread(lambda q, h: s.go.at[q, 64 * h : 64 * h + 64])
    x_h3.wait_recv()
    layer_out[...] = (s.h3[...] + s.hpb[k] + s.hxb[...]).astype(BF)

    def pull_out(q):
        g = mm_nt(s.go[q], s.wo[...].reshape(256, D)).astype(BF)
        s.pair[...] = g
        for h in range(2):
            s.gheads[h, q] = s.pair[:, 128 * h : 128 * (h + 1)]
        s.gmine[2 * q + k] = s.gheads[k, q]
        return put(s.gheads.at[k2, q], s.gmine.at[2 * q + k], sib)

    gas_in = [pull_out(p)]
    relay(go_in)
    up_partial(s.n3, s.gu3)
    s.gsu_own[...] = s.gsu[:, own_z, :]
    g3u_z = to_planes(
        lambda d: s.gsu.at[:, pl.ds(pl.multiple_of(plane[d] * 256, 256), 256)], lambda d: s.zg.at[d - 1]
    )
    for d in (1, 2):
        near(go_in, d)
        gas_in.append(pull_out(chip[d]))
    far(go_in)
    gas_in.append(pull_out(chip[3]))
    down_partial(s.z3, s.cpair)
    g3d = down_fold()
    arrived(gas_in)

    def attend_back(b, carry):
        dps = mm_nt(s.gmine[b], s.mine[:, 2].reshape(D, 128))
        probs = s.a1[b].astype(F32)
        delta = jnp.sum(probs * dps, axis=1, keepdims=True) / jnp.sum(probs, axis=1, keepdims=True)
        dss = (probs * (dps - delta) * SELF_SCALE).astype(BF)
        s.a2[b] = dss
        s.heads[lax.div(b, 4), lax.rem(b, 4), 0] = mm(dss, s.mine[:, 1].reshape(D, 128)).astype(BF)
        return carry

    sent(qkv_in)
    lax.fori_loop(0, 8, attend_back, 0)
    fold_on(g3d)
    for t in range(4):
        cols = slice(256 * t, 256 * (t + 1))
        dk = mm_tn(s.a2[:, :, cols].reshape(D, 256), s.mine[:, 0].reshape(D, 128))
        dv = mm_tn(s.a1[:, :, cols].reshape(D, 256), s.gmine[...].reshape(D, 128))
        two = slice(2 * (t % 2), 2 * (t % 2) + 2)
        s.heads[t // 2, two, 1] = dk.astype(BF).reshape(2, 128, 128)
        s.heads[t // 2, two, 2] = dv.astype(BF).reshape(2, 128, 128)

    def sort(q, carry):
        high, low = lax.div(q, 2), 2 * lax.rem(q, 2)
        s.dsend[q] = s.heads[high, low + k2]
        for i in range(3):
            s.dpar[q, i, k] = s.heads[high, low + k, i]
        return carry

    lax.fori_loop(0, 4, sort, 0)
    x_dp = put(s.dsend, s.dpar.at[:, :, k], sib)
    g3d_z = down_to_planes(g3d, s.sd3, s.zd3)
    x_dp.wait_recv()

    def pull_in(q, write):
        for t in range(4):
            cols = slice(256 * t, 256 * (t + 1))
            acc = jnp.zeros((128, 256), F32)
            for i in range(3):
                w = jnp.concatenate([s.wqkv[i, 0, cols, :], s.wqkv[i, 1, cols, :]], axis=1)
                acc += mm_nt(jnp.concatenate([s.dpar[q, i, 0], s.dpar[q, i, 1]], axis=1), w)
            write(cols, acc)

    sent(out_in[2])
    sent(out_in[3])
    for d in (3, 1, 2):

        def write(cols, acc):
            s.outp[d - 1, :, cols] = acc.astype(BF)

        pull_in(chip[d], write)
    dn_in = fold(rows_out, rows_in)

    def write(cols, acc):
        s.hxb[:, cols] = acc

    pull_in(p, write)

    def project_grad(i):
        g = jnp.concatenate([s.dpar[:, i, 0].reshape(PARITY_ROWS, 128), s.dpar[:, i, 1].reshape(PARITY_ROWS, 128)], axis=1)
        for t in range(4):
            cols = slice(256 * t, 256 * (t + 1))
            w = mm_tn(s.n2[:, :, cols].reshape(PARITY_ROWS, 256), g).astype(BF)
            for h in range(2):
                s.pg[i, h, cols, :] = w[:, 128 * h : 128 * (h + 1)]
        return put(s.pg.at[i, k2], s.pgr.at[i], sib)

    def project_planes(i):
        x_pg[i].wait_recv()
        s.pg[i, k] = (s.pg[i, k].astype(F32) + s.pgr[i].astype(F32)).astype(BF)
        return to_planes(
            lambda d: s.pg.at[i, k, pl.ds(pl.multiple_of(plane[d] * 256, 256), 256)],
            lambda d: s.zq.at[d - 1, i],
        )

    x_pg = [project_grad(0)]
    fold_on(dn_in)
    x_pg.append(project_grad(1))
    pg_z = [project_planes(0)]
    x_pg.append(project_grad(2))
    pg_z.append(project_planes(1))
    g = jnp.concatenate([s.aspar[:, 0].reshape(PARITY_ROWS, 128), s.aspar[:, 1].reshape(PARITY_ROWS, 128)], axis=1)
    for t in range(4):
        cols = slice(256 * t, 256 * (t + 1))
        w = mm_tn(g, s.go[:, :, cols].reshape(PARITY_ROWS, 256)).astype(BF)
        s.pgo[:, :, cols] = w.reshape(2, 128, 256)
    x_pgo = put(s.pgo.at[k2], s.pgor, sib)
    arrived(dn_in[3])
    dn2 = s.hxb[...] + s.outr[1].astype(F32) + s.outr[2].astype(F32)
    dx, gg_self = norm_back(dn2, s.h2[...], g_self[...])
    s.dh[...] += dx

    s.gpair[k] = s.dh[...].astype(BF)
    x_g = put(s.gpair.at[k], s.gpair.at[k], sib)
    pg_z.append(project_planes(2))
    x_g.wait_recv()
    sent([x_d3])
    x_d1 = mlp_back(s.gpair, s.wu1, s.wd1, s.u1, s.gu1, s.hpa, s.hs, s.hr)
    x_pgo.wait_recv()
    s.pgo[k] = (s.pgo[k].astype(F32) + s.pgor[...].astype(F32)).astype(BF)
    s.wz[p] = s.pgo[k, piece, :]
    pgo_in = to_peers(
        lambda d: s.pgo.at[k, pl.ds(pl.multiple_of(32 * chip[d], 32), 32)], lambda d: s.wz.at[p]
    )
    sent(g3d[2])
    sent(g3d[3])
    down_partial(s.z1, s.gpair)
    g1d = down_fold()
    x_d1.wait_recv()
    dx, gg_cmlp = norm_back(s.hpa[k] + s.hr[...].astype(F32), s.h1[...], g_cmlp[...])
    dh1 = s.dh[...] + dx
    s.dh[...] = dh1

    go1 = dh1.astype(BF)
    gv = jnp.zeros((128, CP), F32)
    for j in range(4):
        w = jnp.concatenate([s.wvo[2 * j], s.wvo[2 * j + 1]], axis=1)
        gv += mm_nt(go1[:, 256 * j : 256 * (j + 1)], w)
    gv = gv.astype(BF).astype(F32)
    delta = jnp.sum(jnp.where(lane < 261, s.px[...] * gv, 0.0), axis=1, keepdims=True)
    s.gv[p] = tag(gv, lane, lse, delta)
    gv_in = spread(lambda q, h: s.gv.at[q, 64 * h : 64 * h + 64])
    arrived(pgo_in)
    pgo_z = to_planes(lambda d: s.wz.at[plane[d]], lambda d: s.zo.at[d - 1])
    fold_on(g1d)
    for j in range(4):
        f_part = mm_tn(s.pxl[...], go1[:, 256 * j : 256 * (j + 1)])[:CR].astype(BF)
        s.fst[j, 0] = f_part[:, :128]
        s.fst[j, 1] = f_part[:, 128:]
    sent(wvo_in[1])
    sent(wvo_s)
    x_f = put(s.fst.at[:, k2], s.fsr, sib)
    sent(g3u_z)
    up_partial(s.n1, s.gu1)
    g1u = up_fold()
    def cross_back(q):
        val, last, delta = untag(s.gv[q], lane)
        ratio = jnp.exp(s.tops[q][:, 0:1] - last)
        s.gvr[q] = (val * ratio).astype(BF)
        acc = jnp.zeros((128, CP), F32)
        for h in range(2):
            dp = mm(s.gv[q], s.xt[h])
            ds = (s.ee[2 * q + h].astype(F32) * ((dp - delta) * (ratio * CROSS_SCALE))).astype(BF)
            s.a2[2 * q + h] = ds
            acc += mm_nt(ds, s.xt[h])
        s.pxs[q] = acc.astype(BF)
        return acc

    sent(px_in)
    s.dqk[...] = cross_back(p)
    relay(gv_in)
    x_f.wait_recv()
    s.fst[:, k] = (s.fst[:, k].astype(F32) + s.fsr[...].astype(F32)).astype(BF)
    f_in = fold(
        lambda d, h: s.fst.at[chip[d], k, 144 * h : 144 * h + 144], lambda i, h: s.fpr.at[i, 144 * h : 144 * h + 144]
    )
    for d in (1, 2):
        near(gv_in, d)
        cross_back(chip[d])
    far(gv_in)
    cross_back(chip[3])
    g1d_z = down_to_planes(g1d, s.sd1, s.zd1)
    all_of(ln_in)
    for j in range(4):
        e = mm_tn(s.lnp[:, :, 256 * j : 256 * (j + 1)].reshape(PARITY_ROWS, 256), s.pxs[...].reshape(PARITY_ROWS, CP))
        s.est[j] = e.astype(BF).reshape(4, 2, 32, CP)
    x_e = put(s.est.at[:, :, k2], s.esr, sib)
    dq_in = fold(
        lambda d, h: s.pxs.at[chip[d], 64 * h : 64 * h + 64], lambda i, h: s.pxr.at[i, 64 * h : 64 * h + 64]
    )
    fold_on(f_in)
    for q in range(4):
        for j in range(3):
            cols = slice(128 * j, 128 * (j + 1))
            s.a1[j, :, 128 * q : 128 * (q + 1)] = s.qk[q, :, cols].T
            s.a1[j, :, 512 + 128 * q : 512 + 128 * (q + 1)] = s.gvr[q, :, cols].T

    def pixel_cols(h, t):
        cols = slice(256 * t, 256 * (t + 1))
        parts = [s.a2[2 * q + h, :, cols] for q in range(4)] + [s.ee[2 * q + h, :, cols] for q in range(4)]
        return mm(s.a1[0:3].reshape(CP, 1024), jnp.concatenate(parts, axis=0))

    for t in range(4):
        s.dxs[:, 256 * t : 256 * (t + 1)] = pixel_cols(k2, t)[:CX].astype(BF)
    x_dx = put(s.dxs, s.dxr, sib)
    x_e.wait_recv()
    s.est[:, :, k] = (s.est[:, :, k].astype(F32) + s.esr[...].astype(F32)).astype(BF)
    e_in = to_peers(lambda d: s.est.at[:, chip[d], k], lambda d: s.epr.at[d - 1])
    fold_on(dq_in)
    fold_on(g1u)
    arrived(dq_in[3])
    dqk = (s.dqk[...] + s.pxr[1].astype(F32) + s.pxr[2].astype(F32)).astype(BF)
    dx, gg_lat = norm_back(mm_nt(dqk, s.wqk[...].reshape(D, CP)), lat[...].astype(F32), g_lat[...])
    s.dh[...] += dx
    outs.append(fetch(s.dh, d_lat))
    arrived(e_in)
    total = s.est[:, p, k].astype(F32)
    for i in range(3):
        total += s.epr[i].astype(F32)
    s.ez[...] = total.astype(BF)
    e_z = to_planes(lambda d: s.ez.at[plane[d]], lambda d: s.ezr.at[d - 1])
    arrived(f_in[3])
    total = s.fst[p, k].astype(F32)
    for i in (1, 2):
        total += s.fpr[i].astype(F32)
    s.fz[0] = total.astype(BF)
    f_z = to_planes(lambda d: s.fz.at[0], lambda d: s.fz.at[d])
    g1u_z = up_to_planes(g1u, s.su1, s.zu1)
    arrived(g3u_z)
    s.zs[...] = (s.gsu_own[...].astype(F32) + sum(s.zg[i].astype(F32) for i in range(3))).astype(BF)
    g3u_in = to_peers(lambda d: s.zs.at[chip[d]], lambda d: s.zu3.at[d - 1])
    g3d_ag = down_total(g3d_z, s.sd3, s.zd3, s.agd3)

    x_dx.wait_recv()
    gg_in = jnp.zeros((261, 1), F32)
    for t in range(4):
        cols = slice(256 * t, 256 * (t + 1))
        dxn = (pixel_cols(k, t)[:CX] + s.dxr[:, cols].astype(F32))[:261]
        hat, r = norm_cols(pix[:, cols].astype(F32))
        dhat = dxn * s.gcol[0:261, 0:1]
        even = jnp.mean(dhat, axis=0, keepdims=True)
        tilt = jnp.mean(dhat * hat, axis=0, keepdims=True)
        d_pix[:, cols] = r * (dhat - even - hat * tilt)
        gg_in += jnp.sum(dxn * hat, axis=1, keepdims=True)
    s.gcol[0:261, :] = jnp.broadcast_to(gg_in, (261, 128))
    s.ga[k] = jnp.zeros((8, D), F32)
    s.ga[k, 0:1, 0:CP] = s.gcol[...].T[0:1, :]
    for i, gg in enumerate((gg_lat, gg_cmlp, gg_self, gg_smlp)):
        s.ga[k, i + 1 : i + 2, :] = gg
    x_ga = put(s.ga.at[k], s.ga.at[k], sib)

    arrived(e_z)
    total = s.ez[z].astype(F32)
    for i in range(3):
        total += s.ezr[i].astype(F32)
    s.eag[c] = total.astype(BF)
    e_s = to_plane(s.eag.at[c])
    x_ga.wait_recv()
    s.gb[p] = s.ga[0] + s.ga[1]
    gb_in = to_peers(lambda d: s.gb.at[p], lambda d: s.gb.at[p])
    relay(g3d_ag[1])
    arrived(g3u_in)
    s.agu3[c] = (s.zs[p].astype(F32) + sum(s.zu3[i].astype(F32) for i in range(3))).astype(BF)
    g3u_ag = gather(lambda i: s.agu3.at[i], lambda i, h: s.agu3.at[i, 128 * h : 128 * h + 128])
    for copies in pg_z:
        arrived(copies)
    for i in range(3):
        total = s.pg[i, k, own_z, :].astype(F32)
        for d in range(3):
            total += s.zq[d, i].astype(F32)
        s.agq[c, i] = total.astype(BF)
    q_ag = gather(lambda i: s.agq.at[i], lambda i, h: s.agq.at[i, :, 128 * h : 128 * h + 128])
    arrived(gb_in)
    s.gc[z] = s.gb[0] + s.gb[1] + s.gb[2] + s.gb[3]
    gc_in = to_planes(lambda d: s.gc.at[z], lambda d: s.gc.at[z])
    relay(g3u_ag[1])
    relay(q_ag[1])
    wo_ag = down_total(pgo_z, s.wz, s.zo, s.ago)
    g3d_s = pass_on(g3d_ag)
    arrived(f_z)
    s.wvo[c, 0:CR, :] = sum(s.fz[d].astype(F32) for d in range(4)).astype(BF)

    def f_slot(i):
        return s.wvo.at[i, 0:CR]

    f_ag = gather(f_slot, lambda i, h: s.wvo.at[i, 144 * h : 144 * h + 144])
    eighth = pl.ds(pl.multiple_of(c * 48, 16), 48)
    arrived(e_s)
    e_all = s.eag[...].reshape(256, CP)
    for j in range(4):
        s.gks[j] = mm_tn(e_all, s.wq_z[:, 256 * j : 256 * (j + 1)]).astype(BF)
    gk_z = to_planes(lambda d: s.gks.at[plane[d], eighth], lambda d: s.gkr.at[d - 1])
    sent([x_n3])
    for j in range(4):
        s.n3[:, :, 256 * j : 256 * (j + 1)] = mm(e_all, s.wk[j]).astype(BF).reshape(2, 128, 256)
    outs.extend(fetch(s.n3.at[i], d_big.at[8, 128 * i : 128 * (i + 1)]) for i in range(2))
    g3u_s = pass_on(g3u_ag)
    q_s = pass_on(q_ag)
    relay(wo_ag[1])
    g1d_ag = down_total(g1d_z, s.sd1, s.zd1, s.agd1)
    g1u_ag = up_total(g1u_z, s.su1, s.zu1, s.agu1)
    relay(f_ag[1])
    f_s = pass_on(f_ag)
    arrived(gk_z)
    total = s.gks[z, eighth, :].astype(F32)
    for i in range(3):
        total += s.gkr[i].astype(F32)
    s.gkh[eighth, :] = total.astype(BF)
    x_gk = to_plane(s.gkh.at[eighth])
    relay(g1d_ag[1])
    relay(g1u_ag[1])
    wo_s_ = pass_on(wo_ag)
    arrived(g3d_s)
    out_rows(s.agd3, 7)
    arrived(g3u_s)
    out_cols(s.agu3, 6)
    arrived(f_s)
    sent([x_n1])
    acc = jnp.zeros((CP, 256), F32)
    for j in range(4):
        f_two = jnp.concatenate([s.wvo[2 * j], s.wvo[2 * j + 1]], axis=1)
        acc += mm_nt(f_two, s.wo_z[:, 256 * j : 256 * (j + 1)])
        s.n1[:, :, 256 * j : 256 * (j + 1)] = mm_tn(s.wv_z[...], f_two).astype(BF).reshape(2, 128, 256)
    d_wv[...] = acc[:261]
    outs.extend(fetch(s.n1.at[i], d_big.at[9, 128 * i : 128 * (i + 1)]) for i in range(2))
    g1d_s = pass_on(g1d_ag)
    g1u_s = pass_on(g1u_ag)
    arrived(q_s)
    for i in range(3):
        for j in range(8):
            outs.append(fetch(s.agq.at[j, i], d_big.at[2 + i, :, 128 * j : 128 * (j + 1)]))
    arrived(wo_s_)
    out_rows(s.ago, 5)
    arrived(gc_in)
    d_gain[...] = s.gc[0] + s.gc[1] + s.gc[2] + s.gc[3]
    arrived(x_gk)
    d_wk[...] = s.gkh[...].astype(F32)[0:261]
    arrived(g1d_s)
    out_rows(s.agd1, 1)
    arrived(g1u_s)
    out_cols(s.agu1, 0)
    for copy in outs:
        copy.wait()
    for when, copy in sends:
        if when is None:
            copy.wait_send()
        else:
            pl.when(when)(copy.wait_send)


def norm_cols(x):
    center = x - jnp.mean(x, axis=0, keepdims=True)
    r = lax.rsqrt(jnp.mean(center * center, axis=0, keepdims=True) + 1e-05)
    return center * r, r


def tag(val, lane, one, two):
    for i, x in enumerate((one, two)):
        for j in range(3):
            part = x.astype(BF).astype(F32)
            val = jnp.where(lane == 261 + 3 * i + j, part, val)
            x = x - part
    return val.astype(BF)


def untag(low, lane):
    val = low.astype(F32)

    def column(i):
        here = (lane >= 261 + 3 * i) & (lane < 264 + 3 * i)
        return jnp.sum(jnp.where(here, val, 0.0), axis=1, keepdims=True)

    return jnp.where(lane < 261, val, 0.0), column(0), column(1)


SCRATCH = {
    "ssem": 400, "rsem": 400, "lsem": 96,

    "wk": ((4, CP, 256), BF), "wqk": ((4, 2, 128, CP), BF), "wq_z": ((256, 1024), BF), "wo_z": ((256, 1024), BF),
    "wv_z": ((CP, 256), BF), "wvz": ((4, CR, 128), BF), "wvo": ((8, CP, 128), BF),
    "wu1": ((4, 1024, 128), BF), "wu3": ((4, 1024, 128), BF), "wd1": ((4, 4, 32, 1024), BF), "wd3": ((4, 4, 32, 1024), BF),
    "wqkv": ((3, 2, 1024, 128), BF), "wo": ((2, 128, 1024), BF),
    "xt": ((2, CP, 1024), BF), "span": ((1024, 128), jnp.int32), "pos": ((8, 1024), jnp.int32), "row": ((8, CP), F32), "gcol": ((CP, 128), F32), "lnp": ((4, 128, 1024), BF), "qk": ((4, 128, CP), BF),
    "pxs": ((4, 128, CP), BF), "pxr": ((3, 128, CP), BF), "px": ((128, CP), F32), "pxl": ((128, CP), BF),
    "cpair": ((2, 128, 1024), BF), "n1": ((2, 128, 1024), BF), "n3": ((2, 128, 1024), BF),
    "u1": ((2, 256, 256), F32), "u3": ((2, 256, 256), F32), "z1": ((2, 256, 256), BF), "z3": ((2, 256, 256), BF),
    "gu1": ((2, 256, 256), BF), "gu3": ((2, 256, 256), BF),


    "h1": ((128, 1024), F32), "h2": ((128, 1024), F32), "h3": ((128, 1024), F32), "dh": ((128, 1024), F32),
    "n2": ((4, 128, 1024), BF), "go": ((4, 128, 1024), BF), "pair": ((128, 256), BF),
    "heads": ((2, 4, 3, 128, 128), BF), "mine": ((8, 3, 128, 128), BF),
    "a1": ((8, 128, 1024), BF), "a2": ((8, 128, 1024), BF), "send": ((4, 128, 128), BF), "aspar": ((4, 2, 128, 128), BF),
    "outp": ((3, 128, 1024), BF), "outr": ((3, 128, 1024), BF),
    "gheads": ((2, 4, 128, 128), BF), "gmine": ((8, 128, 128), BF),
    "dsend": ((4, 3, 128, 128), BF), "dpar": ((4, 3, 2, 128, 128), BF),


    "zu1": ((3, 256, 128), BF), "zu3": ((3, 256, 128), BF), "zd1": ((3, 32, 1024), BF), "zd3": ((3, 32, 1024), BF),
    "agu1": ((8, 256, 128), BF), "agu3": ((8, 256, 128), BF), "agd1": ((2, 4, 32, 1024), BF), "agd3": ((2, 4, 32, 1024), BF),
    "pg": ((3, 2, 1024, 128), BF), "pgr": ((3, 1024, 128), BF), "zq": ((3, 3, 256, 128), BF), "agq": ((8, 3, 256, 128), BF),
    "pgo": ((2, 128, 1024), BF), "pgor": ((128, 1024), BF), "zo": ((3, 32, 1024), BF), "ago": ((2, 4, 32, 1024), BF), "woz": ((4, 32, 1024), BF), "wz": ((4, 32, 1024), BF),
    "gv": ((4, 128, CP), BF), "dqk": ((128, CP), F32),
    "dxs": ((CX, 1024), BF), "dxr": ((CX, 1024), BF),
    "fst": ((4, 2, CR, 128), BF), "fsr": ((4, CR, 128), BF), "fpr": ((3, CR, 128), BF), "fz": ((4, CR, 128), BF),
    "est": ((4, 4, 2, 32, CP), BF), "esr": ((4, 4, 32, CP), BF), "epr": ((3, 4, 32, CP), BF), "ez": ((4, 32, CP), BF),
    "ezr": ((3, 32, CP), BF), "eag": ((8, 32, CP), BF),
    "gks": ((4, CP, 256), BF), "gkr": ((3, 48, 256), BF), "gkh": ((CP, 256), BF), "gpair": ((2, 128, 1024), BF), "zg": ((3, 4, 256, 128), BF), "zs": ((4, 256, 128), BF), "gsu_own": ((4, 256, 128), BF), "hs": ((128, 1024), BF), "hr": ((128, 1024), BF),
    "ga": ((2, 8, 1024), F32), "gb": ((4, 8, 1024), F32), "gc": ((4, 8, 1024), F32),
    "hpa": ((2, 128, 1024), F32), "hpb": ((2, 128, 1024), F32), "hxa": ((128, 1024), F32), "hxb": ((128, 1024), F32),
    "ee": ((8, 128, 1024), BF), "tops": ((4, 128, 128), F32), "gvr": ((4, 128, CP), BF),
    "gsu": ((4, 1024, 128), BF), "gsd": ((4, 4, 32, 1024), BF), "gru": ((3, 1024, 128), BF), "grd": ((3, 4, 32, 1024), BF),
    "su1": ((1024, 128), BF), "sd1": ((4, 32, 1024), BF), "sd3": ((4, 32, 1024), BF),
}


def unpack(layer_in, lat_in, big_in, wk_in, wv_in, gain_in, pix_in, layer_out, d_lat, *rest):
    big = rest[:10]
    wk_out, wv_out, gains, first, pix_out = rest[10], rest[11], rest[12:16], rest[16], rest[17]
    low, wide, pix_rows, sem_in, sem_out = rest[18:]
    loads = [pltpu.make_async_copy(big_in.at[i], low.at[i], sem_in.at[i]) for i in range(10)]
    for copy in loads:
        copy.start()
    pairs = ((layer_in, layer_out), (lat_in, d_lat), (wk_in, wk_out), (wv_in, wv_out))
    stores = [pltpu.make_async_copy(a, b, sem_out.at[i]) for i, (a, b) in enumerate(pairs)]
    for copy in stores:
        copy.start()
    for i in range(10):
        loads[i].wait()
        wide[i] = low[i].astype(F32)
        stores.append(pltpu.make_async_copy(wide.at[i], big[i], sem_out.at[4 + i]))
        stores[-1].start()
    pix_rows[...] = pix_in[...].reshape(261, 1, 1024)
    stores.append(pltpu.make_async_copy(pix_rows, pix_out, sem_out.at[18]))
    stores[-1].start()
    first[...] = gain_in[0:1, 0:261].reshape(261)
    for i in range(4):
        stores.append(pltpu.make_async_copy(gain_in.at[i + 1 : i + 2], gains[i], sem_out.at[14 + i]))
        stores[-1].start()
    for copy in stores:
        copy.wait()


def one_kernel(
    pixels, latents, cotangent, doc_lengths, latent_offsets, block_deal,
    wq_c, wk_c, wv_c, wo_c, wu_c, wd_c, wq_s, wk_s, wv_s, wo_s, wu_s, wd_s,
    g_in, g_lat, g_cmlp, g_self, g_smlp,
):
    vmem, hbm = pl.BlockSpec(memory_space=pltpu.VMEM), pl.BlockSpec(memory_space=pl.ANY)
    smem = pl.BlockSpec(memory_space=pltpu.SMEM)

    def shape(dims, kind=F32):
        return jax.ShapeDtypeStruct(dims, kind)

    layer_out, d_pix, d_lat, big, d_wk, d_wv, gains = pl.pallas_call(
        fused,
        out_shape=(
            shape((128, D), BF), shape((261, 1024)), shape((128, D)), shape((10, 256, D), BF),
            shape((261, 256)), shape((261, 256)), shape((8, D)),
        ),
        in_specs=[vmem, vmem, vmem, smem, vmem, smem] + [vmem] * 5 + [hbm] * 12,
        out_specs=(vmem, vmem, hbm, hbm, vmem, vmem, vmem),
        scratch_shapes=[
            pltpu.SemaphoreType.DMA((what,)) if isinstance(what, int) else pltpu.VMEM(*what)
            for what in SCRATCH.values()
        ],
        compiler_params=pltpu.CompilerParams(
            collective_id=0, has_side_effects=True, vmem_limit_bytes=VMEM_BYTES
        ),
        cost_estimate=pl.CostEstimate(flops=26 * 10**9, bytes_accessed=40 * 10**6, transcendentals=10**7),
    )(
        pixels[0].T, latents[0], cotangent[0], doc_lengths, latent_offsets, block_deal,
        g_in, g_lat[None], g_cmlp[None], g_self[None], g_smlp[None],
        wq_c, wk_c, wv_c, wo_c, wu_c, wd_c, wq_s, wk_s, wv_s, wo_s, wu_s, wd_s,
    )
    outs = pl.pallas_call(
        unpack,
        out_shape=(
            shape((128, D), BF), shape((128, D)), *[shape((256, D))] * 10, *[shape((261, 256))] * 2, *[shape((1, D))] * 4,
            shape((261,)), shape((261, 1, 1024)),
        ),
        in_specs=[vmem, vmem, hbm, vmem, vmem, vmem, vmem],
        out_specs=(*[hbm] * 18, vmem, hbm),
        scratch_shapes=[
            pltpu.VMEM((10, 256, D), BF), pltpu.VMEM((10, 256, D), F32), pltpu.VMEM((261, 1, 1024), F32),
            pltpu.SemaphoreType.DMA((10,)), pltpu.SemaphoreType.DMA((19,)),
        ],
        compiler_params=pltpu.CompilerParams(vmem_limit_bytes=VMEM_BYTES),
        cost_estimate=pl.CostEstimate(flops=0, bytes_accessed=18 * 10**6, transcendentals=0),
    )(layer_out, d_lat, big, d_wk, d_wv, gains, d_pix)
    layer_out, d_lat, d_big, d_wk, d_wv, d_gain = outs[0], outs[1], outs[2:12], outs[12], outs[13], outs[14:18]
    return (
        layer_out[None], outs[19].transpose(1, 2, 0), d_lat[None], d_big[8], d_wk, d_wv, d_big[9], *d_big[:8],
        outs[18], *(g[0] for g in d_gain),
    )


VMEM_BYTES = 65472 * 2**10


def solution(mesh):
    rows, row, col, all_ = P("fsdp", "ctx", None), P("fsdp", None), P(None, "fsdp"), P()
    weights = (row, col, col, *(row,) * 9)
    small = mesh.shape["ctx"] == 8 and mesh.shape["fsdp"] == 4
    return jax.shard_map(
        one_kernel if small else plain,
        mesh=mesh,
        in_specs=(rows, rows, rows, row, row, all_, *weights, *(all_,) * 5),
        out_specs=(rows, rows, rows, *weights, *(all_,) * 5),
        check_vma=False,
    )
```

```python
import math
import types

import jax
import jax.numpy as jnp
from jax import lax
from jax.experimental import pallas as pl
from jax.experimental.pallas import tpu as pltpu
from jax.sharding import PartitionSpec as P

D = 1024
HEADS = 8
HEAD = D // HEADS
STRIDE = 8
LBLK = 64
BF = jnp.bfloat16
F32 = jnp.float32
CROSS_SCALE = 1.0 / math.sqrt(D)
SELF_SCALE = 1.0 / math.sqrt(HEAD)
MASKED = -1e30
GELU_K = math.sqrt(2.0 / math.pi)
GELU_A = 0.044715


def mm(a, b):
    return jnp.dot(a, b, preferred_element_type=F32)


def mm_nt(a, b):
    return lax.dot_general(a, b, (((1,), (1,)), ((), ())), preferred_element_type=F32)


def mm_tn(a, b):
    return lax.dot_general(a, b, (((0,), (0,)), ((), ())), preferred_element_type=F32)


def norm_parts(x):
    center = x - jnp.mean(x, axis=-1, keepdims=True)
    r = lax.rsqrt(jnp.mean(center * center, axis=-1, keepdims=True) + 1e-05)
    return center * r, r


def norm_back(dy, x, gain):
    hat, r = norm_parts(x)
    dhat = dy * gain
    dx = r * (
        dhat
        - jnp.mean(dhat, axis=-1, keepdims=True)
        - hat * jnp.mean(dhat * hat, axis=-1, keepdims=True)
    )
    return dx, jnp.sum(dy * hat, axis=0, keepdims=True)


def gelu(u):
    return 0.5 * u * (1.0 + jnp.tanh(GELU_K * (u + GELU_A * u * u * u)))


def gelu_slope(u):
    t = jnp.tanh(GELU_K * (u + GELU_A * u * u * u))
    return 0.5 * (1.0 + t) + 0.5 * u * (1.0 - t * t) * GELU_K * (1.0 + 3.0 * GELU_A * u * u)


def intervals(lengths, offsets, deal):
    count = lengths.shape[0]
    before = jnp.arange(count)[:, None] > jnp.arange(count)[None, :]
    starts = jnp.sum(jnp.where(before, lengths[None, :], 0), axis=1)
    base = (deal[:, None] * LBLK + jnp.arange(LBLK, dtype=jnp.int32)[None, :]).reshape(-1)
    pos = base * STRIDE + offsets
    lo = jnp.max(jnp.where(starts[None, :] <= pos[:, None], starts[None, :], -1), axis=1)
    return lo, pos


def plain(
    pixels, latents, cotangent, doc_lengths, latent_offsets, block_deal,
    wq_c, wk_c, wv_c, wo_c, wu_c, wd_c, wq_s, wk_s, wv_s, wo_s, wu_s, wd_s,
    g_in, g_lat, g_cmlp, g_self, g_smlp,
):
    n = lax.axis_size("ctx")
    me = lax.axis_index("ctx")
    rows = latents.shape[1]
    npix = pixels.shape[1]
    c = pixels.shape[2]
    lo, pos = intervals(doc_lengths[0], latent_offsets[0], block_deal)
    own_lo = lax.dynamic_slice_in_dim(lo, me * rows, rows)
    own_pos = lax.dynamic_slice_in_dim(pos, me * rows, rows)
    pix_pos = me * npix + jnp.arange(npix, dtype=jnp.int32)
    mask = (lo[:, None] <= pix_pos[None, :]) & (pix_pos[None, :] <= pos[:, None])
    smask = (own_lo[:, None] <= pos[None, :]) & (pos[None, :] <= own_pos[:, None])

    wq_c, wk_c, wv_c, wo_c = (w.astype(BF) for w in (wq_c, wk_c, wv_c, wo_c))
    wk_all = lax.all_gather(wk_c, "fsdp", axis=1, tiled=True)
    wqk = lax.all_gather(mm_nt(wq_c, wk_all).astype(BF), "fsdp", axis=0, tiled=True)
    wvo = lax.psum(mm(wv_c, wo_c), "fsdp").astype(BF)
    big = jnp.stack([w.astype(BF) for w in (wu_c, wd_c, wq_s, wk_s, wv_s, wo_s, wu_s, wd_s)])
    wu1, wd1, wq, wk, wv, wo, wu3, wd3 = lax.all_gather(big, "fsdp", axis=1, tiled=True)

    xin = pixels[0].astype(F32)
    xn = (norm_parts(xin)[0] * g_in).astype(BF)
    lat = latents[0].astype(F32)
    ln = (norm_parts(lat)[0] * g_lat).astype(BF)
    qk_all = lax.all_gather(mm(ln, wqk).astype(BF), "ctx", axis=0, tiled=True)
    s = jnp.where(mask, mm_nt(qk_all, xn) * CROSS_SCALE, MASKED)
    top = jnp.max(s, axis=1, keepdims=True)
    e = lax.optimization_barrier(jnp.where(mask, jnp.exp(s - top), 0.0).astype(BF))
    total = jnp.sum(e.astype(F32), axis=1, keepdims=True)
    part = jnp.concatenate([mm(e, xn), top, total], axis=1)
    parts = lax.all_to_all(part.reshape(n, rows, c + 2), "ctx", 0, 0)
    tops = parts[:, :, c : c + 1]
    high = jnp.max(tops, axis=0)
    share = jnp.exp(tops - high[None])
    full = jnp.sum(share * parts[:, :, c + 1 :], axis=0)
    px = jnp.sum(share * parts[:, :, :c], axis=0) / full
    lse = high + jnp.log(full)
    px_low = px.astype(BF)
    h1 = lat + mm(px_low, wvo)
    n1 = (norm_parts(h1)[0] * g_cmlp).astype(BF)
    u1 = mm(n1, wu1)
    z1 = gelu(u1).astype(BF)
    h2 = h1 + mm(z1, wd1)
    n2 = (norm_parts(h2)[0] * g_self).astype(BF)
    q = mm(n2, wq).astype(BF).reshape(rows, HEADS, HEAD)
    kv = jnp.concatenate([mm(n2, wk), mm(n2, wv)], axis=1).astype(BF)
    kv = lax.all_gather(kv, "ctx", axis=0, tiled=True)
    k = kv[:, :D].reshape(n * rows, HEADS, HEAD)
    v = kv[:, D:].reshape(n * rows, HEADS, HEAD)
    ss = jnp.einsum("qhd,khd->hqk", q, k, preferred_element_type=F32) * SELF_SCALE
    ss = jnp.where(smask[None], ss, MASKED)
    se = jnp.exp(ss - jnp.max(ss, axis=-1, keepdims=True))
    ps = se / jnp.sum(se, axis=-1, keepdims=True)
    psl = ps.astype(BF)
    sa = jnp.einsum("hqk,khd->qhd", psl, v, preferred_element_type=F32)
    sa = sa.reshape(rows, D).astype(BF)
    h3 = h2 + mm(sa, wo)
    n3 = (norm_parts(h3)[0] * g_smlp).astype(BF)
    u3 = mm(n3, wu3)
    z3 = gelu(u3).astype(BF)
    layer_out = (h3 + mm(z3, wd3)).astype(BF)

    gy3 = cotangent[0]
    gu3 = (mm_nt(gy3, wd3) * gelu_slope(u3)).astype(BF)
    dx, gg_smlp = norm_back(mm_nt(gu3, wu3), h3, g_smlp)
    dh3 = gy3.astype(F32) + dx
    go3 = dh3.astype(BF)
    gas = mm_nt(go3, wo).astype(BF).reshape(rows, HEADS, HEAD)
    dps = jnp.einsum("qhd,khd->hqk", gas, v, preferred_element_type=F32)
    sdelta = jnp.sum(ps * dps, axis=-1, keepdims=True)
    dss = (ps * (dps - sdelta) * SELF_SCALE).astype(BF)
    dqs = jnp.einsum("hqk,khd->qhd", dss, k, preferred_element_type=F32)
    dqs = dqs.reshape(rows, D).astype(BF)
    dks = jnp.einsum("hqk,qhd->khd", dss, q, preferred_element_type=F32).reshape(n * rows, D)
    dvs = jnp.einsum("hqk,qhd->khd", psl, gas, preferred_element_type=F32).reshape(n * rows, D)
    dkv = lax.psum_scatter(
        jnp.concatenate([dks, dvs], axis=1), "ctx", scatter_dimension=0, tiled=True
    ).astype(BF)
    dks, dvs = dkv[:, :D], dkv[:, D:]
    dn2 = mm_nt(dqs, wq) + mm_nt(dks, wk) + mm_nt(dvs, wv)
    dx, gg_self = norm_back(dn2, h2, g_self)
    dh2 = dh3 + dx
    gy1 = dh2.astype(BF)
    gu1 = (mm_nt(gy1, wd1) * gelu_slope(u1)).astype(BF)
    dx, gg_cmlp = norm_back(mm_nt(gu1, wu1), h1, g_cmlp)
    dh1 = dh2 + dx
    go1 = dh1.astype(BF)
    gv = lax.optimization_barrier(mm_nt(go1, wvo).astype(BF))
    delta = jnp.sum(px * gv.astype(F32), axis=1, keepdims=True)
    gv_all = lax.all_gather(gv, "ctx", axis=0, tiled=True)
    stat = lax.all_gather(jnp.concatenate([lse, delta], axis=1), "ctx", axis=0, tiled=True)
    p = jnp.where(mask, jnp.exp(s - stat[:, :1]), 0.0)
    ds = (p * (mm_nt(gv_all, xn) - stat[:, 1:]) * CROSS_SCALE).astype(BF)
    dxn = mm_tn(ds, qk_all) + mm_tn(p.astype(BF), gv_all)
    dpix, gg_in = norm_back(dxn, xin, g_in)
    dqk = lax.psum_scatter(mm(ds, xn), "ctx", scatter_dimension=0, tiled=True).astype(BF)
    dx, gg_lat = norm_back(mm_nt(dqk, wqk), lat, g_lat)
    dlat = dh1 + dx

    e_sum = lax.psum_scatter(mm_tn(ln, dqk), "fsdp", scatter_dimension=0, tiled=True)
    e_sum, f_sum = lax.psum((e_sum, lax.psum(mm_tn(px_low, go1), "fsdp")), "ctx")
    e_sum, f_sum = e_sum.astype(BF), f_sum.astype(BF)
    d_wq_c = mm(e_sum, wk_all)
    d_wk_c = lax.psum_scatter(mm_tn(e_sum, wq_c), "fsdp", scatter_dimension=1, tiled=True)
    d_wv_c = mm_nt(f_sum, wo_c)
    d_wo_c = mm_tn(wv_c, f_sum)
    pairs = ((n1, gu1), (z1, gy1), (n2, dqs), (n2, dks), (n2, dvs), (sa, go3), (n3, gu3), (z3, gy3))
    d_big = [
        lax.psum(lax.psum_scatter(mm_tn(a, b), "fsdp", scatter_dimension=0, tiled=True), "ctx")
        for a, b in pairs
    ]
    gains = lax.psum(jnp.concatenate([gg_in[0], gg_lat[0], gg_cmlp[0], gg_self[0], gg_smlp[0]]), ("ctx", "fsdp"))
    return (
        layer_out[None], dpix[None], dlat[None], d_wq_c, d_wk_c, d_wv_c, d_wo_c, *d_big,
        gains[:c], gains[c : c + D], gains[c + D : c + 2 * D],
        gains[c + 2 * D : c + 3 * D], gains[c + 3 * D :],
    )


CP = 384
CR = 288
CX = 272
PARITY_ROWS = 4 * 128


def fused(
    pix, lat, cot, lengths, offsets, deal, g_in, g_lat, g_cmlp, g_self, g_smlp,
    wq_c, wk_c, wv_c, wo_c, wu_1, wd_1, wq_s, wk_s, wv_s, wo_s, wu_3, wd_3,
    layer_out, d_pix, d_lat, d_big, d_wk, d_wv, d_gain,
    *scratch,
):
    s = types.SimpleNamespace(**dict(zip(SCRATCH, scratch)))
    c, z = lax.axis_index("ctx"), lax.axis_index("fsdp")
    k, p = lax.rem(c, 2), lax.div(c, 2)
    k2 = 1 - k

    def flip(v, d):
        low, high = lax.rem(v, 2), lax.div(v, 2)
        return (1 - low if d & 1 else low) + 2 * (1 - high if d & 2 else high)

    chip = {d: flip(p, d) for d in (1, 2, 3)}
    plane = {d: flip(z, d) for d in (1, 2, 3)}
    sib = {"ctx": 2 * p + k2}

    def peer(d):
        return {"ctx": 2 * chip[d] + k}

    def across(d):
        return {"ctx": 2 * chip[d] + k2}

    def level(d):
        return {"fsdp": plane[d]}

    used = [0, 0]
    sends = []

    def make(src, dst, target, slot=None):
        if slot is None:
            slot = used[0]
            used[0] += 1
        send = used[1]
        used[1] += 1
        return pltpu.make_async_remote_copy(
            src_ref=src, dst_ref=dst, send_sem=s.ssem.at[send], recv_sem=s.rsem.at[slot],
            device_id=target, device_id_type=pl.DeviceIdType.MESH,
        )

    def put(src, dst, target):
        copy = make(src, dst, target)
        copy.start()
        sends.append((None, copy))
        return copy

    def sent(copies):
        for copy in copies.values() if isinstance(copies, dict) else copies:
            copy.wait_send()
            sends[:] = [pair for pair in sends if pair[1] is not copy]

    def to_peers(src_of, dst_of, order=(3, 1, 2)):
        return {d: put(src_of(d), dst_of(d), peer(d)) for d in order}

    def to_planes(src_of, dst_of):
        return {d: put(src_of(d), dst_of(d), level(d)) for d in (1, 2, 3)}

    def arrived(copies):
        for copy in copies.values() if isinstance(copies, dict) else copies:
            copy.wait_recv()

    locals_ = [0]

    def fetch(src, dst):
        copy = pltpu.make_async_copy(src, dst, s.lsem.at[locals_[0]])
        locals_[0] += 1
        copy.start()
        return copy

    def spread(part_of):
        mine = [part_of(p, h) for h in range(2)]
        copies = {(d, h): put(mine[h], mine[h], peer(d)) for d, h in ((1, 0), (2, 1), (1, 1), (2, 0))}
        return part_of, copies, []

    def relay(state):
        part_of, copies, on = state
        for d, h in ((1, 0), (2, 1)):
            copies[d, h].wait_recv()
            part = part_of(chip[d], h)
            on.append(put(part, part, peer(3 - d)))

    def near(state, d):
        state[1][d, 2 - d].wait_recv()

    def far(state):
        arrived(state[2])

    def all_of(state):
        near(state, 1)
        near(state, 2)
        far(state)

    def fold(part_of, into):
        first = [put(part_of(3, h), into(0, h), peer(1 + h)) for h in range(2)]
        near_ = [put(part_of(1 + h, h), into(1, h), peer(1 + h)) for h in range(2)]
        return part_of, into, first, near_

    def fold_on(state):
        part_of, into, first, near_ = state
        for h in range(2):
            first[h].wait_recv()
            part = part_of(2 - h, h)
            part[...] = (part[...].astype(F32) + into(0, h)[...].astype(F32)).astype(BF)
            near_.append(put(part, into(2, h), peer(2 - h)))

    def gather(slot_of, half_of=None):
        own = put(slot_of(c), slot_of(c), sib)
        if half_of is None:
            return slot_of, to_peers(lambda d: slot_of(c), lambda d: slot_of(c)), [own]
        return slot_of, spread(lambda q, h: half_of(2 * q + k, h)), [own]

    def pass_on(state):
        slot_of, copies, to_sib = state
        if not isinstance(copies, dict):
            all_of(copies)
        for d in (1, 2, 3):
            if isinstance(copies, dict):
                copies[d].wait_recv()
            there = slot_of(2 * chip[d] + k)
            to_sib.append(put(there, there, sib))
        return to_sib

    def to_plane(part):
        return [put(part, part, to) for to in (*(peer(d) for d in (1, 2, 3)), *(across(d) for d in (1, 2, 3)), sib)]

    for j in range(4):
        s.wk[j, 256:CP, :] = jnp.zeros((CP - 256, 256), BF)
    s.wv_z[256:CP, :] = jnp.zeros((CP - 256, 256), BF)
    for j in range(2):
        s.xt[j, 256:CP, :] = jnp.zeros((CP - 256, 1024), BF)
    for j in range(8):
        s.wvo[j, CR:CP, :] = jnp.zeros((CP - CR, 128), BF)
    barrier = pltpu.get_barrier_semaphore()
    near_by = (sib, *(across(d) for d in (1, 2, 3)), *(peer(d) for d in (1, 2, 3)))
    for target in (*near_by, *(level(d) for d in (1, 2, 3))):
        pl.semaphore_signal(barrier, inc=1, device_id=target, device_id_type=pl.DeviceIdType.MESH)
    lanes = pl.ds(pl.multiple_of(c * 128, 128), 128)
    quarter = pl.ds(pl.multiple_of(k * 128 + p * 32, 32), 32)
    f_wk = [fetch(wk_c.at[0:256], s.u1.at[0]), fetch(wk_c.at[256:261], s.u1.at[1, 0:5])]
    f_wq = [fetch(wq_c.at[128 * i : 128 * (i + 1)], s.hpa.at[i]) for i in range(2)]
    f_wv = [fetch(wv_c.at[0:256], s.u3.at[0]), fetch(wv_c.at[256:261], s.u3.at[1, 0:5])]
    f_wo = [fetch(wo_c.at[128 * i : 128 * (i + 1)], s.hpb.at[i]) for i in range(2)]

    def early(i):
        return (s.dh if i < 8 else s.hxb).at[:, 128 * (i % 8) : 128 * (i % 8) + 128]

    f_u = [
        fetch(w.at[128 * j : 128 * (j + 1), lanes], early(2 * i + j))
        for i, w in enumerate((wu_1, wu_3, wq_s, wk_s, wv_s))
        for j in range(2)
    ]
    f_d = [fetch(w.at[quarter, :], s.h3.at[32 * i : 32 * (i + 1)]) for i, w in enumerate((wd_1, wo_s))]
    f_d3 = fetch(wd_3.at[pl.ds(pl.multiple_of(k * 128, 128), 128), :], s.hxa)
    pl.semaphore_wait(barrier, 10)

    for copy in f_wk:
        copy.wait()
    s.wk[z, 0:256, :] = s.u1[0].astype(BF)
    s.wk[z, 256:261, :] = s.u1[1, 0:5, :].astype(BF)
    half = pl.ds(pl.multiple_of(k * 144, 16), 144)
    wk_z = to_planes(lambda d: s.wk.at[z, half], lambda d: s.wk.at[z, half])
    for copy in f_u:
        copy.wait()
    own_z = pl.ds(pl.multiple_of(z * 256, 256), 256)
    for j in range(2):
        half_z = pl.ds(pl.multiple_of(z * 256 + 128 * j, 128), 128)
        s.wu1[p, half_z, :] = early(j)[...].astype(BF)
    wu1_z = to_planes(lambda d: s.wu1.at[p, own_z], lambda d: s.wu1.at[p, own_z])
    s.cpair[k] = cot[...]
    x_cot = put(s.cpair.at[k], s.cpair.at[k], sib)

    order = lax.broadcasted_iota(jnp.int32, (8, D), 1)
    block = lax.div(order, LBLK)
    base = jnp.zeros((8, D), jnp.int32)
    for i in range(D // LBLK):
        base = jnp.where(block == i, deal[i], base)
    pos_r = (base * LBLK + lax.rem(order, LBLK)) * STRIDE + offsets[...]
    lo_r = jnp.zeros((8, D), jnp.int32)
    start = lengths[0, 0]
    for i in range(1, lengths.shape[1]):
        lo_r = jnp.where(start <= pos_r, start, lo_r)
        start = start + lengths[0, i]
    s.pos[...] = pos_r
    top_row = lax.broadcasted_iota(jnp.int32, (128, 128), 0) == 0
    for b in range(8):
        cols = slice(128 * b, 128 * (b + 1))
        both_rows = jnp.where(top_row, lo_r[0:1, cols], pos_r[0:1, cols]).astype(F32)
        s.span[cols, :] = both_rows.T.astype(jnp.int32)
    s.row[0:1, 0:256] = g_in[0:256].reshape(1, 256)
    s.row[0:1, 256:261] = g_in[256:261].reshape(1, 5)
    s.gcol[...] = jnp.broadcast_to(s.row[0:1, :], (128, CP)).T

    def norm_pixels(t):
        cols = slice(256 * t, 256 * (t + 1))
        normed = (norm_cols(pix[:, cols].astype(F32))[0] * s.gcol[0:261, 0:1]).astype(BF)
        s.xt[k, 0:256, cols] = normed[0:256]
        s.xt[k, 256:261, cols] = normed[256:261]

    for t in range(4):
        norm_pixels(t)
    ln = (norm_parts(lat[...].astype(F32))[0] * g_lat[...]).astype(BF)
    s.lnp[p] = ln
    ln_in = spread(lambda q, h: s.lnp.at[q, 64 * h : 64 * h + 64])
    for i in range(2):
        f_wq[i].wait()
        s.wq_z[128 * i : 128 * (i + 1), :] = s.hpa[i].astype(BF)
    wk_s_in = []
    for d in (1, 2, 3):
        wk_z[d].wait_recv()
        there = s.wk.at[plane[d], half]
        wk_s_in.append(put(there, there, sib))
    relay(ln_in)
    for copy in f_wv:
        copy.wait()
    s.wv_z[0:256, :] = s.u3[0].astype(BF)
    s.wv_z[256:261, :] = s.u3[1, 0:5, :].astype(BF)
    for i in range(2):
        f_wo[i].wait()
        s.wo_z[128 * i : 128 * (i + 1), :] = s.hpb[i].astype(BF)
    wvo_part = mm(s.wv_z[...], s.wo_z[:, lanes])
    s.wvz[0] = wvo_part[:CR].astype(BF)
    arrived(wk_s_in)
    own_rows = pl.ds(pl.multiple_of(k * 128, 128), 128)
    part = jnp.zeros((128, CP), F32)
    for j in range(4):
        part += mm_nt(s.wq_z[own_rows, 256 * j : 256 * (j + 1)], s.wk[j])
    s.wqk[z, k] = part.astype(BF)
    wqk_z = to_planes(lambda d: s.wqk.at[z, k], lambda d: s.wqk.at[z, k])
    wqk_s = [put(s.wqk.at[z, k], s.wqk.at[z, k], sib)]
    wvo_z = to_planes(lambda d: s.wvz.at[0], lambda d: s.wvz.at[d])
    x_xn = put(s.xt.at[k, 0:CX], s.xt.at[k, 0:CX], sib)
    for copy in f_d:
        copy.wait()
    s.wd1[z, p] = s.h3[0:32, :].astype(BF)
    wd1_z = to_planes(lambda d: s.wd1.at[z, p], lambda d: s.wd1.at[z, p])

    for j in range(2):
        half_z = pl.ds(pl.multiple_of(z * 256 + 128 * j, 128), 128)
        s.wu3[p, half_z, :] = early(2 + j)[...].astype(BF)
        for i in range(3):
            s.wqkv[i, k, half_z, :] = early(4 + 2 * i + j)[...].astype(BF)
    s.woz[z] = s.h3[32:64, :].astype(BF)
    f_d3.wait()
    s.wd3[z] = s.hxa[...].astype(BF).reshape(4, 32, D)
    arrived(wu1_z)
    wu1_in = spread(lambda q, h: s.wu1.at[q, 512 * h : 512 * h + 512])
    for d in (1, 2, 3):
        wqk_z[d].wait_recv()
        there = s.wqk.at[plane[d], k]
        wqk_s.append(put(there, there, sib))
    relay(wu1_in)
    arrived(wqk_s)
    wqk = s.wqk[...].reshape(D, CP)
    s.qk[p] = mm(ln, wqk).astype(BF)
    qk_in = to_peers(lambda d: s.qk.at[p], lambda d: s.qk.at[p])
    arrived(wvo_z)
    s.wvo[c, 0:CR, :] = sum(s.wvz[d].astype(F32) for d in range(4)).astype(BF)

    def wvo_slot(i):
        return s.wvo.at[i, 0:CR]

    wvo_in = gather(wvo_slot)
    wu3_z = to_planes(lambda d: s.wu3.at[p, own_z], lambda d: s.wu3.at[p, own_z])
    qkv_z = to_planes(lambda d: s.wqkv.at[:, k, own_z], lambda d: s.wqkv.at[:, k, own_z])
    wo_z = to_planes(lambda d: s.woz.at[z], lambda d: s.woz.at[z])
    wd3_z = to_planes(lambda d: s.wd3.at[z], lambda d: s.wd3.at[z])
    x_xn.wait_recv()

    wide = lax.broadcasted_iota(jnp.int32, (128, 1024), 1)
    lane = lax.broadcasted_iota(jnp.int32, (128, CP), 1)

    def cross_block(q):
        rows = pl.ds(pl.multiple_of((2 * q + k) * 128, 128), 128)
        low, high = s.span[rows, 0:1], s.span[rows, 1:2]
        scores = []
        for h in range(2):
            at = wide + (2 * p + h) * 1024
            sc = mm(s.qk[q], s.xt[h]) * CROSS_SCALE
            scores.append(jnp.where((at >= low) & (at <= high), sc, MASKED))
        top = jnp.maximum(*(jnp.max(sc, axis=1, keepdims=True) for sc in scores))
        total = jnp.zeros((128, 1), F32)
        acc = jnp.zeros((128, CP), F32)
        for h in range(2):
            e = jnp.where(scores[h] > 0.5 * MASKED, jnp.exp(scores[h] - top), 0.0).astype(BF)
            s.ee[2 * q + h] = e
            total += jnp.sum(e.astype(F32), axis=1, keepdims=True)
            acc += mm_nt(e, s.xt[h])
        s.tops[q] = jnp.broadcast_to(top, (128, 128))
        s.pxs[q] = tag(acc, lane, top, total)

    cross_block(p)
    px_in = {}
    for d in (1, 2, 3):
        qk_in[d].wait_recv()
        cross_block(chip[d])
        px_in[d] = put(s.pxs.at[chip[d]], s.pxr.at[d - 1], peer(d))
    wvo_s = pass_on(wvo_in)
    arrived(wd1_z)
    wd1_in = spread(lambda q, h: s.wd1.at[2 * h : 2 * h + 2, q])
    arrived(px_in)
    found = [untag(s.pxs[p], lane)] + [untag(s.pxr[i], lane) for i in range(3)]
    high = found[0][1]
    for f in found[1:]:
        high = jnp.maximum(high, f[1])
    px, total = jnp.zeros((128, CP), F32), jnp.zeros((128, 1), F32)
    for val, top, tot in found:
        share = jnp.exp(top - high)
        px += share * val
        total += share * tot
    px = px / total
    s.px[...] = px
    lse = high + jnp.log(total)
    s.pxl[...] = px.astype(BF)
    relay(wd1_in)
    arrived(wvo_s)
    lat_f = lat[...].astype(F32)
    pxl = s.pxl[...]
    for j in range(4):
        cols = slice(256 * j, 256 * (j + 1))
        w = jnp.concatenate([s.wvo[2 * j], s.wvo[2 * j + 1]], axis=1)
        s.h1[:, cols] = lat[:, cols].astype(F32) + mm(pxl, w)

    def mlp_start(h_ref, gain, npair):
        npair[k] = (norm_parts(h_ref[...])[0] * gain[...]).astype(BF)
        return put(npair.at[k], npair.at[k], sib)

    def mlp_up(npair, wu, u, zb):
        rows = npair[...].reshape(256, D)
        for j in range(2):
            w = jnp.concatenate([wu[2 * j], wu[2 * j + 1]], axis=1)
            hidden = mm(rows, w)
            u[j] = hidden
            zb[j] = gelu(hidden).astype(BF)

    def mlp_down(zb, wd, hp, hx):
        for t in range(4):
            cols = slice(256 * t, 256 * (t + 1))
            acc = mm(zb[0], wd[0:2, :, :, cols].reshape(256, 256))
            acc += mm(zb[1], wd[2:4, :, :, cols].reshape(256, 256))
            hp[:, :, cols] = acc.reshape(2, 128, 256)
        return put(hp.at[k2], hx, sib)

    def mlp_back(gpair, wu, wd, u, gub, hp, hs, hx):
        rows = gpair[...].reshape(256, D)
        for j in range(2):
            gz = mm_nt(rows, wd[2 * j : 2 * j + 2].reshape(256, D))
            gub[j] = (gz * gelu_slope(u[j])).astype(BF)
        for t in range(4):
            cols = slice(256 * t, 256 * (t + 1))
            acc = jnp.zeros((256, 256), F32)
            for j in range(2):
                w = jnp.concatenate([wu[2 * j, cols, :], wu[2 * j + 1, cols, :]], axis=1)
                acc += mm_nt(gub[j], w)
            hp[:, :, cols] = acc.reshape(2, 128, 256)
        hs[...] = hp[k2].astype(BF)
        return put(hs, hx, sib)

    def up_partial(npair, gub):
        for j in range(2):
            for t in range(4):
                cols = slice(256 * t, 256 * (t + 1))
                g = mm_tn(npair[:, :, cols].reshape(256, 256), gub[j]).astype(BF)
                s.gsu[2 * j, cols, :] = g[:, :128]
                s.gsu[2 * j + 1, cols, :] = g[:, 128:]

    def up_fold():
        return fold(
            lambda d, h: s.gsu.at[chip[d], 512 * h : 512 * h + 512],
            lambda i, h: s.gru.at[i, 512 * h : 512 * h + 512],
        )

    def down_partial(zb, gpair):
        for j in range(2):
            for t in range(4):
                cols = slice(256 * t, 256 * (t + 1))
                g = mm_tn(zb[j], gpair[:, :, cols].reshape(256, 256)).astype(BF)
                s.gsd[2 * j : 2 * j + 2, :, :, cols] = g.reshape(2, 4, 32, 256)

    def down_fold():
        return fold(
            lambda d, h: s.gsd.at[2 * h : 2 * h + 2, chip[d]],
            lambda i, h: s.grd.at[i, 2 * h : 2 * h + 2],
        )

    def up_to_planes(up, zs, zr):
        arrived(up[3])
        total = s.gsu[p].astype(F32)
        for i in (1, 2):
            total += s.gru[i].astype(F32)
        zs[...] = total.astype(BF)
        return to_planes(
            lambda d: zs.at[pl.ds(pl.multiple_of(plane[d] * 256, 256), 256)], lambda d: zr.at[d - 1]
        )

    def down_to_planes(down, zs, zr):
        arrived(down[3])
        total = s.gsd[:, p].astype(F32)
        for i in (1, 2):
            total += s.grd[i].astype(F32)
        zs[...] = total.astype(BF)
        return to_planes(lambda d: zs.at[plane[d]], lambda d: zr.at[d - 1])

    def up_total(copies, zs, zr, ag):
        arrived(copies)
        total = zs[own_z, :].astype(F32)
        for i in range(3):
            total += zr[i].astype(F32)
        ag[c] = total.astype(BF)
        return gather(lambda i: ag.at[i], lambda i, h: ag.at[i, 128 * h : 128 * h + 128])

    def row_slot(ag):
        return lambda i: ag.at[lax.rem(i, 2), lax.div(i, 2)]

    def row_half(ag):
        return lambda i, h: ag.at[lax.rem(i, 2), lax.div(i, 2), 16 * h : 16 * h + 16]

    def down_total(copies, zs, zr, ag):
        arrived(copies)
        total = zs[z].astype(F32)
        for i in range(3):
            total += zr[i].astype(F32)
        ag[k, p] = total.astype(BF)
        return gather(row_slot(ag), row_half(ag))

    outs = []

    def out_cols(ag, w):
        for j in range(8):
            outs.append(fetch(ag.at[j], d_big.at[w, :, 128 * j : 128 * (j + 1)]))

    def out_rows(ag, w):
        for kk in range(2):
            for q in range(4):
                at = 128 * kk + 32 * q
                outs.append(fetch(ag.at[kk, q], d_big.at[w, at : at + 32, :]))

    x_n1 = mlp_start(s.h1, g_cmlp, s.n1)
    arrived(wu3_z)
    wu3_in = spread(lambda q, h: s.wu3.at[q, 512 * h : 512 * h + 512])
    all_of(wu1_in)
    x_n1.wait_recv()
    mlp_up(s.n1, s.wu1, s.u1, s.z1)
    all_of(wd1_in)
    x_h1 = mlp_down(s.z1, s.wd1, s.hpa, s.hxa)
    relay(wu3_in)
    arrived(qkv_z)
    x_qkv = put(s.wqkv.at[:, k], s.wqkv.at[:, k], sib)
    x_h1.wait_recv()
    s.h2[...] = s.h1[...] + s.hpa[k] + s.hxa[...]

    s.n2[p] = (norm_parts(s.h2[...])[0] * g_self[...]).astype(BF)
    n2_in = spread(lambda q, h: s.n2.at[q, 64 * h : 64 * h + 64])
    x_qkv.wait_recv()

    def project(q):
        rows = s.n2[q]
        for i in range(3):
            w = jnp.concatenate([s.wqkv[i, 0], s.wqkv[i, 1]], axis=1)
            s.pair[...] = mm(rows, w).astype(BF).reshape(128, 256)
            for h in range(2):
                s.heads[h, q, i] = s.pair[:, 128 * h : 128 * (h + 1)]
        s.mine[2 * q + k] = s.heads[k, q]
        return put(s.heads.at[k2, q], s.mine.at[2 * q + k], sib)

    qkv_in = [project(p)]
    relay(n2_in)
    for d in (1, 2):
        near(n2_in, d)
        qkv_in.append(project(chip[d]))
    far(n2_in)
    qkv_in.append(project(chip[3]))
    arrived(wo_z)
    piece = pl.ds(pl.multiple_of(32 * p, 32), 32)
    s.wo[k, piece, :] = s.woz[p]
    wo_in = to_peers(lambda d: s.woz.at[chip[d]], lambda d: s.wo.at[k, piece])
    arrived(qkv_in)

    def attend(b):
        rows = pl.ds(pl.multiple_of(b * 128, 128), 128)
        keys = s.mine[:, 1].reshape(D, 128)
        sc = mm_nt(s.mine[b, 0], keys) * SELF_SCALE
        at = s.pos[0:1, :]
        sc = jnp.where((at >= s.span[rows, 0:1]) & (at <= s.span[rows, 1:2]), sc, MASKED)
        e = jnp.exp(sc - jnp.max(sc, axis=1, keepdims=True))
        low = (e / jnp.sum(e, axis=1, keepdims=True)).astype(BF)
        s.a1[b] = low
        return mm(low, s.mine[:, 2].reshape(D, 128)).astype(BF)

    def other_rows(q, carry):
        s.send[q] = attend(2 * q + k2)
        return carry

    def own_parity(q, carry):
        s.aspar[q, k] = attend(2 * q + k)
        return carry

    lax.fori_loop(0, 4, other_rows, 0)
    x_as = put(s.send, s.aspar.at[:, k], sib)
    arrived(wo_in)
    x_wo = put(s.wo.at[k], s.wo.at[k], sib)
    lax.fori_loop(0, 4, own_parity, 0)
    x_wo.wait_recv()
    x_as.wait_recv()

    def both(ref, q):
        return jnp.concatenate([ref[q, 0], ref[q, 1]], axis=1)

    for d in (3, 1, 2):
        s.outp[d - 1] = mm(both(s.aspar, chip[d]), s.wo[...].reshape(256, D)).astype(BF)

    def rows_out(d, h):
        return s.outp.at[d - 1, 64 * h : 64 * h + 64]

    def rows_in(i, h):
        return s.outr.at[i, 64 * h : 64 * h + 64]

    out_in = fold(rows_out, rows_in)
    s.h3[...] = s.h2[...] + mm(both(s.aspar, p), s.wo[...].reshape(256, D))
    fold_on(out_in)
    arrived(out_in[3])
    s.h3[...] += s.outr[1].astype(F32) + s.outr[2].astype(F32)

    x_n3 = mlp_start(s.h3, g_smlp, s.n3)
    all_of(wu3_in)
    x_n3.wait_recv()
    mlp_up(s.n3, s.wu3, s.u3, s.z3)
    arrived(wd3_z)
    x_cot.wait_recv()
    sent([x_h1])
    x_d3 = mlp_back(s.cpair, s.wu3, s.wd3, s.u3, s.gu3, s.hpa, s.hs, s.hr)
    x_h3 = mlp_down(s.z3, s.wd3, s.hpb, s.hxb)
    x_d3.wait_recv()
    dx, gg_smlp = norm_back(s.hpa[k] + s.hr[...].astype(F32), s.h3[...], g_smlp[...])
    dh3 = cot[...].astype(F32) + dx
    s.dh[...] = dh3
    s.go[p] = dh3.astype(BF)
    go_in = spread(lambda q, h: s.go.at[q, 64 * h : 64 * h + 64])
    x_h3.wait_recv()
    layer_out[...] = (s.h3[...] + s.hpb[k] + s.hxb[...]).astype(BF)

    def pull_out(q):
        g = mm_nt(s.go[q], s.wo[...].reshape(256, D)).astype(BF)
        s.pair[...] = g
        for h in range(2):
            s.gheads[h, q] = s.pair[:, 128 * h : 128 * (h + 1)]
        s.gmine[2 * q + k] = s.gheads[k, q]
        return put(s.gheads.at[k2, q], s.gmine.at[2 * q + k], sib)

    gas_in = [pull_out(p)]
    relay(go_in)
    up_partial(s.n3, s.gu3)
    s.gsu_own[...] = s.gsu[:, own_z, :]
    g3u_z = to_planes(
        lambda d: s.gsu.at[:, pl.ds(pl.multiple_of(plane[d] * 256, 256), 256)], lambda d: s.zg.at[d - 1]
    )
    for d in (1, 2):
        near(go_in, d)
        gas_in.append(pull_out(chip[d]))
    far(go_in)
    gas_in.append(pull_out(chip[3]))
    down_partial(s.z3, s.cpair)
    g3d = down_fold()
    arrived(gas_in)

    def attend_back(b, carry):
        dps = mm_nt(s.gmine[b], s.mine[:, 2].reshape(D, 128))
        probs = s.a1[b].astype(F32)
        delta = jnp.sum(probs * dps, axis=1, keepdims=True) / jnp.sum(probs, axis=1, keepdims=True)
        dss = (probs * (dps - delta) * SELF_SCALE).astype(BF)
        s.a2[b] = dss
        s.heads[lax.div(b, 4), lax.rem(b, 4), 0] = mm(dss, s.mine[:, 1].reshape(D, 128)).astype(BF)
        return carry

    sent(qkv_in)
    lax.fori_loop(0, 8, attend_back, 0)
    fold_on(g3d)
    for t in range(4):
        cols = slice(256 * t, 256 * (t + 1))
        dk = mm_tn(s.a2[:, :, cols].reshape(D, 256), s.mine[:, 0].reshape(D, 128))
        dv = mm_tn(s.a1[:, :, cols].reshape(D, 256), s.gmine[...].reshape(D, 128))
        two = slice(2 * (t % 2), 2 * (t % 2) + 2)
        s.heads[t // 2, two, 1] = dk.astype(BF).reshape(2, 128, 128)
        s.heads[t // 2, two, 2] = dv.astype(BF).reshape(2, 128, 128)

    def sort(q, carry):
        high, low = lax.div(q, 2), 2 * lax.rem(q, 2)
        s.dsend[q] = s.heads[high, low + k2]
        for i in range(3):
            s.dpar[q, i, k] = s.heads[high, low + k, i]
        return carry

    lax.fori_loop(0, 4, sort, 0)
    x_dp = put(s.dsend, s.dpar.at[:, :, k], sib)
    g3d_z = down_to_planes(g3d, s.sd3, s.zd3)
    x_dp.wait_recv()

    def pull_in(q, write):
        for t in range(4):
            cols = slice(256 * t, 256 * (t + 1))
            acc = jnp.zeros((128, 256), F32)
            for i in range(3):
                w = jnp.concatenate([s.wqkv[i, 0, cols, :], s.wqkv[i, 1, cols, :]], axis=1)
                acc += mm_nt(jnp.concatenate([s.dpar[q, i, 0], s.dpar[q, i, 1]], axis=1), w)
            write(cols, acc)

    sent(out_in[2])
    sent(out_in[3])
    for d in (3, 1, 2):

        def write(cols, acc):
            s.outp[d - 1, :, cols] = acc.astype(BF)

        pull_in(chip[d], write)
    dn_in = fold(rows_out, rows_in)

    def write(cols, acc):
        s.hxb[:, cols] = acc

    pull_in(p, write)

    def project_grad(i):
        g = jnp.concatenate([s.dpar[:, i, 0].reshape(PARITY_ROWS, 128), s.dpar[:, i, 1].reshape(PARITY_ROWS, 128)], axis=1)
        for t in range(4):
            cols = slice(256 * t, 256 * (t + 1))
            w = mm_tn(s.n2[:, :, cols].reshape(PARITY_ROWS, 256), g).astype(BF)
            for h in range(2):
                s.pg[i, h, cols, :] = w[:, 128 * h : 128 * (h + 1)]
        return put(s.pg.at[i, k2], s.pgr.at[i], sib)

    def project_planes(i):
        x_pg[i].wait_recv()
        s.pg[i, k] = (s.pg[i, k].astype(F32) + s.pgr[i].astype(F32)).astype(BF)
        return to_planes(
            lambda d: s.pg.at[i, k, pl.ds(pl.multiple_of(plane[d] * 256, 256), 256)],
            lambda d: s.zq.at[d - 1, i],
        )

    x_pg = [project_grad(0)]
    fold_on(dn_in)
    x_pg.append(project_grad(1))
    pg_z = [project_planes(0)]
    x_pg.append(project_grad(2))
    pg_z.append(project_planes(1))
    g = jnp.concatenate([s.aspar[:, 0].reshape(PARITY_ROWS, 128), s.aspar[:, 1].reshape(PARITY_ROWS, 128)], axis=1)
    for t in range(4):
        cols = slice(256 * t, 256 * (t + 1))
        w = mm_tn(g, s.go[:, :, cols].reshape(PARITY_ROWS, 256)).astype(BF)
        s.pgo[:, :, cols] = w.reshape(2, 128, 256)
    x_pgo = put(s.pgo.at[k2], s.pgor, sib)
    arrived(dn_in[3])
    dn2 = s.hxb[...] + s.outr[1].astype(F32) + s.outr[2].astype(F32)
    dx, gg_self = norm_back(dn2, s.h2[...], g_self[...])
    s.dh[...] += dx

    s.gpair[k] = s.dh[...].astype(BF)
    x_g = put(s.gpair.at[k], s.gpair.at[k], sib)
    pg_z.append(project_planes(2))
    x_g.wait_recv()
    sent([x_d3])
    x_d1 = mlp_back(s.gpair, s.wu1, s.wd1, s.u1, s.gu1, s.hpa, s.hs, s.hr)
    x_pgo.wait_recv()
    s.pgo[k] = (s.pgo[k].astype(F32) + s.pgor[...].astype(F32)).astype(BF)
    s.wz[p] = s.pgo[k, piece, :]
    pgo_in = to_peers(
        lambda d: s.pgo.at[k, pl.ds(pl.multiple_of(32 * chip[d], 32), 32)], lambda d: s.wz.at[p]
    )
    sent(g3d[2])
    sent(g3d[3])
    down_partial(s.z1, s.gpair)
    g1d = down_fold()
    x_d1.wait_recv()
    dx, gg_cmlp = norm_back(s.hpa[k] + s.hr[...].astype(F32), s.h1[...], g_cmlp[...])
    dh1 = s.dh[...] + dx
    s.dh[...] = dh1

    go1 = dh1.astype(BF)
    gv = jnp.zeros((128, CP), F32)
    for j in range(4):
        w = jnp.concatenate([s.wvo[2 * j], s.wvo[2 * j + 1]], axis=1)
        gv += mm_nt(go1[:, 256 * j : 256 * (j + 1)], w)
    gv = gv.astype(BF).astype(F32)
    delta = jnp.sum(jnp.where(lane < 261, s.px[...] * gv, 0.0), axis=1, keepdims=True)
    s.gv[p] = tag(gv, lane, lse, delta)
    gv_in = spread(lambda q, h: s.gv.at[q, 64 * h : 64 * h + 64])
    arrived(pgo_in)
    pgo_z = to_planes(lambda d: s.wz.at[plane[d]], lambda d: s.zo.at[d - 1])
    fold_on(g1d)
    for j in range(4):
        f_part = mm_tn(s.pxl[...], go1[:, 256 * j : 256 * (j + 1)])[:CR].astype(BF)
        s.fst[j, 0] = f_part[:, :128]
        s.fst[j, 1] = f_part[:, 128:]
    sent(wvo_in[1])
    sent(wvo_s)
    x_f = put(s.fst.at[:, k2], s.fsr, sib)
    sent(g3u_z)
    up_partial(s.n1, s.gu1)
    g1u = up_fold()
    def cross_back(q):
        val, last, delta = untag(s.gv[q], lane)
        ratio = jnp.exp(s.tops[q][:, 0:1] - last)
        s.gvr[q] = (val * ratio).astype(BF)
        acc = jnp.zeros((128, CP), F32)
        for h in range(2):
            dp = mm(s.gv[q], s.xt[h])
            ds = (s.ee[2 * q + h].astype(F32) * ((dp - delta) * (ratio * CROSS_SCALE))).astype(BF)
            s.a2[2 * q + h] = ds
            acc += mm_nt(ds, s.xt[h])
        s.pxs[q] = acc.astype(BF)
        return acc

    sent(px_in)
    s.dqk[...] = cross_back(p)
    relay(gv_in)
    x_f.wait_recv()
    s.fst[:, k] = (s.fst[:, k].astype(F32) + s.fsr[...].astype(F32)).astype(BF)
    f_in = fold(
        lambda d, h: s.fst.at[chip[d], k, 144 * h : 144 * h + 144], lambda i, h: s.fpr.at[i, 144 * h : 144 * h + 144]
    )
    for d in (1, 2):
        near(gv_in, d)
        cross_back(chip[d])
    far(gv_in)
    cross_back(chip[3])
    g1d_z = down_to_planes(g1d, s.sd1, s.zd1)
    fold_on(g1u)
    all_of(ln_in)
    for j in range(4):
        e = mm_tn(s.lnp[:, :, 256 * j : 256 * (j + 1)].reshape(PARITY_ROWS, 256), s.pxs[...].reshape(PARITY_ROWS, CP))
        s.est[j] = e.astype(BF).reshape(4, 2, 32, CP)
    x_e = put(s.est.at[:, :, k2], s.esr, sib)
    dq_in = fold(
        lambda d, h: s.pxs.at[chip[d], 64 * h : 64 * h + 64], lambda i, h: s.pxr.at[i, 64 * h : 64 * h + 64]
    )
    fold_on(f_in)
    for q in range(4):
        for j in range(3):
            cols = slice(128 * j, 128 * (j + 1))
            s.a1[j, :, 128 * q : 128 * (q + 1)] = s.qk[q, :, cols].T
            s.a1[j, :, 512 + 128 * q : 512 + 128 * (q + 1)] = s.gvr[q, :, cols].T

    def pixel_cols(h, t):
        cols = slice(256 * t, 256 * (t + 1))
        parts = [s.a2[2 * q + h, :, cols] for q in range(4)] + [s.ee[2 * q + h, :, cols] for q in range(4)]
        return mm(s.a1[0:3].reshape(CP, 1024), jnp.concatenate(parts, axis=0))

    for t in range(4):
        s.dxs[:, 256 * t : 256 * (t + 1)] = pixel_cols(k2, t)[:CX].astype(BF)
    x_dx = put(s.dxs, s.dxr, sib)
    x_e.wait_recv()
    s.est[:, :, k] = (s.est[:, :, k].astype(F32) + s.esr[...].astype(F32)).astype(BF)
    e_in = to_peers(lambda d: s.est.at[:, chip[d], k], lambda d: s.epr.at[d - 1])
    g1u_z = up_to_planes(g1u, s.su1, s.zu1)
    fold_on(dq_in)
    arrived(dq_in[3])
    dqk = (s.dqk[...] + s.pxr[1].astype(F32) + s.pxr[2].astype(F32)).astype(BF)
    dx, gg_lat = norm_back(mm_nt(dqk, s.wqk[...].reshape(D, CP)), lat[...].astype(F32), g_lat[...])
    s.dh[...] += dx
    outs.append(fetch(s.dh, d_lat))
    arrived(e_in)
    total = s.est[:, p, k].astype(F32)
    for i in range(3):
        total += s.epr[i].astype(F32)
    s.ez[...] = total.astype(BF)
    e_z = to_planes(lambda d: s.ez.at[plane[d]], lambda d: s.ezr.at[d - 1])
    arrived(f_in[3])
    total = s.fst[p, k].astype(F32)
    for i in (1, 2):
        total += s.fpr[i].astype(F32)
    s.fz[0] = total.astype(BF)
    f_z = to_planes(lambda d: s.fz.at[0], lambda d: s.fz.at[d])
    arrived(g3u_z)
    s.zs[...] = (s.gsu_own[...].astype(F32) + sum(s.zg[i].astype(F32) for i in range(3))).astype(BF)
    g3u_in = to_peers(lambda d: s.zs.at[chip[d]], lambda d: s.zu3.at[d - 1])
    g3d_ag = down_total(g3d_z, s.sd3, s.zd3, s.agd3)

    x_dx.wait_recv()
    gg_in = jnp.zeros((261, 1), F32)
    for t in range(4):
        cols = slice(256 * t, 256 * (t + 1))
        dxn = (pixel_cols(k, t)[:CX] + s.dxr[:, cols].astype(F32))[:261]
        hat, r = norm_cols(pix[:, cols].astype(F32))
        dhat = dxn * s.gcol[0:261, 0:1]
        even = jnp.mean(dhat, axis=0, keepdims=True)
        tilt = jnp.mean(dhat * hat, axis=0, keepdims=True)
        d_pix[:, cols] = r * (dhat - even - hat * tilt)
        gg_in += jnp.sum(dxn * hat, axis=1, keepdims=True)
    s.gcol[0:261, :] = jnp.broadcast_to(gg_in, (261, 128))
    s.ga[k] = jnp.zeros((8, D), F32)
    s.ga[k, 0:1, 0:CP] = s.gcol[...].T[0:1, :]
    for i, gg in enumerate((gg_lat, gg_cmlp, gg_self, gg_smlp)):
        s.ga[k, i + 1 : i + 2, :] = gg
    x_ga = put(s.ga.at[k], s.ga.at[k], sib)

    arrived(e_z)
    total = s.ez[z].astype(F32)
    for i in range(3):
        total += s.ezr[i].astype(F32)
    s.eag[c] = total.astype(BF)
    e_s = to_plane(s.eag.at[c])
    x_ga.wait_recv()
    s.gb[p] = s.ga[0] + s.ga[1]
    gb_in = to_peers(lambda d: s.gb.at[p], lambda d: s.gb.at[p])
    relay(g3d_ag[1])
    arrived(g3u_in)
    s.agu3[c] = (s.zs[p].astype(F32) + sum(s.zu3[i].astype(F32) for i in range(3))).astype(BF)
    g3u_ag = gather(lambda i: s.agu3.at[i], lambda i, h: s.agu3.at[i, 128 * h : 128 * h + 128])
    for copies in pg_z:
        arrived(copies)
    for i in range(3):
        total = s.pg[i, k, own_z, :].astype(F32)
        for d in range(3):
            total += s.zq[d, i].astype(F32)
        s.agq[c, i] = total.astype(BF)
    q_ag = gather(lambda i: s.agq.at[i], lambda i, h: s.agq.at[i, :, 128 * h : 128 * h + 128])
    arrived(gb_in)
    s.gc[z] = s.gb[0] + s.gb[1] + s.gb[2] + s.gb[3]
    gc_in = to_planes(lambda d: s.gc.at[z], lambda d: s.gc.at[z])
    relay(g3u_ag[1])
    relay(q_ag[1])
    wo_ag = down_total(pgo_z, s.wz, s.zo, s.ago)
    g3d_s = pass_on(g3d_ag)
    arrived(f_z)
    s.wvo[c, 0:CR, :] = sum(s.fz[d].astype(F32) for d in range(4)).astype(BF)

    def f_slot(i):
        return s.wvo.at[i, 0:CR]

    f_ag = gather(f_slot, lambda i, h: s.wvo.at[i, 144 * h : 144 * h + 144])
    eighth = pl.ds(pl.multiple_of(c * 48, 16), 48)
    arrived(e_s)
    e_all = s.eag[...].reshape(256, CP)
    for j in range(4):
        s.gks[j] = mm_tn(e_all, s.wq_z[:, 256 * j : 256 * (j + 1)]).astype(BF)
    gk_z = to_planes(lambda d: s.gks.at[plane[d], eighth], lambda d: s.gkr.at[d - 1])
    sent([x_n3])
    for j in range(4):
        s.n3[:, :, 256 * j : 256 * (j + 1)] = mm(e_all, s.wk[j]).astype(BF).reshape(2, 128, 256)
    outs.extend(fetch(s.n3.at[i], d_big.at[8, 128 * i : 128 * (i + 1)]) for i in range(2))
    g1d_ag = down_total(g1d_z, s.sd1, s.zd1, s.agd1)
    g1u_ag = up_total(g1u_z, s.su1, s.zu1, s.agu1)
    relay(f_ag[1])
    relay(wo_ag[1])
    g3u_s = pass_on(g3u_ag)
    relay(g1d_ag[1])
    relay(g1u_ag[1])
    arrived(gk_z)
    total = s.gks[z, eighth, :].astype(F32)
    for i in range(3):
        total += s.gkr[i].astype(F32)
    s.gkh[eighth, :] = total.astype(BF)
    x_gk = to_plane(s.gkh.at[eighth])
    q_s = pass_on(q_ag)
    f_s = pass_on(f_ag)
    wo_s_ = pass_on(wo_ag)
    g1d_s = pass_on(g1d_ag)
    g1u_s = pass_on(g1u_ag)
    arrived(g3d_s)
    out_rows(s.agd3, 7)
    arrived(g3u_s)
    out_cols(s.agu3, 6)
    arrived(f_s)
    sent([x_n1])
    acc = jnp.zeros((CP, 256), F32)
    for j in range(4):
        f_two = jnp.concatenate([s.wvo[2 * j], s.wvo[2 * j + 1]], axis=1)
        acc += mm_nt(f_two, s.wo_z[:, 256 * j : 256 * (j + 1)])
        s.n1[:, :, 256 * j : 256 * (j + 1)] = mm_tn(s.wv_z[...], f_two).astype(BF).reshape(2, 128, 256)
    d_wv[...] = acc[:261]
    outs.extend(fetch(s.n1.at[i], d_big.at[9, 128 * i : 128 * (i + 1)]) for i in range(2))
    arrived(q_s)
    for i in range(3):
        for j in range(8):
            outs.append(fetch(s.agq.at[j, i], d_big.at[2 + i, :, 128 * j : 128 * (j + 1)]))
    arrived(wo_s_)
    out_rows(s.ago, 5)
    arrived(gc_in)
    d_gain[...] = s.gc[0] + s.gc[1] + s.gc[2] + s.gc[3]
    arrived(x_gk)
    d_wk[...] = s.gkh[...].astype(F32)[0:261]
    arrived(g1d_s)
    out_rows(s.agd1, 1)
    arrived(g1u_s)
    out_cols(s.agu1, 0)
    for copy in outs:
        copy.wait()
    for when, copy in sends:
        if when is None:
            copy.wait_send()
        else:
            pl.when(when)(copy.wait_send)


def norm_cols(x):
    center = x - jnp.mean(x, axis=0, keepdims=True)
    r = lax.rsqrt(jnp.mean(center * center, axis=0, keepdims=True) + 1e-05)
    return center * r, r


def tag(val, lane, one, two):
    for i, x in enumerate((one, two)):
        for j in range(3):
            part = x.astype(BF).astype(F32)
            val = jnp.where(lane == 261 + 3 * i + j, part, val)
            x = x - part
    return val.astype(BF)


def untag(low, lane):
    val = low.astype(F32)

    def column(i):
        here = (lane >= 261 + 3 * i) & (lane < 264 + 3 * i)
        return jnp.sum(jnp.where(here, val, 0.0), axis=1, keepdims=True)

    return jnp.where(lane < 261, val, 0.0), column(0), column(1)


SCRATCH = {
    "ssem": 400, "rsem": 400, "lsem": 96,

    "wk": ((4, CP, 256), BF), "wqk": ((4, 2, 128, CP), BF), "wq_z": ((256, 1024), BF), "wo_z": ((256, 1024), BF),
    "wv_z": ((CP, 256), BF), "wvz": ((4, CR, 128), BF), "wvo": ((8, CP, 128), BF),
    "wu1": ((4, 1024, 128), BF), "wu3": ((4, 1024, 128), BF), "wd1": ((4, 4, 32, 1024), BF), "wd3": ((4, 4, 32, 1024), BF),
    "wqkv": ((3, 2, 1024, 128), BF), "wo": ((2, 128, 1024), BF),
    "xt": ((2, CP, 1024), BF), "span": ((1024, 128), jnp.int32), "pos": ((8, 1024), jnp.int32), "row": ((8, CP), F32), "gcol": ((CP, 128), F32), "lnp": ((4, 128, 1024), BF), "qk": ((4, 128, CP), BF),
    "pxs": ((4, 128, CP), BF), "pxr": ((3, 128, CP), BF), "px": ((128, CP), F32), "pxl": ((128, CP), BF),
    "cpair": ((2, 128, 1024), BF), "n1": ((2, 128, 1024), BF), "n3": ((2, 128, 1024), BF),
    "u1": ((2, 256, 256), F32), "u3": ((2, 256, 256), F32), "z1": ((2, 256, 256), BF), "z3": ((2, 256, 256), BF),
    "gu1": ((2, 256, 256), BF), "gu3": ((2, 256, 256), BF),


    "h1": ((128, 1024), F32), "h2": ((128, 1024), F32), "h3": ((128, 1024), F32), "dh": ((128, 1024), F32),
    "n2": ((4, 128, 1024), BF), "go": ((4, 128, 1024), BF), "pair": ((128, 256), BF),
    "heads": ((2, 4, 3, 128, 128), BF), "mine": ((8, 3, 128, 128), BF),
    "a1": ((8, 128, 1024), BF), "a2": ((8, 128, 1024), BF), "send": ((4, 128, 128), BF), "aspar": ((4, 2, 128, 128), BF),
    "outp": ((3, 128, 1024), BF), "outr": ((3, 128, 1024), BF),
    "gheads": ((2, 4, 128, 128), BF), "gmine": ((8, 128, 128), BF),
    "dsend": ((4, 3, 128, 128), BF), "dpar": ((4, 3, 2, 128, 128), BF),


    "zu1": ((3, 256, 128), BF), "zu3": ((3, 256, 128), BF), "zd1": ((3, 32, 1024), BF), "zd3": ((3, 32, 1024), BF),
    "agu1": ((8, 256, 128), BF), "agu3": ((8, 256, 128), BF), "agd1": ((2, 4, 32, 1024), BF), "agd3": ((2, 4, 32, 1024), BF),
    "pg": ((3, 2, 1024, 128), BF), "pgr": ((3, 1024, 128), BF), "zq": ((3, 3, 256, 128), BF), "agq": ((8, 3, 256, 128), BF),
    "pgo": ((2, 128, 1024), BF), "pgor": ((128, 1024), BF), "zo": ((3, 32, 1024), BF), "ago": ((2, 4, 32, 1024), BF), "woz": ((4, 32, 1024), BF), "wz": ((4, 32, 1024), BF),
    "gv": ((4, 128, CP), BF), "dqk": ((128, CP), F32),
    "dxs": ((CX, 1024), BF), "dxr": ((CX, 1024), BF),
    "fst": ((4, 2, CR, 128), BF), "fsr": ((4, CR, 128), BF), "fpr": ((3, CR, 128), BF), "fz": ((4, CR, 128), BF),
    "est": ((4, 4, 2, 32, CP), BF), "esr": ((4, 4, 32, CP), BF), "epr": ((3, 4, 32, CP), BF), "ez": ((4, 32, CP), BF),
    "ezr": ((3, 32, CP), BF), "eag": ((8, 32, CP), BF),
    "gks": ((4, CP, 256), BF), "gkr": ((3, 48, 256), BF), "gkh": ((CP, 256), BF), "gpair": ((2, 128, 1024), BF), "zg": ((3, 4, 256, 128), BF), "zs": ((4, 256, 128), BF), "gsu_own": ((4, 256, 128), BF), "hs": ((128, 1024), BF), "hr": ((128, 1024), BF),
    "ga": ((2, 8, 1024), F32), "gb": ((4, 8, 1024), F32), "gc": ((4, 8, 1024), F32),
    "hpa": ((2, 128, 1024), F32), "hpb": ((2, 128, 1024), F32), "hxa": ((128, 1024), F32), "hxb": ((128, 1024), F32),
    "ee": ((8, 128, 1024), BF), "tops": ((4, 128, 128), F32), "gvr": ((4, 128, CP), BF),
    "gsu": ((4, 1024, 128), BF), "gsd": ((4, 4, 32, 1024), BF), "gru": ((3, 1024, 128), BF), "grd": ((3, 4, 32, 1024), BF),
    "su1": ((1024, 128), BF), "sd1": ((4, 32, 1024), BF), "sd3": ((4, 32, 1024), BF),
}


def unpack(layer_in, lat_in, big_in, wk_in, wv_in, gain_in, pix_in, layer_out, d_lat, *rest):
    big = rest[:10]
    wk_out, wv_out, gains, first, pix_out = rest[10], rest[11], rest[12:16], rest[16], rest[17]
    low, wide, pix_rows, sem_in, sem_out = rest[18:]
    loads = [pltpu.make_async_copy(big_in.at[i], low.at[i], sem_in.at[i]) for i in range(10)]
    for copy in loads:
        copy.start()
    pairs = ((layer_in, layer_out), (lat_in, d_lat), (wk_in, wk_out), (wv_in, wv_out))
    stores = [pltpu.make_async_copy(a, b, sem_out.at[i]) for i, (a, b) in enumerate(pairs)]
    for copy in stores:
        copy.start()
    for i in range(10):
        loads[i].wait()
        wide[i] = low[i].astype(F32)
        stores.append(pltpu.make_async_copy(wide.at[i], big[i], sem_out.at[4 + i]))
        stores[-1].start()
    pix_rows[...] = pix_in[...].reshape(261, 1, 1024)
    stores.append(pltpu.make_async_copy(pix_rows, pix_out, sem_out.at[18]))
    stores[-1].start()
    first[...] = gain_in[0:1, 0:261].reshape(261)
    for i in range(4):
        stores.append(pltpu.make_async_copy(gain_in.at[i + 1 : i + 2], gains[i], sem_out.at[14 + i]))
        stores[-1].start()
    for copy in stores:
        copy.wait()


def one_kernel(
    pixels, latents, cotangent, doc_lengths, latent_offsets, block_deal,
    wq_c, wk_c, wv_c, wo_c, wu_c, wd_c, wq_s, wk_s, wv_s, wo_s, wu_s, wd_s,
    g_in, g_lat, g_cmlp, g_self, g_smlp,
):
    vmem, hbm = pl.BlockSpec(memory_space=pltpu.VMEM), pl.BlockSpec(memory_space=pl.ANY)
    smem = pl.BlockSpec(memory_space=pltpu.SMEM)

    def shape(dims, kind=F32):
        return jax.ShapeDtypeStruct(dims, kind)

    layer_out, d_pix, d_lat, big, d_wk, d_wv, gains = pl.pallas_call(
        fused,
        out_shape=(
            shape((128, D), BF), shape((261, 1024)), shape((128, D)), shape((10, 256, D), BF),
            shape((261, 256)), shape((261, 256)), shape((8, D)),
        ),
        in_specs=[vmem, vmem, vmem, smem, vmem, smem] + [vmem] * 5 + [hbm] * 12,
        out_specs=(vmem, vmem, hbm, hbm, vmem, vmem, vmem),
        scratch_shapes=[
            pltpu.SemaphoreType.DMA((what,)) if isinstance(what, int) else pltpu.VMEM(*what)
            for what in SCRATCH.values()
        ],
        compiler_params=pltpu.CompilerParams(
            collective_id=0, has_side_effects=True, vmem_limit_bytes=VMEM_BYTES
        ),
        cost_estimate=pl.CostEstimate(flops=26 * 10**9, bytes_accessed=40 * 10**6, transcendentals=10**7),
    )(
        pixels[0].T, latents[0], cotangent[0], doc_lengths, latent_offsets, block_deal,
        g_in, g_lat[None], g_cmlp[None], g_self[None], g_smlp[None],
        wq_c, wk_c, wv_c, wo_c, wu_c, wd_c, wq_s, wk_s, wv_s, wo_s, wu_s, wd_s,
    )
    outs = pl.pallas_call(
        unpack,
        out_shape=(
            shape((128, D), BF), shape((128, D)), *[shape((256, D))] * 10, *[shape((261, 256))] * 2, *[shape((1, D))] * 4,
            shape((261,)), shape((261, 1, 1024)),
        ),
        in_specs=[vmem, vmem, hbm, vmem, vmem, vmem, vmem],
        out_specs=(*[hbm] * 18, vmem, hbm),
        scratch_shapes=[
            pltpu.VMEM((10, 256, D), BF), pltpu.VMEM((10, 256, D), F32), pltpu.VMEM((261, 1, 1024), F32),
            pltpu.SemaphoreType.DMA((10,)), pltpu.SemaphoreType.DMA((19,)),
        ],
        compiler_params=pltpu.CompilerParams(vmem_limit_bytes=VMEM_BYTES),
        cost_estimate=pl.CostEstimate(flops=0, bytes_accessed=18 * 10**6, transcendentals=0),
    )(layer_out, d_lat, big, d_wk, d_wv, gains, d_pix)
    layer_out, d_lat, d_big, d_wk, d_wv, d_gain = outs[0], outs[1], outs[2:12], outs[12], outs[13], outs[14:18]
    return (
        layer_out[None], outs[19].transpose(1, 2, 0), d_lat[None], d_big[8], d_wk, d_wv, d_big[9], *d_big[:8],
        outs[18], *(g[0] for g in d_gain),
    )


VMEM_BYTES = 65472 * 2**10


def solution(mesh):
    rows, row, col, all_ = P("fsdp", "ctx", None), P("fsdp", None), P(None, "fsdp"), P()
    weights = (row, col, col, *(row,) * 9)
    small = mesh.shape["ctx"] == 8 and mesh.shape["fsdp"] == 4
    return jax.shard_map(
        one_kernel if small else plain,
        mesh=mesh,
        in_specs=(rows, rows, rows, row, row, all_, *weights, *(all_,) * 5),
        out_specs=(rows, rows, rows, *weights, *(all_,) * 5),
        check_vma=False,
    )
```

```python
import math
import types

import jax
import jax.numpy as jnp
from jax import lax
from jax.experimental import pallas as pl
from jax.experimental.pallas import tpu as pltpu
from jax.sharding import PartitionSpec as P

D = 1024
HEADS = 8
HEAD = D // HEADS
STRIDE = 8
LBLK = 64
BF = jnp.bfloat16
F32 = jnp.float32
CROSS_SCALE = 1.0 / math.sqrt(D)
SELF_SCALE = 1.0 / math.sqrt(HEAD)
MASKED = -1e30
GELU_K = math.sqrt(2.0 / math.pi)
GELU_A = 0.044715


def mm(a, b):
    return jnp.dot(a, b, preferred_element_type=F32)


def mm_nt(a, b):
    return lax.dot_general(a, b, (((1,), (1,)), ((), ())), preferred_element_type=F32)


def mm_tn(a, b):
    return lax.dot_general(a, b, (((0,), (0,)), ((), ())), preferred_element_type=F32)


def norm_parts(x):
    center = x - jnp.mean(x, axis=-1, keepdims=True)
    r = lax.rsqrt(jnp.mean(center * center, axis=-1, keepdims=True) + 1e-05)
    return center * r, r


def norm_back(dy, x, gain):
    hat, r = norm_parts(x)
    dhat = dy * gain
    dx = r * (
        dhat
        - jnp.mean(dhat, axis=-1, keepdims=True)
        - hat * jnp.mean(dhat * hat, axis=-1, keepdims=True)
    )
    return dx, jnp.sum(dy * hat, axis=0, keepdims=True)


def gelu(u):
    return 0.5 * u * (1.0 + jnp.tanh(GELU_K * (u + GELU_A * u * u * u)))


def gelu_slope(u):
    t = jnp.tanh(GELU_K * (u + GELU_A * u * u * u))
    return 0.5 * (1.0 + t) + 0.5 * u * (1.0 - t * t) * GELU_K * (1.0 + 3.0 * GELU_A * u * u)


def intervals(lengths, offsets, deal):
    count = lengths.shape[0]
    before = jnp.arange(count)[:, None] > jnp.arange(count)[None, :]
    starts = jnp.sum(jnp.where(before, lengths[None, :], 0), axis=1)
    base = (deal[:, None] * LBLK + jnp.arange(LBLK, dtype=jnp.int32)[None, :]).reshape(-1)
    pos = base * STRIDE + offsets
    lo = jnp.max(jnp.where(starts[None, :] <= pos[:, None], starts[None, :], -1), axis=1)
    return lo, pos


def plain(
    pixels, latents, cotangent, doc_lengths, latent_offsets, block_deal,
    wq_c, wk_c, wv_c, wo_c, wu_c, wd_c, wq_s, wk_s, wv_s, wo_s, wu_s, wd_s,
    g_in, g_lat, g_cmlp, g_self, g_smlp,
):
    n = lax.axis_size("ctx")
    me = lax.axis_index("ctx")
    rows = latents.shape[1]
    npix = pixels.shape[1]
    c = pixels.shape[2]
    lo, pos = intervals(doc_lengths[0], latent_offsets[0], block_deal)
    own_lo = lax.dynamic_slice_in_dim(lo, me * rows, rows)
    own_pos = lax.dynamic_slice_in_dim(pos, me * rows, rows)
    pix_pos = me * npix + jnp.arange(npix, dtype=jnp.int32)
    mask = (lo[:, None] <= pix_pos[None, :]) & (pix_pos[None, :] <= pos[:, None])
    smask = (own_lo[:, None] <= pos[None, :]) & (pos[None, :] <= own_pos[:, None])

    wq_c, wk_c, wv_c, wo_c = (w.astype(BF) for w in (wq_c, wk_c, wv_c, wo_c))
    wk_all = lax.all_gather(wk_c, "fsdp", axis=1, tiled=True)
    wqk = lax.all_gather(mm_nt(wq_c, wk_all).astype(BF), "fsdp", axis=0, tiled=True)
    wvo = lax.psum(mm(wv_c, wo_c), "fsdp").astype(BF)
    big = jnp.stack([w.astype(BF) for w in (wu_c, wd_c, wq_s, wk_s, wv_s, wo_s, wu_s, wd_s)])
    wu1, wd1, wq, wk, wv, wo, wu3, wd3 = lax.all_gather(big, "fsdp", axis=1, tiled=True)

    xin = pixels[0].astype(F32)
    xn = (norm_parts(xin)[0] * g_in).astype(BF)
    lat = latents[0].astype(F32)
    ln = (norm_parts(lat)[0] * g_lat).astype(BF)
    qk_all = lax.all_gather(mm(ln, wqk).astype(BF), "ctx", axis=0, tiled=True)
    s = jnp.where(mask, mm_nt(qk_all, xn) * CROSS_SCALE, MASKED)
    top = jnp.max(s, axis=1, keepdims=True)
    e = lax.optimization_barrier(jnp.where(mask, jnp.exp(s - top), 0.0).astype(BF))
    total = jnp.sum(e.astype(F32), axis=1, keepdims=True)
    part = jnp.concatenate([mm(e, xn), top, total], axis=1)
    parts = lax.all_to_all(part.reshape(n, rows, c + 2), "ctx", 0, 0)
    tops = parts[:, :, c : c + 1]
    high = jnp.max(tops, axis=0)
    share = jnp.exp(tops - high[None])
    full = jnp.sum(share * parts[:, :, c + 1 :], axis=0)
    px = jnp.sum(share * parts[:, :, :c], axis=0) / full
    lse = high + jnp.log(full)
    px_low = px.astype(BF)
    h1 = lat + mm(px_low, wvo)
    n1 = (norm_parts(h1)[0] * g_cmlp).astype(BF)
    u1 = mm(n1, wu1)
    z1 = gelu(u1).astype(BF)
    h2 = h1 + mm(z1, wd1)
    n2 = (norm_parts(h2)[0] * g_self).astype(BF)
    q = mm(n2, wq).astype(BF).reshape(rows, HEADS, HEAD)
    kv = jnp.concatenate([mm(n2, wk), mm(n2, wv)], axis=1).astype(BF)
    kv = lax.all_gather(kv, "ctx", axis=0, tiled=True)
    k = kv[:, :D].reshape(n * rows, HEADS, HEAD)
    v = kv[:, D:].reshape(n * rows, HEADS, HEAD)
    ss = jnp.einsum("qhd,khd->hqk", q, k, preferred_element_type=F32) * SELF_SCALE
    ss = jnp.where(smask[None], ss, MASKED)
    se = jnp.exp(ss - jnp.max(ss, axis=-1, keepdims=True))
    ps = se / jnp.sum(se, axis=-1, keepdims=True)
    psl = ps.astype(BF)
    sa = jnp.einsum("hqk,khd->qhd", psl, v, preferred_element_type=F32)
    sa = sa.reshape(rows, D).astype(BF)
    h3 = h2 + mm(sa, wo)
    n3 = (norm_parts(h3)[0] * g_smlp).astype(BF)
    u3 = mm(n3, wu3)
    z3 = gelu(u3).astype(BF)
    layer_out = (h3 + mm(z3, wd3)).astype(BF)

    gy3 = cotangent[0]
    gu3 = (mm_nt(gy3, wd3) * gelu_slope(u3)).astype(BF)
    dx, gg_smlp = norm_back(mm_nt(gu3, wu3), h3, g_smlp)
    dh3 = gy3.astype(F32) + dx
    go3 = dh3.astype(BF)
    gas = mm_nt(go3, wo).astype(BF).reshape(rows, HEADS, HEAD)
    dps = jnp.einsum("qhd,khd->hqk", gas, v, preferred_element_type=F32)
    sdelta = jnp.sum(ps * dps, axis=-1, keepdims=True)
    dss = (ps * (dps - sdelta) * SELF_SCALE).astype(BF)
    dqs = jnp.einsum("hqk,khd->qhd", dss, k, preferred_element_type=F32)
    dqs = dqs.reshape(rows, D).astype(BF)
    dks = jnp.einsum("hqk,qhd->khd", dss, q, preferred_element_type=F32).reshape(n * rows, D)
    dvs = jnp.einsum("hqk,qhd->khd", psl, gas, preferred_element_type=F32).reshape(n * rows, D)
    dkv = lax.psum_scatter(
        jnp.concatenate([dks, dvs], axis=1), "ctx", scatter_dimension=0, tiled=True
    ).astype(BF)
    dks, dvs = dkv[:, :D], dkv[:, D:]
    dn2 = mm_nt(dqs, wq) + mm_nt(dks, wk) + mm_nt(dvs, wv)
    dx, gg_self = norm_back(dn2, h2, g_self)
    dh2 = dh3 + dx
    gy1 = dh2.astype(BF)
    gu1 = (mm_nt(gy1, wd1) * gelu_slope(u1)).astype(BF)
    dx, gg_cmlp = norm_back(mm_nt(gu1, wu1), h1, g_cmlp)
    dh1 = dh2 + dx
    go1 = dh1.astype(BF)
    gv = lax.optimization_barrier(mm_nt(go1, wvo).astype(BF))
    delta = jnp.sum(px * gv.astype(F32), axis=1, keepdims=True)
    gv_all = lax.all_gather(gv, "ctx", axis=0, tiled=True)
    stat = lax.all_gather(jnp.concatenate([lse, delta], axis=1), "ctx", axis=0, tiled=True)
    p = jnp.where(mask, jnp.exp(s - stat[:, :1]), 0.0)
    ds = (p * (mm_nt(gv_all, xn) - stat[:, 1:]) * CROSS_SCALE).astype(BF)
    dxn = mm_tn(ds, qk_all) + mm_tn(p.astype(BF), gv_all)
    dpix, gg_in = norm_back(dxn, xin, g_in)
    dqk = lax.psum_scatter(mm(ds, xn), "ctx", scatter_dimension=0, tiled=True).astype(BF)
    dx, gg_lat = norm_back(mm_nt(dqk, wqk), lat, g_lat)
    dlat = dh1 + dx

    e_sum = lax.psum_scatter(mm_tn(ln, dqk), "fsdp", scatter_dimension=0, tiled=True)
    e_sum, f_sum = lax.psum((e_sum, lax.psum(mm_tn(px_low, go1), "fsdp")), "ctx")
    e_sum, f_sum = e_sum.astype(BF), f_sum.astype(BF)
    d_wq_c = mm(e_sum, wk_all)
    d_wk_c = lax.psum_scatter(mm_tn(e_sum, wq_c), "fsdp", scatter_dimension=1, tiled=True)
    d_wv_c = mm_nt(f_sum, wo_c)
    d_wo_c = mm_tn(wv_c, f_sum)
    pairs = ((n1, gu1), (z1, gy1), (n2, dqs), (n2, dks), (n2, dvs), (sa, go3), (n3, gu3), (z3, gy3))
    d_big = [
        lax.psum(lax.psum_scatter(mm_tn(a, b), "fsdp", scatter_dimension=0, tiled=True), "ctx")
        for a, b in pairs
    ]
    gains = lax.psum(jnp.concatenate([gg_in[0], gg_lat[0], gg_cmlp[0], gg_self[0], gg_smlp[0]]), ("ctx", "fsdp"))
    return (
        layer_out[None], dpix[None], dlat[None], d_wq_c, d_wk_c, d_wv_c, d_wo_c, *d_big,
        gains[:c], gains[c : c + D], gains[c + D : c + 2 * D],
        gains[c + 2 * D : c + 3 * D], gains[c + 3 * D :],
    )


CP = 384
CR = 288
CX = 272
PARITY_ROWS = 4 * 128


def fused(
    pix, lat, cot, lengths, offsets, deal, g_in, g_lat, g_cmlp, g_self, g_smlp,
    wq_c, wk_c, wv_c, wo_c, wu_1, wd_1, wq_s, wk_s, wv_s, wo_s, wu_3, wd_3,
    layer_out, d_pix, d_lat, d_big, d_wk, d_wv, d_gain,
    *scratch,
):
    s = types.SimpleNamespace(**dict(zip(SCRATCH, scratch)))
    c, z = lax.axis_index("ctx"), lax.axis_index("fsdp")
    k, p = lax.rem(c, 2), lax.div(c, 2)
    k2 = 1 - k

    def flip(v, d):
        low, high = lax.rem(v, 2), lax.div(v, 2)
        return (1 - low if d & 1 else low) + 2 * (1 - high if d & 2 else high)

    chip = {d: flip(p, d) for d in (1, 2, 3)}
    plane = {d: flip(z, d) for d in (1, 2, 3)}
    sib = {"ctx": 2 * p + k2}

    def peer(d):
        return {"ctx": 2 * chip[d] + k}

    def across(d):
        return {"ctx": 2 * chip[d] + k2}

    def level(d):
        return {"fsdp": plane[d]}

    used = [0, 0]
    sends = []

    def make(src, dst, target, slot=None):
        if slot is None:
            slot = used[0]
            used[0] += 1
        send = used[1]
        used[1] += 1
        return pltpu.make_async_remote_copy(
            src_ref=src, dst_ref=dst, send_sem=s.ssem.at[send], recv_sem=s.rsem.at[slot],
            device_id=target, device_id_type=pl.DeviceIdType.MESH,
        )

    def put(src, dst, target):
        copy = make(src, dst, target)
        copy.start()
        sends.append((None, copy))
        return copy

    def sent(copies):
        for copy in copies.values() if isinstance(copies, dict) else copies:
            copy.wait_send()
            sends[:] = [pair for pair in sends if pair[1] is not copy]

    def to_peers(src_of, dst_of, order=(3, 1, 2)):
        return {d: put(src_of(d), dst_of(d), peer(d)) for d in order}

    def to_planes(src_of, dst_of):
        return {d: put(src_of(d), dst_of(d), level(d)) for d in (1, 2, 3)}

    def arrived(copies):
        for copy in copies.values() if isinstance(copies, dict) else copies:
            copy.wait_recv()

    locals_ = [0]

    def fetch(src, dst):
        copy = pltpu.make_async_copy(src, dst, s.lsem.at[locals_[0]])
        locals_[0] += 1
        copy.start()
        return copy

    def spread(part_of):
        mine = [part_of(p, h) for h in range(2)]
        copies = {(d, h): put(mine[h], mine[h], peer(d)) for d, h in ((1, 0), (2, 1), (1, 1), (2, 0))}
        return part_of, copies, []

    def relay(state):
        part_of, copies, on = state
        for d, h in ((1, 0), (2, 1)):
            copies[d, h].wait_recv()
            part = part_of(chip[d], h)
            on.append(put(part, part, peer(3 - d)))

    def near(state, d):
        state[1][d, 2 - d].wait_recv()

    def far(state):
        arrived(state[2])

    def all_of(state):
        near(state, 1)
        near(state, 2)
        far(state)

    def fold(part_of, into):
        first = [put(part_of(3, h), into(0, h), peer(1 + h)) for h in range(2)]
        near_ = [put(part_of(1 + h, h), into(1, h), peer(1 + h)) for h in range(2)]
        return part_of, into, first, near_

    def fold_on(state):
        part_of, into, first, near_ = state
        for h in range(2):
            first[h].wait_recv()
            part = part_of(2 - h, h)
            part[...] = (part[...].astype(F32) + into(0, h)[...].astype(F32)).astype(BF)
            near_.append(put(part, into(2, h), peer(2 - h)))

    def gather(slot_of, half_of=None):
        own = put(slot_of(c), slot_of(c), sib)
        if half_of is None:
            return slot_of, to_peers(lambda d: slot_of(c), lambda d: slot_of(c)), [own]
        return slot_of, spread(lambda q, h: half_of(2 * q + k, h)), [own]

    def pass_on(state):
        slot_of, copies, to_sib = state
        if not isinstance(copies, dict):
            all_of(copies)
        for d in (1, 2, 3):
            if isinstance(copies, dict):
                copies[d].wait_recv()
            there = slot_of(2 * chip[d] + k)
            to_sib.append(put(there, there, sib))
        return to_sib

    def to_plane(part):
        return [put(part, part, to) for to in (*(peer(d) for d in (1, 2, 3)), *(across(d) for d in (1, 2, 3)), sib)]

    for j in range(4):
        s.wk[j, 256:CP, :] = jnp.zeros((CP - 256, 256), BF)
    s.wv_z[256:CP, :] = jnp.zeros((CP - 256, 256), BF)
    for j in range(2):
        s.xt[j, 256:CP, :] = jnp.zeros((CP - 256, 1024), BF)
    for j in range(8):
        s.wvo[j, CR:CP, :] = jnp.zeros((CP - CR, 128), BF)
    barrier = pltpu.get_barrier_semaphore()
    near_by = (sib, *(across(d) for d in (1, 2, 3)), *(peer(d) for d in (1, 2, 3)))
    for target in (*near_by, *(level(d) for d in (1, 2, 3))):
        pl.semaphore_signal(barrier, inc=1, device_id=target, device_id_type=pl.DeviceIdType.MESH)
    lanes = pl.ds(pl.multiple_of(c * 128, 128), 128)
    quarter = pl.ds(pl.multiple_of(k * 128 + p * 32, 32), 32)
    f_wk = [fetch(wk_c.at[0:256], s.u1.at[0]), fetch(wk_c.at[256:261], s.u1.at[1, 0:5])]
    f_wq = [fetch(wq_c.at[128 * i : 128 * (i + 1)], s.hpa.at[i]) for i in range(2)]
    f_wv = [fetch(wv_c.at[0:256], s.u3.at[0]), fetch(wv_c.at[256:261], s.u3.at[1, 0:5])]
    f_wo = [fetch(wo_c.at[128 * i : 128 * (i + 1)], s.hpb.at[i]) for i in range(2)]

    def early(i):
        return (s.dh if i < 8 else s.hxb).at[:, 128 * (i % 8) : 128 * (i % 8) + 128]

    f_u = [
        fetch(w.at[128 * j : 128 * (j + 1), lanes], early(2 * i + j))
        for i, w in enumerate((wu_1, wu_3, wq_s, wk_s, wv_s))
        for j in range(2)
    ]
    f_d = [fetch(w.at[quarter, :], s.h3.at[32 * i : 32 * (i + 1)]) for i, w in enumerate((wd_1, wo_s))]
    f_d3 = fetch(wd_3.at[pl.ds(pl.multiple_of(k * 128, 128), 128), :], s.hxa)
    pl.semaphore_wait(barrier, 10)

    for copy in f_wk:
        copy.wait()
    s.wk[z, 0:256, :] = s.u1[0].astype(BF)
    s.wk[z, 256:261, :] = s.u1[1, 0:5, :].astype(BF)
    half = pl.ds(pl.multiple_of(k * 144, 16), 144)
    wk_z = to_planes(lambda d: s.wk.at[z, half], lambda d: s.wk.at[z, half])
    for copy in f_u:
        copy.wait()
    own_z = pl.ds(pl.multiple_of(z * 256, 256), 256)
    for j in range(2):
        half_z = pl.ds(pl.multiple_of(z * 256 + 128 * j, 128), 128)
        s.wu1[p, half_z, :] = early(j)[...].astype(BF)
    wu1_z = to_planes(lambda d: s.wu1.at[p, own_z], lambda d: s.wu1.at[p, own_z])
    s.cpair[k] = cot[...]
    x_cot = put(s.cpair.at[k], s.cpair.at[k], sib)

    order = lax.broadcasted_iota(jnp.int32, (8, D), 1)
    block = lax.div(order, LBLK)
    base = jnp.zeros((8, D), jnp.int32)
    for i in range(D // LBLK):
        base = jnp.where(block == i, deal[i], base)
    pos_r = (base * LBLK + lax.rem(order, LBLK)) * STRIDE + offsets[...]
    lo_r = jnp.zeros((8, D), jnp.int32)
    start = lengths[0, 0]
    for i in range(1, lengths.shape[1]):
        lo_r = jnp.where(start <= pos_r, start, lo_r)
        start = start + lengths[0, i]
    s.pos[...] = pos_r
    top_row = lax.broadcasted_iota(jnp.int32, (128, 128), 0) == 0
    for b in range(8):
        cols = slice(128 * b, 128 * (b + 1))
        both_rows = jnp.where(top_row, lo_r[0:1, cols], pos_r[0:1, cols]).astype(F32)
        s.span[cols, :] = both_rows.T.astype(jnp.int32)
    s.row[0:1, 0:256] = g_in[0:256].reshape(1, 256)
    s.row[0:1, 256:261] = g_in[256:261].reshape(1, 5)
    s.gcol[...] = jnp.broadcast_to(s.row[0:1, :], (128, CP)).T

    def norm_pixels(t):
        cols = slice(256 * t, 256 * (t + 1))
        normed = (norm_cols(pix[:, cols].astype(F32))[0] * s.gcol[0:261, 0:1]).astype(BF)
        s.xt[k, 0:256, cols] = normed[0:256]
        s.xt[k, 256:261, cols] = normed[256:261]

    for t in range(4):
        norm_pixels(t)
    ln = (norm_parts(lat[...].astype(F32))[0] * g_lat[...]).astype(BF)
    s.lnp[p] = ln
    ln_in = spread(lambda q, h: s.lnp.at[q, 64 * h : 64 * h + 64])
    for i in range(2):
        f_wq[i].wait()
        s.wq_z[128 * i : 128 * (i + 1), :] = s.hpa[i].astype(BF)
    wk_s_in = []
    for d in (1, 2, 3):
        wk_z[d].wait_recv()
        there = s.wk.at[plane[d], half]
        wk_s_in.append(put(there, there, sib))
    relay(ln_in)
    for copy in f_wv:
        copy.wait()
    s.wv_z[0:256, :] = s.u3[0].astype(BF)
    s.wv_z[256:261, :] = s.u3[1, 0:5, :].astype(BF)
    for i in range(2):
        f_wo[i].wait()
        s.wo_z[128 * i : 128 * (i + 1), :] = s.hpb[i].astype(BF)
    wvo_part = mm(s.wv_z[...], s.wo_z[:, lanes])
    s.wvz[0] = wvo_part[:CR].astype(BF)
    arrived(wk_s_in)
    own_rows = pl.ds(pl.multiple_of(k * 128, 128), 128)
    part = jnp.zeros((128, CP), F32)
    for j in range(4):
        part += mm_nt(s.wq_z[own_rows, 256 * j : 256 * (j + 1)], s.wk[j])
    s.wqk[z, k] = part.astype(BF)
    wqk_z = to_planes(lambda d: s.wqk.at[z, k], lambda d: s.wqk.at[z, k])
    wqk_s = [put(s.wqk.at[z, k], s.wqk.at[z, k], sib)]
    wvo_z = to_planes(lambda d: s.wvz.at[0], lambda d: s.wvz.at[d])
    x_xn = put(s.xt.at[k, 0:CX], s.xt.at[k, 0:CX], sib)
    for copy in f_d:
        copy.wait()
    s.wd1[z, p] = s.h3[0:32, :].astype(BF)
    wd1_z = to_planes(lambda d: s.wd1.at[z, p], lambda d: s.wd1.at[z, p])

    for j in range(2):
        half_z = pl.ds(pl.multiple_of(z * 256 + 128 * j, 128), 128)
        s.wu3[p, half_z, :] = early(2 + j)[...].astype(BF)
        for i in range(3):
            s.wqkv[i, k, half_z, :] = early(4 + 2 * i + j)[...].astype(BF)
    s.woz[z] = s.h3[32:64, :].astype(BF)
    f_d3.wait()
    s.wd3[z] = s.hxa[...].astype(BF).reshape(4, 32, D)
    arrived(wu1_z)
    wu1_in = spread(lambda q, h: s.wu1.at[q, 512 * h : 512 * h + 512])
    for d in (1, 2, 3):
        wqk_z[d].wait_recv()
        there = s.wqk.at[plane[d], k]
        wqk_s.append(put(there, there, sib))
    relay(wu1_in)
    arrived(wqk_s)
    wqk = s.wqk[...].reshape(D, CP)
    s.qk[p] = mm(ln, wqk).astype(BF)
    qk_in = to_peers(lambda d: s.qk.at[p], lambda d: s.qk.at[p])
    arrived(wvo_z)
    s.wvo[c, 0:CR, :] = sum(s.wvz[d].astype(F32) for d in range(4)).astype(BF)

    def wvo_slot(i):
        return s.wvo.at[i, 0:CR]

    wvo_in = gather(wvo_slot)
    wu3_z = to_planes(lambda d: s.wu3.at[p, own_z], lambda d: s.wu3.at[p, own_z])
    qkv_z = to_planes(lambda d: s.wqkv.at[:, k, own_z], lambda d: s.wqkv.at[:, k, own_z])
    wo_z = to_planes(lambda d: s.woz.at[z], lambda d: s.woz.at[z])
    wd3_z = to_planes(lambda d: s.wd3.at[z], lambda d: s.wd3.at[z])
    x_xn.wait_recv()

    wide = lax.broadcasted_iota(jnp.int32, (128, 1024), 1)
    lane = lax.broadcasted_iota(jnp.int32, (128, CP), 1)

    def cross_block(q):
        rows = pl.ds(pl.multiple_of((2 * q + k) * 128, 128), 128)
        low, high = s.span[rows, 0:1], s.span[rows, 1:2]
        scores = []
        for h in range(2):
            at = wide + (2 * p + h) * 1024
            sc = mm(s.qk[q], s.xt[h]) * CROSS_SCALE
            scores.append(jnp.where((at >= low) & (at <= high), sc, MASKED))
        top = jnp.maximum(*(jnp.max(sc, axis=1, keepdims=True) for sc in scores))
        total = jnp.zeros((128, 1), F32)
        acc = jnp.zeros((128, CP), F32)
        for h in range(2):
            e = jnp.where(scores[h] > 0.5 * MASKED, jnp.exp(scores[h] - top), 0.0).astype(BF)
            s.ee[2 * q + h] = e
            total += jnp.sum(e.astype(F32), axis=1, keepdims=True)
            acc += mm_nt(e, s.xt[h])
        s.tops[q] = jnp.broadcast_to(top, (128, 128))
        s.pxs[q] = tag(acc, lane, top, total)

    cross_block(p)
    px_in = {}
    for d in (1, 2, 3):
        qk_in[d].wait_recv()
        cross_block(chip[d])
        px_in[d] = put(s.pxs.at[chip[d]], s.pxr.at[d - 1], peer(d))
    wvo_s = pass_on(wvo_in)
    arrived(wd1_z)
    wd1_in = spread(lambda q, h: s.wd1.at[2 * h : 2 * h + 2, q])
    arrived(px_in)
    found = [untag(s.pxs[p], lane)] + [untag(s.pxr[i], lane) for i in range(3)]
    high = found[0][1]
    for f in found[1:]:
        high = jnp.maximum(high, f[1])
    px, total = jnp.zeros((128, CP), F32), jnp.zeros((128, 1), F32)
    for val, top, tot in found:
        share = jnp.exp(top - high)
        px += share * val
        total += share * tot
    px = px / total
    s.px[...] = px
    lse = high + jnp.log(total)
    s.pxl[...] = px.astype(BF)
    relay(wd1_in)
    arrived(wvo_s)
    lat_f = lat[...].astype(F32)
    pxl = s.pxl[...]
    for j in range(4):
        cols = slice(256 * j, 256 * (j + 1))
        w = jnp.concatenate([s.wvo[2 * j], s.wvo[2 * j + 1]], axis=1)
        s.h1[:, cols] = lat[:, cols].astype(F32) + mm(pxl, w)

    def mlp_start(h_ref, gain, npair):
        npair[k] = (norm_parts(h_ref[...])[0] * gain[...]).astype(BF)
        return put(npair.at[k], npair.at[k], sib)

    def mlp_up(npair, wu, u, zb):
        rows = npair[...].reshape(256, D)
        for j in range(2):
            w = jnp.concatenate([wu[2 * j], wu[2 * j + 1]], axis=1)
            hidden = mm(rows, w)
            u[j] = hidden
            zb[j] = gelu(hidden).astype(BF)

    def mlp_down(zb, wd, hp, hx):
        for t in range(4):
            cols = slice(256 * t, 256 * (t + 1))
            acc = mm(zb[0], wd[0:2, :, :, cols].reshape(256, 256))
            acc += mm(zb[1], wd[2:4, :, :, cols].reshape(256, 256))
            hp[:, :, cols] = acc.reshape(2, 128, 256)
        return put(hp.at[k2], hx, sib)

    def mlp_back(gpair, wu, wd, u, gub, hp, hs, hx):
        rows = gpair[...].reshape(256, D)
        for j in range(2):
            gz = mm_nt(rows, wd[2 * j : 2 * j + 2].reshape(256, D))
            gub[j] = (gz * gelu_slope(u[j])).astype(BF)
        for t in range(4):
            cols = slice(256 * t, 256 * (t + 1))
            acc = jnp.zeros((256, 256), F32)
            for j in range(2):
                w = jnp.concatenate([wu[2 * j, cols, :], wu[2 * j + 1, cols, :]], axis=1)
                acc += mm_nt(gub[j], w)
            hp[:, :, cols] = acc.reshape(2, 128, 256)
        hs[...] = hp[k2].astype(BF)
        return put(hs, hx, sib)

    def up_partial(npair, gub):
        for j in range(2):
            for t in range(4):
                cols = slice(256 * t, 256 * (t + 1))
                g = mm_tn(npair[:, :, cols].reshape(256, 256), gub[j]).astype(BF)
                s.gsu[2 * j, cols, :] = g[:, :128]
                s.gsu[2 * j + 1, cols, :] = g[:, 128:]

    def up_fold():
        return fold(
            lambda d, h: s.gsu.at[chip[d], 512 * h : 512 * h + 512],
            lambda i, h: s.gru.at[i, 512 * h : 512 * h + 512],
        )

    def down_partial(zb, gpair):
        for j in range(2):
            for t in range(4):
                cols = slice(256 * t, 256 * (t + 1))
                g = mm_tn(zb[j], gpair[:, :, cols].reshape(256, 256)).astype(BF)
                s.gsd[2 * j : 2 * j + 2, :, :, cols] = g.reshape(2, 4, 32, 256)

    def down_fold():
        return fold(
            lambda d, h: s.gsd.at[2 * h : 2 * h + 2, chip[d]],
            lambda i, h: s.grd.at[i, 2 * h : 2 * h + 2],
        )

    def up_to_planes(up, zs, zr):
        arrived(up[3])
        total = s.gsu[p].astype(F32)
        for i in (1, 2):
            total += s.gru[i].astype(F32)
        zs[...] = total.astype(BF)
        return to_planes(
            lambda d: zs.at[pl.ds(pl.multiple_of(plane[d] * 256, 256), 256)], lambda d: zr.at[d - 1]
        )

    def down_to_planes(down, zs, zr):
        arrived(down[3])
        total = s.gsd[:, p].astype(F32)
        for i in (1, 2):
            total += s.grd[i].astype(F32)
        zs[...] = total.astype(BF)
        return to_planes(lambda d: zs.at[plane[d]], lambda d: zr.at[d - 1])

    def up_total(copies, zs, zr, ag):
        arrived(copies)
        total = zs[own_z, :].astype(F32)
        for i in range(3):
            total += zr[i].astype(F32)
        ag[c] = total.astype(BF)
        return gather(lambda i: ag.at[i], lambda i, h: ag.at[i, 128 * h : 128 * h + 128])

    def row_slot(ag):
        return lambda i: ag.at[lax.rem(i, 2), lax.div(i, 2)]

    def row_half(ag):
        return lambda i, h: ag.at[lax.rem(i, 2), lax.div(i, 2), 16 * h : 16 * h + 16]

    def down_total(copies, zs, zr, ag):
        arrived(copies)
        total = zs[z].astype(F32)
        for i in range(3):
            total += zr[i].astype(F32)
        ag[k, p] = total.astype(BF)
        return gather(row_slot(ag), row_half(ag))

    outs = []

    def out_cols(ag, w):
        for j in range(8):
            outs.append(fetch(ag.at[j], d_big.at[w, :, 128 * j : 128 * (j + 1)]))

    def out_rows(ag, w):
        for kk in range(2):
            for q in range(4):
                at = 128 * kk + 32 * q
                outs.append(fetch(ag.at[kk, q], d_big.at[w, at : at + 32, :]))

    x_n1 = mlp_start(s.h1, g_cmlp, s.n1)
    arrived(wu3_z)
    wu3_in = spread(lambda q, h: s.wu3.at[q, 512 * h : 512 * h + 512])
    all_of(wu1_in)
    x_n1.wait_recv()
    mlp_up(s.n1, s.wu1, s.u1, s.z1)
    all_of(wd1_in)
    x_h1 = mlp_down(s.z1, s.wd1, s.hpa, s.hxa)
    relay(wu3_in)
    arrived(qkv_z)
    x_qkv = put(s.wqkv.at[:, k], s.wqkv.at[:, k], sib)
    x_h1.wait_recv()
    s.h2[...] = s.h1[...] + s.hpa[k] + s.hxa[...]

    s.n2[p] = (norm_parts(s.h2[...])[0] * g_self[...]).astype(BF)
    n2_in = spread(lambda q, h: s.n2.at[q, 64 * h : 64 * h + 64])
    x_qkv.wait_recv()

    def project(q):
        rows = s.n2[q]
        for i in range(3):
            w = jnp.concatenate([s.wqkv[i, 0], s.wqkv[i, 1]], axis=1)
            s.pair[...] = mm(rows, w).astype(BF).reshape(128, 256)
            for h in range(2):
                s.heads[h, q, i] = s.pair[:, 128 * h : 128 * (h + 1)]
        s.mine[2 * q + k] = s.heads[k, q]
        return put(s.heads.at[k2, q], s.mine.at[2 * q + k], sib)

    qkv_in = [project(p)]
    relay(n2_in)
    for d in (1, 2):
        near(n2_in, d)
        qkv_in.append(project(chip[d]))
    far(n2_in)
    qkv_in.append(project(chip[3]))
    arrived(wo_z)
    piece = pl.ds(pl.multiple_of(32 * p, 32), 32)
    s.wo[k, piece, :] = s.woz[p]
    wo_in = to_peers(lambda d: s.woz.at[chip[d]], lambda d: s.wo.at[k, piece])
    arrived(qkv_in)

    def attend(b):
        rows = pl.ds(pl.multiple_of(b * 128, 128), 128)
        keys = s.mine[:, 1].reshape(D, 128)
        sc = mm_nt(s.mine[b, 0], keys) * SELF_SCALE
        at = s.pos[0:1, :]
        sc = jnp.where((at >= s.span[rows, 0:1]) & (at <= s.span[rows, 1:2]), sc, MASKED)
        e = jnp.exp(sc - jnp.max(sc, axis=1, keepdims=True))
        low = (e / jnp.sum(e, axis=1, keepdims=True)).astype(BF)
        s.a1[b] = low
        return mm(low, s.mine[:, 2].reshape(D, 128)).astype(BF)

    def other_rows(q, carry):
        s.send[q] = attend(2 * q + k2)
        return carry

    def own_parity(q, carry):
        s.aspar[q, k] = attend(2 * q + k)
        return carry

    lax.fori_loop(0, 4, other_rows, 0)
    x_as = put(s.send, s.aspar.at[:, k], sib)
    arrived(wo_in)
    x_wo = put(s.wo.at[k], s.wo.at[k], sib)
    lax.fori_loop(0, 4, own_parity, 0)
    x_wo.wait_recv()
    x_as.wait_recv()

    def both(ref, q):
        return jnp.concatenate([ref[q, 0], ref[q, 1]], axis=1)

    for d in (3, 1, 2):
        s.outp[d - 1] = mm(both(s.aspar, chip[d]), s.wo[...].reshape(256, D)).astype(BF)

    def rows_out(d, h):
        return s.outp.at[d - 1, 64 * h : 64 * h + 64]

    def rows_in(i, h):
        return s.outr.at[i, 64 * h : 64 * h + 64]

    out_in = fold(rows_out, rows_in)
    s.h3[...] = s.h2[...] + mm(both(s.aspar, p), s.wo[...].reshape(256, D))
    fold_on(out_in)
    arrived(out_in[3])
    s.h3[...] += s.outr[1].astype(F32) + s.outr[2].astype(F32)

    x_n3 = mlp_start(s.h3, g_smlp, s.n3)
    all_of(wu3_in)
    x_n3.wait_recv()
    mlp_up(s.n3, s.wu3, s.u3, s.z3)
    arrived(wd3_z)
    x_cot.wait_recv()
    sent([x_h1])
    x_d3 = mlp_back(s.cpair, s.wu3, s.wd3, s.u3, s.gu3, s.hpa, s.hs, s.hr)
    x_h3 = mlp_down(s.z3, s.wd3, s.hpb, s.hxb)
    x_d3.wait_recv()
    dx, gg_smlp = norm_back(s.hpa[k] + s.hr[...].astype(F32), s.h3[...], g_smlp[...])
    dh3 = cot[...].astype(F32) + dx
    s.dh[...] = dh3
    s.go[p] = dh3.astype(BF)
    go_in = spread(lambda q, h: s.go.at[q, 64 * h : 64 * h + 64])
    x_h3.wait_recv()
    layer_out[...] = (s.h3[...] + s.hpb[k] + s.hxb[...]).astype(BF)

    def pull_out(q):
        g = mm_nt(s.go[q], s.wo[...].reshape(256, D)).astype(BF)
        s.pair[...] = g
        for h in range(2):
            s.gheads[h, q] = s.pair[:, 128 * h : 128 * (h + 1)]
        s.gmine[2 * q + k] = s.gheads[k, q]
        return put(s.gheads.at[k2, q], s.gmine.at[2 * q + k], sib)

    gas_in = [pull_out(p)]
    relay(go_in)
    up_partial(s.n3, s.gu3)
    s.gsu_own[...] = s.gsu[:, own_z, :]
    g3u_z = to_planes(
        lambda d: s.gsu.at[:, pl.ds(pl.multiple_of(plane[d] * 256, 256), 256)], lambda d: s.zg.at[d - 1]
    )
    for d in (1, 2):
        near(go_in, d)
        gas_in.append(pull_out(chip[d]))
    far(go_in)
    gas_in.append(pull_out(chip[3]))
    down_partial(s.z3, s.cpair)
    g3d = down_fold()
    arrived(gas_in)

    def attend_back(b, carry):
        dps = mm_nt(s.gmine[b], s.mine[:, 2].reshape(D, 128))
        probs = s.a1[b].astype(F32)
        delta = jnp.sum(probs * dps, axis=1, keepdims=True) / jnp.sum(probs, axis=1, keepdims=True)
        dss = (probs * (dps - delta) * SELF_SCALE).astype(BF)
        s.a2[b] = dss
        s.heads[lax.div(b, 4), lax.rem(b, 4), 0] = mm(dss, s.mine[:, 1].reshape(D, 128)).astype(BF)
        return carry

    sent(qkv_in)
    lax.fori_loop(0, 8, attend_back, 0)
    fold_on(g3d)
    for t in range(4):
        cols = slice(256 * t, 256 * (t + 1))
        dk = mm_tn(s.a2[:, :, cols].reshape(D, 256), s.mine[:, 0].reshape(D, 128))
        dv = mm_tn(s.a1[:, :, cols].reshape(D, 256), s.gmine[...].reshape(D, 128))
        two = slice(2 * (t % 2), 2 * (t % 2) + 2)
        s.heads[t // 2, two, 1] = dk.astype(BF).reshape(2, 128, 128)
        s.heads[t // 2, two, 2] = dv.astype(BF).reshape(2, 128, 128)

    def sort(q, carry):
        high, low = lax.div(q, 2), 2 * lax.rem(q, 2)
        s.dsend[q] = s.heads[high, low + k2]
        for i in range(3):
            s.dpar[q, i, k] = s.heads[high, low + k, i]
        return carry

    lax.fori_loop(0, 4, sort, 0)
    x_dp = put(s.dsend, s.dpar.at[:, :, k], sib)
    g3d_z = down_to_planes(g3d, s.sd3, s.zd3)
    x_dp.wait_recv()

    def pull_in(q, write):
        for t in range(4):
            cols = slice(256 * t, 256 * (t + 1))
            acc = jnp.zeros((128, 256), F32)
            for i in range(3):
                w = jnp.concatenate([s.wqkv[i, 0, cols, :], s.wqkv[i, 1, cols, :]], axis=1)
                acc += mm_nt(jnp.concatenate([s.dpar[q, i, 0], s.dpar[q, i, 1]], axis=1), w)
            write(cols, acc)

    sent(out_in[2])
    sent(out_in[3])
    for d in (3, 1, 2):

        def write(cols, acc):
            s.outp[d - 1, :, cols] = acc.astype(BF)

        pull_in(chip[d], write)
    dn_in = fold(rows_out, rows_in)

    def write(cols, acc):
        s.hxb[:, cols] = acc

    pull_in(p, write)

    def project_grad(i):
        g = jnp.concatenate([s.dpar[:, i, 0].reshape(PARITY_ROWS, 128), s.dpar[:, i, 1].reshape(PARITY_ROWS, 128)], axis=1)
        for t in range(4):
            cols = slice(256 * t, 256 * (t + 1))
            w = mm_tn(s.n2[:, :, cols].reshape(PARITY_ROWS, 256), g).astype(BF)
            for h in range(2):
                s.pg[i, h, cols, :] = w[:, 128 * h : 128 * (h + 1)]
        return put(s.pg.at[i, k2], s.pgr.at[i], sib)

    def project_planes(i):
        x_pg[i].wait_recv()
        s.pg[i, k] = (s.pg[i, k].astype(F32) + s.pgr[i].astype(F32)).astype(BF)
        return to_planes(
            lambda d: s.pg.at[i, k, pl.ds(pl.multiple_of(plane[d] * 256, 256), 256)],
            lambda d: s.zq.at[d - 1, i],
        )

    x_pg = [project_grad(0)]
    fold_on(dn_in)
    x_pg.append(project_grad(1))
    pg_z = [project_planes(0)]
    x_pg.append(project_grad(2))
    pg_z.append(project_planes(1))
    g = jnp.concatenate([s.aspar[:, 0].reshape(PARITY_ROWS, 128), s.aspar[:, 1].reshape(PARITY_ROWS, 128)], axis=1)
    for t in range(4):
        cols = slice(256 * t, 256 * (t + 1))
        w = mm_tn(g, s.go[:, :, cols].reshape(PARITY_ROWS, 256)).astype(BF)
        s.pgo[:, :, cols] = w.reshape(2, 128, 256)
    x_pgo = put(s.pgo.at[k2], s.pgor, sib)
    arrived(dn_in[3])
    dn2 = s.hxb[...] + s.outr[1].astype(F32) + s.outr[2].astype(F32)
    dx, gg_self = norm_back(dn2, s.h2[...], g_self[...])
    s.dh[...] += dx

    s.gpair[k] = s.dh[...].astype(BF)
    x_g = put(s.gpair.at[k], s.gpair.at[k], sib)
    pg_z.append(project_planes(2))
    x_g.wait_recv()
    sent([x_d3])
    x_d1 = mlp_back(s.gpair, s.wu1, s.wd1, s.u1, s.gu1, s.hpa, s.hs, s.hr)
    x_pgo.wait_recv()
    s.pgo[k] = (s.pgo[k].astype(F32) + s.pgor[...].astype(F32)).astype(BF)
    s.wz[p] = s.pgo[k, piece, :]
    pgo_in = to_peers(
        lambda d: s.pgo.at[k, pl.ds(pl.multiple_of(32 * chip[d], 32), 32)], lambda d: s.wz.at[p]
    )
    sent(g3d[2])
    sent(g3d[3])
    down_partial(s.z1, s.gpair)
    g1d = down_fold()
    x_d1.wait_recv()
    dx, gg_cmlp = norm_back(s.hpa[k] + s.hr[...].astype(F32), s.h1[...], g_cmlp[...])
    dh1 = s.dh[...] + dx
    s.dh[...] = dh1

    go1 = dh1.astype(BF)
    gv = jnp.zeros((128, CP), F32)
    for j in range(4):
        w = jnp.concatenate([s.wvo[2 * j], s.wvo[2 * j + 1]], axis=1)
        gv += mm_nt(go1[:, 256 * j : 256 * (j + 1)], w)
    gv = gv.astype(BF).astype(F32)
    delta = jnp.sum(jnp.where(lane < 261, s.px[...] * gv, 0.0), axis=1, keepdims=True)
    s.gv[p] = tag(gv, lane, lse, delta)
    gv_in = spread(lambda q, h: s.gv.at[q, 64 * h : 64 * h + 64])
    arrived(pgo_in)
    pgo_z = to_planes(lambda d: s.wz.at[plane[d]], lambda d: s.zo.at[d - 1])
    fold_on(g1d)
    for j in range(4):
        f_part = mm_tn(s.pxl[...], go1[:, 256 * j : 256 * (j + 1)])[:CR].astype(BF)
        s.fst[j, 0] = f_part[:, :128]
        s.fst[j, 1] = f_part[:, 128:]
    sent(wvo_in[1])
    sent(wvo_s)
    x_f = put(s.fst.at[:, k2], s.fsr, sib)
    sent(g3u_z)
    up_partial(s.n1, s.gu1)
    g1u = up_fold()
    def cross_back(q):
        val, last, delta = untag(s.gv[q], lane)
        ratio = jnp.exp(s.tops[q][:, 0:1] - last)
        s.gvr[q] = (val * ratio).astype(BF)
        acc = jnp.zeros((128, CP), F32)
        for h in range(2):
            dp = mm(s.gv[q], s.xt[h])
            ds = (s.ee[2 * q + h].astype(F32) * ((dp - delta) * (ratio * CROSS_SCALE))).astype(BF)
            s.a2[2 * q + h] = ds
            acc += mm_nt(ds, s.xt[h])
        s.pxs[q] = acc.astype(BF)
        return acc

    sent(px_in)
    s.dqk[...] = cross_back(p)
    relay(gv_in)
    x_f.wait_recv()
    s.fst[:, k] = (s.fst[:, k].astype(F32) + s.fsr[...].astype(F32)).astype(BF)
    f_in = fold(
        lambda d, h: s.fst.at[chip[d], k, 144 * h : 144 * h + 144], lambda i, h: s.fpr.at[i, 144 * h : 144 * h + 144]
    )
    for d in (1, 2):
        near(gv_in, d)
        cross_back(chip[d])
    far(gv_in)
    cross_back(chip[3])
    g1d_z = down_to_planes(g1d, s.sd1, s.zd1)
    fold_on(g1u)
    all_of(ln_in)
    for j in range(4):
        e = mm_tn(s.lnp[:, :, 256 * j : 256 * (j + 1)].reshape(PARITY_ROWS, 256), s.pxs[...].reshape(PARITY_ROWS, CP))
        s.est[j] = e.astype(BF).reshape(4, 2, 32, CP)
    x_e = put(s.est.at[:, :, k2], s.esr, sib)
    dq_in = fold(
        lambda d, h: s.pxs.at[chip[d], 64 * h : 64 * h + 64], lambda i, h: s.pxr.at[i, 64 * h : 64 * h + 64]
    )
    fold_on(f_in)
    for q in range(4):
        for j in range(3):
            cols = slice(128 * j, 128 * (j + 1))
            s.a1[j, :, 128 * q : 128 * (q + 1)] = s.qk[q, :, cols].T
            s.a1[j, :, 512 + 128 * q : 512 + 128 * (q + 1)] = s.gvr[q, :, cols].T

    def pixel_cols(h, t):
        cols = slice(256 * t, 256 * (t + 1))
        parts = [s.a2[2 * q + h, :, cols] for q in range(4)] + [s.ee[2 * q + h, :, cols] for q in range(4)]
        return mm(s.a1[0:3].reshape(CP, 1024), jnp.concatenate(parts, axis=0))

    for t in range(4):
        s.dxs[:, 256 * t : 256 * (t + 1)] = pixel_cols(k2, t)[:CX].astype(BF)
    x_dx = put(s.dxs, s.dxr, sib)
    x_e.wait_recv()
    s.est[:, :, k] = (s.est[:, :, k].astype(F32) + s.esr[...].astype(F32)).astype(BF)
    e_in = to_peers(lambda d: s.est.at[:, chip[d], k], lambda d: s.epr.at[d - 1])
    g1u_z = up_to_planes(g1u, s.su1, s.zu1)
    fold_on(dq_in)
    arrived(dq_in[3])
    dqk = (s.dqk[...] + s.pxr[1].astype(F32) + s.pxr[2].astype(F32)).astype(BF)
    dx, gg_lat = norm_back(mm_nt(dqk, s.wqk[...].reshape(D, CP)), lat[...].astype(F32), g_lat[...])
    s.dh[...] += dx
    outs.append(fetch(s.dh, d_lat))
    arrived(e_in)
    total = s.est[:, p, k].astype(F32)
    for i in range(3):
        total += s.epr[i].astype(F32)
    s.ez[...] = total.astype(BF)
    e_z = to_planes(lambda d: s.ez.at[plane[d]], lambda d: s.ezr.at[d - 1])
    arrived(f_in[3])
    total = s.fst[p, k].astype(F32)
    for i in (1, 2):
        total += s.fpr[i].astype(F32)
    s.fz[0] = total.astype(BF)
    f_z = to_planes(lambda d: s.fz.at[0], lambda d: s.fz.at[d])
    arrived(g3u_z)
    s.zs[...] = (s.gsu_own[...].astype(F32) + sum(s.zg[i].astype(F32) for i in range(3))).astype(BF)
    g3u_in = to_peers(lambda d: s.zs.at[chip[d]], lambda d: s.zu3.at[d - 1])
    g3d_ag = down_total(g3d_z, s.sd3, s.zd3, s.agd3)

    x_dx.wait_recv()
    gg_in = jnp.zeros((261, 1), F32)
    for t in range(4):
        cols = slice(256 * t, 256 * (t + 1))
        dxn = (pixel_cols(k, t)[:CX] + s.dxr[:, cols].astype(F32))[:261]
        hat, r = norm_cols(pix[:, cols].astype(F32))
        dhat = dxn * s.gcol[0:261, 0:1]
        even = jnp.mean(dhat, axis=0, keepdims=True)
        tilt = jnp.mean(dhat * hat, axis=0, keepdims=True)
        d_pix[:, cols] = r * (dhat - even - hat * tilt)
        gg_in += jnp.sum(dxn * hat, axis=1, keepdims=True)
    s.gcol[0:261, :] = jnp.broadcast_to(gg_in, (261, 128))
    s.ga[k] = jnp.zeros((8, D), F32)
    s.ga[k, 0:1, 0:CP] = s.gcol[...].T[0:1, :]
    for i, gg in enumerate((gg_lat, gg_cmlp, gg_self, gg_smlp)):
        s.ga[k, i + 1 : i + 2, :] = gg
    x_ga = put(s.ga.at[k], s.ga.at[k], sib)

    arrived(e_z)
    total = s.ez[z].astype(F32)
    for i in range(3):
        total += s.ezr[i].astype(F32)
    s.eag[c] = total.astype(BF)
    e_s = to_plane(s.eag.at[c])
    x_ga.wait_recv()
    s.gb[p] = s.ga[0] + s.ga[1]
    gb_in = to_peers(lambda d: s.gb.at[p], lambda d: s.gb.at[p])
    relay(g3d_ag[1])
    arrived(g3u_in)
    s.agu3[c] = (s.zs[p].astype(F32) + sum(s.zu3[i].astype(F32) for i in range(3))).astype(BF)
    g3u_ag = gather(lambda i: s.agu3.at[i], lambda i, h: s.agu3.at[i, 128 * h : 128 * h + 128])
    for copies in pg_z:
        arrived(copies)
    for i in range(3):
        total = s.pg[i, k, own_z, :].astype(F32)
        for d in range(3):
            total += s.zq[d, i].astype(F32)
        s.agq[c, i] = total.astype(BF)
    q_ag = gather(lambda i: s.agq.at[i], lambda i, h: s.agq.at[i, :, 128 * h : 128 * h + 128])
    arrived(gb_in)
    s.gc[z] = s.gb[0] + s.gb[1] + s.gb[2] + s.gb[3]
    gc_in = to_planes(lambda d: s.gc.at[z], lambda d: s.gc.at[z])
    relay(g3u_ag[1])
    relay(q_ag[1])
    wo_ag = down_total(pgo_z, s.wz, s.zo, s.ago)
    g3d_s = pass_on(g3d_ag)
    arrived(f_z)
    s.wvo[c, 0:CR, :] = sum(s.fz[d].astype(F32) for d in range(4)).astype(BF)

    def f_slot(i):
        return s.wvo.at[i, 0:CR]

    f_ag = gather(f_slot, lambda i, h: s.wvo.at[i, 144 * h : 144 * h + 144])
    eighth = pl.ds(pl.multiple_of(c * 48, 16), 48)
    arrived(e_s)
    e_all = s.eag[...].reshape(256, CP)
    for j in range(4):
        s.gks[j] = mm_tn(e_all, s.wq_z[:, 256 * j : 256 * (j + 1)]).astype(BF)
    gk_z = to_planes(lambda d: s.gks.at[plane[d], eighth], lambda d: s.gkr.at[d - 1])
    sent([x_n3])
    for j in range(4):
        s.n3[:, :, 256 * j : 256 * (j + 1)] = mm(e_all, s.wk[j]).astype(BF).reshape(2, 128, 256)
    outs.extend(fetch(s.n3.at[i], d_big.at[8, 128 * i : 128 * (i + 1)]) for i in range(2))
    g1d_ag = down_total(g1d_z, s.sd1, s.zd1, s.agd1)
    g1u_ag = up_total(g1u_z, s.su1, s.zu1, s.agu1)
    relay(f_ag[1])
    relay(wo_ag[1])
    g3u_s = pass_on(g3u_ag)
    relay(g1d_ag[1])
    relay(g1u_ag[1])
    arrived(gk_z)
    total = s.gks[z, eighth, :].astype(F32)
    for i in range(3):
        total += s.gkr[i].astype(F32)
    s.gkh[eighth, :] = total.astype(BF)
    x_gk = to_plane(s.gkh.at[eighth])
    q_s = pass_on(q_ag)
    f_s = pass_on(f_ag)
    wo_s_ = pass_on(wo_ag)
    g1d_s = pass_on(g1d_ag)
    g1u_s = pass_on(g1u_ag)
    arrived(g3d_s)
    out_rows(s.agd3, 7)
    arrived(g3u_s)
    out_cols(s.agu3, 6)
    arrived(f_s)
    sent([x_n1])
    acc = jnp.zeros((CP, 256), F32)
    for j in range(4):
        f_two = jnp.concatenate([s.wvo[2 * j], s.wvo[2 * j + 1]], axis=1)
        acc += mm_nt(f_two, s.wo_z[:, 256 * j : 256 * (j + 1)])
        s.n1[:, :, 256 * j : 256 * (j + 1)] = mm_tn(s.wv_z[...], f_two).astype(BF).reshape(2, 128, 256)
    d_wv[...] = acc[:261]
    outs.extend(fetch(s.n1.at[i], d_big.at[9, 128 * i : 128 * (i + 1)]) for i in range(2))
    arrived(q_s)
    for i in range(3):
        for j in range(8):
            outs.append(fetch(s.agq.at[j, i], d_big.at[2 + i, :, 128 * j : 128 * (j + 1)]))
    arrived(wo_s_)
    out_rows(s.ago, 5)
    arrived(gc_in)
    d_gain[...] = s.gc[0] + s.gc[1] + s.gc[2] + s.gc[3]
    arrived(x_gk)
    d_wk[...] = s.gkh[...].astype(F32)[0:261]
    arrived(g1d_s)
    out_rows(s.agd1, 1)
    arrived(g1u_s)
    out_cols(s.agu1, 0)
    for copy in outs:
        copy.wait()
    for when, copy in sends:
        if when is None:
            copy.wait_send()
        else:
            pl.when(when)(copy.wait_send)


def norm_cols(x):
    center = x - jnp.mean(x, axis=0, keepdims=True)
    r = lax.rsqrt(jnp.mean(center * center, axis=0, keepdims=True) + 1e-05)
    return center * r, r


def tag(val, lane, one, two):
    for i, x in enumerate((one, two)):
        for j in range(3):
            part = x.astype(BF).astype(F32)
            val = jnp.where(lane == 261 + 3 * i + j, part, val)
            x = x - part
    return val.astype(BF)


def untag(low, lane):
    val = low.astype(F32)

    def column(i):
        here = (lane >= 261 + 3 * i) & (lane < 264 + 3 * i)
        return jnp.sum(jnp.where(here, val, 0.0), axis=1, keepdims=True)

    return jnp.where(lane < 261, val, 0.0), column(0), column(1)


SCRATCH = {
    "ssem": 400, "rsem": 400, "lsem": 96,

    "wk": ((4, CP, 256), BF), "wqk": ((4, 2, 128, CP), BF), "wq_z": ((256, 1024), BF), "wo_z": ((256, 1024), BF),
    "wv_z": ((CP, 256), BF), "wvz": ((4, CR, 128), BF), "wvo": ((8, CP, 128), BF),
    "wu1": ((4, 1024, 128), BF), "wu3": ((4, 1024, 128), BF), "wd1": ((4, 4, 32, 1024), BF), "wd3": ((4, 4, 32, 1024), BF),
    "wqkv": ((3, 2, 1024, 128), BF), "wo": ((2, 128, 1024), BF),
    "xt": ((2, CP, 1024), BF), "span": ((1024, 128), jnp.int32), "pos": ((8, 1024), jnp.int32), "row": ((8, CP), F32), "gcol": ((CP, 128), F32), "lnp": ((4, 128, 1024), BF), "qk": ((4, 128, CP), BF),
    "pxs": ((4, 128, CP), BF), "pxr": ((3, 128, CP), BF), "px": ((128, CP), F32), "pxl": ((128, CP), BF),
    "cpair": ((2, 128, 1024), BF), "n1": ((2, 128, 1024), BF), "n3": ((2, 128, 1024), BF),
    "u1": ((2, 256, 256), F32), "u3": ((2, 256, 256), F32), "z1": ((2, 256, 256), BF), "z3": ((2, 256, 256), BF),
    "gu1": ((2, 256, 256), BF), "gu3": ((2, 256, 256), BF),


    "h1": ((128, 1024), F32), "h2": ((128, 1024), F32), "h3": ((128, 1024), F32), "dh": ((128, 1024), F32),
    "n2": ((4, 128, 1024), BF), "go": ((4, 128, 1024), BF), "pair": ((128, 256), BF),
    "heads": ((2, 4, 3, 128, 128), BF), "mine": ((8, 3, 128, 128), BF),
    "a1": ((8, 128, 1024), BF), "a2": ((8, 128, 1024), BF), "send": ((4, 128, 128), BF), "aspar": ((4, 2, 128, 128), BF),
    "outp": ((3, 128, 1024), BF), "outr": ((3, 128, 1024), BF),
    "gheads": ((2, 4, 128, 128), BF), "gmine": ((8, 128, 128), BF),
    "dsend": ((4, 3, 128, 128), BF), "dpar": ((4, 3, 2, 128, 128), BF),


    "zu1": ((3, 256, 128), BF), "zu3": ((3, 256, 128), BF), "zd1": ((3, 32, 1024), BF), "zd3": ((3, 32, 1024), BF),
    "agu1": ((8, 256, 128), BF), "agu3": ((8, 256, 128), BF), "agd1": ((2, 4, 32, 1024), BF), "agd3": ((2, 4, 32, 1024), BF),
    "pg": ((3, 2, 1024, 128), BF), "pgr": ((3, 1024, 128), BF), "zq": ((3, 3, 256, 128), BF), "agq": ((8, 3, 256, 128), BF),
    "pgo": ((2, 128, 1024), BF), "pgor": ((128, 1024), BF), "zo": ((3, 32, 1024), BF), "ago": ((2, 4, 32, 1024), BF), "woz": ((4, 32, 1024), BF), "wz": ((4, 32, 1024), BF),
    "gv": ((4, 128, CP), BF), "dqk": ((128, CP), F32),
    "dxs": ((CX, 1024), BF), "dxr": ((CX, 1024), BF),
    "fst": ((4, 2, CR, 128), BF), "fsr": ((4, CR, 128), BF), "fpr": ((3, CR, 128), BF), "fz": ((4, CR, 128), BF),
    "est": ((4, 4, 2, 32, CP), BF), "esr": ((4, 4, 32, CP), BF), "epr": ((3, 4, 32, CP), BF), "ez": ((4, 32, CP), BF),
    "ezr": ((3, 32, CP), BF), "eag": ((8, 32, CP), BF),
    "gks": ((4, CP, 256), BF), "gkr": ((3, 48, 256), BF), "gkh": ((CP, 256), BF), "gpair": ((2, 128, 1024), BF), "zg": ((3, 4, 256, 128), BF), "zs": ((4, 256, 128), BF), "gsu_own": ((4, 256, 128), BF), "hs": ((128, 1024), BF), "hr": ((128, 1024), BF),
    "ga": ((2, 8, 1024), F32), "gb": ((4, 8, 1024), F32), "gc": ((4, 8, 1024), F32),
    "hpa": ((2, 128, 1024), F32), "hpb": ((2, 128, 1024), F32), "hxa": ((128, 1024), F32), "hxb": ((128, 1024), F32),
    "ee": ((8, 128, 1024), BF), "tops": ((4, 128, 128), F32), "gvr": ((4, 128, CP), BF),
    "gsu": ((4, 1024, 128), BF), "gsd": ((4, 4, 32, 1024), BF), "gru": ((3, 1024, 128), BF), "grd": ((3, 4, 32, 1024), BF),
    "su1": ((1024, 128), BF), "sd1": ((4, 32, 1024), BF), "sd3": ((4, 32, 1024), BF),
}


def unpack(layer_in, lat_in, big_in, wk_in, wv_in, gain_in, pix_in, layer_out, d_lat, *rest):
    big = rest[:10]
    wk_out, wv_out, gains, first, pix_out = rest[10], rest[11], rest[12:16], rest[16], rest[17]
    low, wide, pix_rows, layer, lat, wk, wv, gain, pix, sem_in, sem_out = rest[18:]

    def load(i, src, dst):
        copy = pltpu.make_async_copy(src, dst, sem_in.at[i])
        copy.start()
        return copy

    def store(i, src, dst):
        copy = pltpu.make_async_copy(src, dst, sem_out.at[i])
        copy.start()
        return copy

    loads = [load(i, big_in.at[i], low.at[i]) for i in range(3)]
    pix_load = load(10, pix_in, pix)
    loads += [load(i, big_in.at[i], low.at[i]) for i in range(3, 10)]
    pairs = ((layer_in, layer, layer_out), (lat_in, lat, d_lat), (wk_in, wk, wk_out), (wv_in, wv, wv_out))
    small = [load(11 + i, src, dst) for i, (src, dst, _) in enumerate(pairs)]
    gain_load = load(15, gain_in, gain)
    stores = []
    for i in range(10):
        loads[i].wait()
        wide[i] = low[i].astype(F32)
        stores.append(store(i, wide.at[i], big[i]))
        if i == 2:
            pix_load.wait()
            pix_rows[...] = pix[...].reshape(261, 1, 1024)
            stores.append(store(10, pix_rows, pix_out))
    for i, (_, src, dst) in enumerate(pairs):
        small[i].wait()
        stores.append(store(11 + i, src, dst))
    gain_load.wait()
    first[...] = gain[0:1, 0:261].reshape(261)
    for i in range(4):
        stores.append(store(15 + i, gain.at[i + 1 : i + 2], gains[i]))
    for copy in stores:
        copy.wait()


def one_kernel(
    pixels, latents, cotangent, doc_lengths, latent_offsets, block_deal,
    wq_c, wk_c, wv_c, wo_c, wu_c, wd_c, wq_s, wk_s, wv_s, wo_s, wu_s, wd_s,
    g_in, g_lat, g_cmlp, g_self, g_smlp,
):
    vmem, hbm = pl.BlockSpec(memory_space=pltpu.VMEM), pl.BlockSpec(memory_space=pl.ANY)
    smem = pl.BlockSpec(memory_space=pltpu.SMEM)

    def shape(dims, kind=F32):
        return jax.ShapeDtypeStruct(dims, kind)

    layer_out, d_pix, d_lat, big, d_wk, d_wv, gains = pl.pallas_call(
        fused,
        out_shape=(
            shape((128, D), BF), shape((261, 1024)), shape((128, D)), shape((10, 256, D), BF),
            shape((261, 256)), shape((261, 256)), shape((8, D)),
        ),
        in_specs=[vmem, vmem, vmem, smem, vmem, smem] + [vmem] * 5 + [hbm] * 12,
        out_specs=(vmem, vmem, hbm, hbm, vmem, vmem, vmem),
        scratch_shapes=[
            pltpu.SemaphoreType.DMA((what,)) if isinstance(what, int) else pltpu.VMEM(*what)
            for what in SCRATCH.values()
        ],
        compiler_params=pltpu.CompilerParams(
            collective_id=0, has_side_effects=True, vmem_limit_bytes=VMEM_BYTES
        ),
        cost_estimate=pl.CostEstimate(flops=26 * 10**9, bytes_accessed=40 * 10**6, transcendentals=10**7),
    )(
        pixels[0].T, latents[0], cotangent[0], doc_lengths, latent_offsets, block_deal,
        g_in, g_lat[None], g_cmlp[None], g_self[None], g_smlp[None],
        wq_c, wk_c, wv_c, wo_c, wu_c, wd_c, wq_s, wk_s, wv_s, wo_s, wu_s, wd_s,
    )
    outs = pl.pallas_call(
        unpack,
        out_shape=(
            shape((128, D), BF), shape((128, D)), *[shape((256, D))] * 10, *[shape((261, 256))] * 2, *[shape((1, D))] * 4,
            shape((261,)), shape((261, 1, 1024)),
        ),
        in_specs=[hbm] * 7,
        out_specs=(*[hbm] * 18, vmem, hbm),
        scratch_shapes=[
            pltpu.VMEM((10, 256, D), BF), pltpu.VMEM((10, 256, D), F32), pltpu.VMEM((261, 1, 1024), F32),
            pltpu.VMEM((128, D), BF), pltpu.VMEM((128, D), F32), pltpu.VMEM((261, 256), F32), pltpu.VMEM((261, 256), F32),
            pltpu.VMEM((8, D), F32), pltpu.VMEM((261, 1024), F32),
            pltpu.SemaphoreType.DMA((16,)), pltpu.SemaphoreType.DMA((19,)),
        ],
        compiler_params=pltpu.CompilerParams(vmem_limit_bytes=VMEM_BYTES),
        cost_estimate=pl.CostEstimate(flops=0, bytes_accessed=18 * 10**6, transcendentals=0),
    )(layer_out, d_lat, big, d_wk, d_wv, gains, d_pix)
    layer_out, d_lat, d_big, d_wk, d_wv, d_gain = outs[0], outs[1], outs[2:12], outs[12], outs[13], outs[14:18]
    return (
        layer_out[None], outs[19].transpose(1, 2, 0), d_lat[None], d_big[8], d_wk, d_wv, d_big[9], *d_big[:8],
        outs[18], *(g[0] for g in d_gain),
    )


VMEM_BYTES = 65472 * 2**10


def solution(mesh):
    rows, row, col, all_ = P("fsdp", "ctx", None), P("fsdp", None), P(None, "fsdp"), P()
    weights = (row, col, col, *(row,) * 9)
    small = mesh.shape["ctx"] == 8 and mesh.shape["fsdp"] == 4
    return jax.shard_map(
        one_kernel if small else plain,
        mesh=mesh,
        in_specs=(rows, rows, rows, row, row, all_, *weights, *(all_,) * 5),
        out_specs=(rows, rows, rows, *weights, *(all_,) * 5),
        check_vma=False,
    )
```
